32 devices in a mesh: groups: 2 (over x), dp: 16 (over z, y, core).
Axes of the slice: x: 2, y: 2, z: 4, core: 2. Of those that a mesh axis runs over, the one named last changes fastest.
Arguments:
- act: bfloat16 [12288, 8192], P(('groups', 'dp')), parts along dimension 0, may hold values from -6 to 6
- grad: bfloat16 [12288, 8192], P(('groups', 'dp')), parts along dimension 0, may hold values from -6 to 6
- val_panels: bfloat16 [2, 384, 8192], P(None, 'dp'), may hold values from -6 to 6
- row_domain: int32 [12288], P(('groups', 'dp')), parts along dimension 0, may hold values from 0 to 4095, as said below
- block_tasks: int32 [192, 4], P(('groups', 'dp')), parts along dimension 0, may hold values from 0 to 15, all different within a row
- block_live: int32 [192], P(('groups', 'dp')), parts along dimension 0, may hold values from 0 to 1, as said below
- domain_tokens: int32 [8192], P(('groups', 'dp')), parts along dimension 0, may hold values from 4 to 256
Outputs:
- domain_score: float32 [16, 8192], P(None, ('groups', 'dp')), parts along dimension 1
The draws below stay inside these ranges and needn't reach their ends.
There are 2 independent parts, one for each index of `groups`. The reference program is written for one: setup_inputs(seed, part) draws one part's arguments, and reference() takes and returns one part's arrays. A program takes and returns all parts, laid end to end along the dimension named above; an argument that names none is the same for every part. Nothing has to cross between parts.
Inputs may be any that keep to these rules, and one draw needn't show every extreme that they name: `block_live`: in each device's 6 slots the live ones come first; every device has one live block or more, and some device has all 6 live. `row_domain`: device i of dp holds domains i * 256 to (i + 1) * 256 - 1 of the output; among the 384 rows of one device, at most 48 have their domain in the range of any one such device, and every device has exactly 48 rows in the range of one common device.
All inputs are finite; a program needn't handle non-finite values.
Results may differ from the reference program's by a relative error of at most 0.0003.
Values may be sent and summed in bfloat16 or wider, within the bound.
No kernel may reach another device: no remote copies, remote signals or barrier semaphores. Data moves between devices by JAX's collectives and lax.ppermute only.
A program may use at most 128 MiB of HBM per device.

```python
import jax
import jax.numpy as jnp
from jax import lax

D = 8192
BLK = 64
BLK_DEV = 6
TASKS = 16
VPT = 24
PAIRS = 4
DOMAINS = 4096
BLOCKS = 96
ROWS = 6144
VAL = 384
DOM_OWN = 256
CAP = 48


def draw_block_live(key, part):
    key = jax.random.fold_in(key, 7)
    first_key, second_key = jax.random.split(key)
    devices_count = BLOCKS // BLK_DEV
    counts = jax.random.randint(first_key, (devices_count,), 1, BLK_DEV + 1)
    chosen = jax.random.randint(second_key, (), 0, devices_count)
    counts = jnp.where(jnp.arange(devices_count) == chosen, BLK_DEV, counts)
    flags = jnp.arange(BLK_DEV)[None, :] < counts[:, None]
    return flags.astype(jnp.int32).reshape(-1)


def draw_row_domain(key, part):
    key = jax.random.fold_in(key, 11)
    common_key, device_key = jax.random.split(key)
    rows_dev = BLK * BLK_DEV
    devices_count = ROWS // rows_dev
    owners_count = DOMAINS // DOM_OWN
    common = jax.random.randint(common_key, (), 0, owners_count)

    def one_device(index):
        slot_key, order_key, local_key = jax.random.split(jax.random.fold_in(device_key, index), 3)
        mixed = jax.random.permutation(slot_key, owners_count * CAP)
        slot_owner = mixed // CAP
        leading = jnp.where(slot_owner == common, 0, 1).astype(jnp.int32)
        order = jnp.argsort(leading, stable=True)
        taken = slot_owner[order][:rows_dev]
        shuffled = taken[jax.random.permutation(order_key, rows_dev)]
        local = jax.random.randint(local_key, (rows_dev,), 0, DOM_OWN)
        return (shuffled * DOM_OWN + local).astype(jnp.int32)
    domains = jax.vmap(one_device)(jnp.arange(devices_count, dtype=jnp.int32))
    return domains.reshape(-1)


def with_ends(drawn, key, least, largest):
    place = [jax.random.randint(jax.random.fold_in(key, axis), (), 0, length) for axis, length in enumerate(drawn.shape)]
    longest = drawn.shape.index(max(drawn.shape))
    neighbour = place[:longest] + [(place[longest] + 1) % drawn.shape[longest]] + place[longest + 1:]
    return drawn.at[tuple(place)].set(least).at[tuple(neighbour)].set(largest)


def block_scale(stream_key, dims, pieces, least, largest):
    gain, own = 1.0, jax.random.fold_in(stream_key, 6)
    for position, blocks in pieces:
        heights = jnp.exp(jax.random.uniform(jax.random.fold_in(own, position), (blocks,), jnp.float32, least / len(pieces), largest / len(pieces)))
        gain = gain * jnp.repeat(heights, dims[position] // blocks).reshape([-1 if axis == position else 1 for axis in range(len(dims))])
    return gain


def distinct(stream_key, rows, amount, top, lift):
    order = jax.random.permutation(jax.random.fold_in(stream_key, 1), amount)
    favour = order
    for power in range(3):
        favour = favour * favour // amount
    favour = favour * lift // amount
    chance = jax.random.randint(jax.random.fold_in(stream_key, 2), (rows, amount), 0, 4096) + favour
    sure = jax.random.permutation(jax.random.fold_in(stream_key, 3), rows)[jnp.arange(amount) % rows]
    chance = jnp.where(jnp.arange(rows)[:, None] == sure[None, :], 1 << 14, chance)
    score = chance * amount + jnp.arange(amount)
    return lax.top_k(score.astype(jnp.int32), top)[1].astype(jnp.int32)


def bell_draw(rng, shape, scale, limit, cuts=(), kind=jnp.bfloat16):
    factor_of = block_scale(rng, shape, cuts, -0.22, 0.18) if cuts else 1.0
    drawn = jax.random.normal(rng, shape, jnp.float32) * scale * factor_of
    return jnp.minimum(jnp.maximum(drawn, -limit), limit).astype(kind)


def setup_inputs(seed: int = 0, part: int = 0) -> dict:
    key_list = jax.random.split(jax.random.key(seed), 8)
    own_keys = jax.random.split(jax.random.fold_in(key_list[7], part), 8)
    act = bell_draw(own_keys[0], (ROWS, D), 1.0, 6.0, ((0, 16),))
    grad = bell_draw(own_keys[1], (ROWS, D), 1.0, 6.0, ((0, 16),))
    val_panels = bell_draw(key_list[2], (2, VAL, D), 1.0, 6.0, ((1, 16),))
    row_domain = draw_row_domain(jax.random.fold_in(jax.random.fold_in(key_list[7], part), 71), part)
    block_tasks = distinct(own_keys[4], BLOCKS, TASKS, PAIRS, 0)
    block_live = draw_block_live(jax.random.fold_in(jax.random.fold_in(key_list[7], part), 71), part)
    domain_tokens = with_ends(jax.random.randint(own_keys[6], (DOMAINS,), 4, 257), jax.random.fold_in(own_keys[6], 1), 4, 256).astype(jnp.int32)
    return {"act": act, "grad": grad, "val_panels": val_panels, "row_domain": row_domain, "block_tasks": block_tasks, "block_live": block_live, "domain_tokens": domain_tokens}


def reference(act, grad, val_panels, row_domain, block_tasks, block_live, domain_tokens):
    width = act.shape[1]
    task_ids = jnp.arange(TASKS, dtype=jnp.int32)
    paired = lax.optimization_barrier(jnp.sum((block_tasks[:, :, None] == task_ids[None, None, :]).astype(jnp.float32), axis=1))
    weights = paired * block_live.astype(jnp.float32)[:, None]
    act_blocks = act.reshape(BLOCKS, BLK, width)
    grad_blocks = grad.reshape(BLOCKS, BLK, width)

    def per_block(items):
        block_act, block_grad, weight_row = items
        act_dots = jnp.dot(block_act, val_panels[0].T, preferred_element_type=jnp.float32)
        grad_dots = jnp.dot(block_grad, val_panels[1].T, preferred_element_type=jnp.float32)
        ghost = act_dots * grad_dots / width
        per_task = lax.optimization_barrier(jnp.sum(ghost.reshape(BLK, TASKS, VPT), axis=2))
        return per_task * weight_row[None, :]
    row_task = lax.map(per_block, (act_blocks, grad_blocks, weights)).reshape(ROWS, TASKS)
    sums = jax.ops.segment_sum(row_task, row_domain, num_segments=DOMAINS)
    scaled = sums / jnp.sqrt(domain_tokens.astype(jnp.float32))[:, None]
    return scaled.T
```

```python
import jax
import jax.numpy as jnp
import numpy as np
from jax import lax
from jax.sharding import PartitionSpec as P

TASKS = 16
AXES = ("groups", "dp")
HIGH = lax.Precision.HIGHEST


def scores(act, grad, rows):
    dims = (((1,), (1,)), ((), ()))
    left = lax.dot_general(rows[0], act, dims, preferred_element_type=jnp.float32)
    right = lax.dot_general(rows[1], grad, dims, preferred_element_type=jnp.float32)
    return left * right


def gather_pieces(val):
    third = val.shape[1] // 3
    g = lax.axis_index("groups")
    d = lax.axis_index("dp")
    z, y, c = d // 4, (d // 2) % 2, d % 2
    every = [(gg, zz, yy, cc) for gg in range(2) for zz in range(4) for yy in range(2) for cc in range(2)]

    def flat(gg, zz, yy, cc):
        return gg * 16 + zz * 4 + yy * 2 + cc

    def along_z(x, step, least):
        perm = []
        for gg, zz, yy, cc in every:
            age = zz if step > 0 else 3 - zz
            if 0 <= zz + step < 4 and age >= least:
                perm.append((flat(gg, zz, yy, cc), flat(gg, zz + step, yy, cc)))
        return lax.ppermute(x, AXES, perm)

    def flip(x, axis):
        perm = []
        for gg, zz, yy, cc in every:
            to = (1 - gg, zz, yy, cc) if axis == "x" else (gg, zz, 1 - yy, cc) if axis == "y" else (gg, zz, yy, 1 - cc)
            perm.append((flat(gg, zz, yy, cc), flat(*to)))
        return lax.ppermute(x, AXES, perm)

    def shard(table, flip_y, flip_c):
        zz = jnp.asarray(np.array(table, np.int32))[z]
        yy = 1 - y if flip_y else y
        cc = 1 - c if flip_c else c
        return zz * 4 + yy * 2 + cc

    first = val[:, :third]
    mine = lax.dynamic_slice_in_dim(val, third * (1 + g), third, 1)
    own = jnp.concatenate([first, mine], axis=1)

    up1 = along_z(own, 1, 0)
    down1 = along_z(own, -1, 0)
    y0 = flip(own, "y")
    own_c = flip(val, "c")
    up2 = along_z(up1, 1, 1)
    down2 = along_z(down1, -1, 1)
    low = z < 2
    slot_a = jnp.where(low, down1, up1)
    y1 = flip(slot_a, "y")
    up3 = along_z(up2, 1, 2)
    down3 = along_z(down2, -1, 2)
    slot_b = jnp.where(z == 0, down2, jnp.where(z == 1, up1, jnp.where(z == 2, down1, up2)))
    y2 = flip(slot_b, "y")
    slot_c = jnp.where(z == 0, down3, jnp.where(z == 1, down2, jnp.where(z == 2, up2, up3)))
    y3 = flip(slot_c, "y")

    tables = {"o": [0, 1, 2, 3], "a": [1, 2, 1, 2], "b": [2, 0, 3, 1], "c": [3, 3, 0, 0]}
    groups = [
        ([slot_a, y0], [("a", False), ("o", True)]),
        ([slot_b, y1], [("b", False), ("a", True)]),
        ([slot_c, y2], [("c", False), ("b", True)]),
        ([y3], [("c", True)]),
    ]
    pieces = [(jnp.concatenate([val, own_c], axis=1), [shard(tables["o"], False, fc) for fc in (False, True) for _ in range(3)])]
    for arrays, names in groups:
        part = jnp.concatenate([a[:, third:] for a in arrays], axis=1)
        across = flip(part, "x")
        full = jnp.concatenate(arrays + [across], axis=1)
        other = flip(full, "c")
        ids = []
        for fc in (False, True):
            two = [shard(tables[n], fy, fc) for n, fy in names]
            ids += [i for i in two for _ in range(2)] + two
        pieces.append((jnp.concatenate([full, other], axis=1), ids))
    return pieces


def shards(act, grad, val_panels, row_domain, block_tasks, block_live, domain_tokens):
    row_count, width = act.shape
    block_count = block_live.shape[0]
    block_rows = row_count // block_count
    n_dp = lax.axis_size("dp")
    owned = domain_tokens.shape[0]
    cap = 2 * row_count // n_dp
    task_ids = jnp.arange(TASKS, dtype=jnp.int32)

    owner = row_domain // owned
    local = row_domain % owned
    at_owner = (owner[:, None] == jnp.arange(n_dp, dtype=jnp.int32)[None, :])
    before = jnp.arange(row_count)[:, None] > jnp.arange(row_count)[None, :]
    rank = lax.dot_general(
        before.astype(jnp.bfloat16), at_owner.astype(jnp.bfloat16), (((1,), (0,)), ((), ())),
        preferred_element_type=jnp.float32,
    )
    rank = jnp.sum(jnp.where(at_owner, rank, 0.0), axis=1).astype(jnp.int32)
    place = owner * cap + rank
    pack = place[:, None] == jnp.arange(n_dp * cap, dtype=jnp.int32)[None, :]
    packed_local = jnp.sum(jnp.where(pack, local[:, None] + 1, 0), axis=0).reshape(n_dp, cap)
    their_local = lax.all_to_all(packed_local, "dp", 0, 0, tiled=True)
    spread = (their_local[:, :, None] == 1 + jnp.arange(owned, dtype=jnp.int32)).astype(jnp.float32)

    paired = jnp.sum((block_tasks[:, None, :] == task_ids[None, :, None]).astype(jnp.float32), axis=2)
    weights = paired * block_live.astype(jnp.float32)[:, None]
    weights = jnp.broadcast_to(weights.T[:, :, None], (TASKS, block_count, block_rows)).reshape(TASKS, row_count)

    if n_dp == 16 and lax.axis_size("groups") == 2:
        sums, ids = [], []
        for rows, sources in gather_pieces(val_panels):
            eight = rows.shape[1] // len(sources)
            sums.append(jnp.sum(scores(act, grad, rows).reshape(len(sources), eight, row_count), axis=1))
            ids += sources
        to_task = (jnp.stack(ids)[None, :] == task_ids[:, None]).astype(jnp.float32)
        per_task = lax.dot_general(to_task, jnp.concatenate(sums), (((1,), (0,)), ((), ())), precision=HIGH)
    else:
        rows = lax.all_gather(val_panels, "dp", axis=1, tiled=True)
        per_task = jnp.sum(scores(act, grad, rows).reshape(TASKS, -1, row_count), axis=1)
    row_task = per_task * (weights / width)

    packed = lax.dot_general(row_task, pack.astype(jnp.float32), (((1,), (0,)), ((), ())), precision=HIGH)
    packed = packed.reshape(TASKS, n_dp, cap).transpose(1, 0, 2)
    theirs = lax.all_to_all(packed, "dp", 0, 0, tiled=True)
    totals = lax.dot_general(theirs, spread, (((0, 2), (0, 1)), ((), ())), precision=HIGH)
    return totals / jnp.sqrt(domain_tokens.astype(jnp.float32))[None, :]


def solution(mesh):
    return jax.shard_map(
        shards,
        mesh=mesh,
        in_specs=(
            P(("groups", "dp"), None),
            P(("groups", "dp"), None),
            P(None, "dp", None),
            P(("groups", "dp")),
            P(("groups", "dp"), None),
            P(("groups", "dp")),
            P(("groups", "dp")),
        ),
        out_specs=P(None, ("groups", "dp")),
        check_vma=False,
    )
```

```python
import jax
import jax.numpy as jnp
from jax import lax
from jax.sharding import PartitionSpec as P

TASKS = 16
AXES = ("groups", "dp")
HIGH = lax.Precision.HIGHEST


def scores(act, grad, rows):
    dims = (((1,), (1,)), ((), ()))
    left = lax.dot_general(rows[0], act, dims, preferred_element_type=jnp.float32)
    right = lax.dot_general(rows[1], grad, dims, preferred_element_type=jnp.float32)
    return left * right


def ring_products(act, grad, val):
    third = val.shape[1] // 3
    row_count = act.shape[0]
    g = lax.axis_index("groups")
    d = lax.axis_index("dp")
    z, y, c = d // 4, (d // 2) % 2, d % 2
    spot = jnp.where(y == 0, z, 7 - z)
    every = [(gg, pp, cc) for gg in range(2) for pp in range(8) for cc in range(2)]

    def flat(gg, pp, cc):
        pp = pp % 8
        zz, yy = (pp, 0) if pp < 4 else (7 - pp, 1)
        return gg * 16 + zz * 4 + yy * 2 + cc

    def ring(x, step):
        return lax.ppermute(x, AXES, [(flat(*e), flat(e[0], e[1] + step, e[2])) for e in every])

    def across(x):
        return lax.ppermute(x, AXES, [(flat(*e), flat(1 - e[0], e[1], e[2])) for e in every])

    def sibling(x):
        return lax.ppermute(x, AXES, [(flat(*e), flat(e[0], e[1], 1 - e[2])) for e in every])

    def source(step, core):
        pp = lax.rem(spot - step + 8, 8)
        zz = jnp.where(pp < 4, pp, 7 - pp)
        yy = jnp.where(pp < 4, 0, 1)
        return zz * 4 + yy * 2 + core

    def products(rows):
        count = rows.shape[1] // third
        return jnp.sum(scores(act, grad, rows).reshape(count, third, row_count), axis=1)

    tie = lax.optimization_barrier
    cat = lambda *xs: jnp.concatenate(xs, axis=1)

    a0 = val[:, :third]
    b0 = lax.dynamic_slice_in_dim(val, third * (1 + g), third, 1)
    ub1, db1 = ring(b0, 1), ring(b0, -1)
    ua1, da1 = ring(a0, 1), ring(a0, -1)
    s0 = sibling(val)

    ub2, db2 = ring(ub1, 1), ring(db1, -1)
    x1 = across(cat(ub1, db1))
    ua1, da1, s0 = tie((ua1, da1, s0))
    ua2, da2 = ring(ua1, 1), ring(da1, -1)
    r0 = products(cat(val, s0))

    ub2, db2, x1 = tie((ub2, db2, x1))
    ub3, db3 = ring(ub2, 1), ring(db2, -1)
    x2 = across(cat(ub2, db2))
    h1 = cat(ua1, da1, ub1, db1, x1)
    s1 = sibling(h1)
    ua2, da2, s1, r0 = tie((ua2, da2, s1, r0))
    ua3, da3 = ring(ua2, 1), ring(da2, -1)
    r1 = products(cat(h1, s1))

    ub3, db3, x2, r1 = tie((ub3, db3, x2, r1))
    db4 = ring(db3, -1)
    x3 = across(cat(ub3, db3))
    h2 = cat(ua2, da2, ub2, db2, x2)
    s2 = sibling(h2)
    ua3, da3, s2 = tie((ua3, da3, s2))
    ua4 = ring(ua3, 1)
    r2 = products(cat(h2, s2))

    db4, x3, r2 = tie((db4, x3, r2))
    x4 = across(db4)
    h3 = cat(ua3, da3, ub3, db3, x3)
    s3 = sibling(h3)
    ua4, s3 = tie((ua4, s3))
    r3 = products(cat(h3, s3))
    x4, r3 = tie((x4, r3))
    h4 = cat(ua4, db4, x4)
    s4 = sibling(h4)
    r4 = products(cat(h4, s4))

    near, far = c, 1 - c
    ids = [source(0, near)] * 3 + [source(0, far)] * 3
    for step in (1, 2, 3):
        for core in (near, far):
            ids += [source(step, core), source(-step, core)] * 3
    ids += [source(4, near)] * 3 + [source(4, far)] * 3
    return jnp.concatenate([r0, r1, r2, r3, r4]), jnp.stack(ids)


def shards(act, grad, val_panels, row_domain, block_tasks, block_live, domain_tokens):
    row_count, width = act.shape
    block_count = block_live.shape[0]
    block_rows = row_count // block_count
    n_dp = lax.axis_size("dp")
    owned = domain_tokens.shape[0]
    cap = 2 * row_count // n_dp
    task_ids = jnp.arange(TASKS, dtype=jnp.int32)

    owner = row_domain // owned
    local = row_domain % owned
    at_owner = (owner[:, None] == jnp.arange(n_dp, dtype=jnp.int32)[None, :])
    before = jnp.arange(row_count)[:, None] > jnp.arange(row_count)[None, :]
    rank = lax.dot_general(
        before.astype(jnp.bfloat16), at_owner.astype(jnp.bfloat16), (((1,), (0,)), ((), ())),
        preferred_element_type=jnp.float32,
    )
    rank = jnp.sum(jnp.where(at_owner, rank, 0.0), axis=1).astype(jnp.int32)
    place = owner * cap + rank
    pack = (place[:, None] == jnp.arange(n_dp * cap, dtype=jnp.int32)[None, :]).astype(jnp.float32)

    paired = jnp.sum((block_tasks[:, None, :] == task_ids[None, :, None]).astype(jnp.float32), axis=2)
    weights = paired * block_live.astype(jnp.float32)[:, None]
    weights = jnp.broadcast_to(weights.T[:, :, None], (TASKS, block_count, block_rows)).reshape(TASKS, row_count)

    if n_dp == 16 and lax.axis_size("groups") == 2:
        sums, ids = ring_products(act, grad, val_panels)
        to_task = (ids[None, :] == task_ids[:, None]).astype(jnp.float32)
        per_task = lax.dot_general(to_task, sums, (((1,), (0,)), ((), ())), precision=HIGH)
    else:
        rows = lax.all_gather(val_panels, "dp", axis=1, tiled=True)
        per_task = jnp.sum(scores(act, grad, rows).reshape(TASKS, -1, row_count), axis=1)
    row_task = per_task * (weights / width)

    sent = jnp.concatenate([row_task, (local + 1).astype(jnp.float32)[None, :]])
    packed = lax.dot_general(sent, pack, (((1,), (0,)), ((), ())), precision=HIGH)
    packed = packed.reshape(TASKS + 1, n_dp, cap).transpose(1, 0, 2)
    theirs = lax.all_to_all(packed, "dp", 0, 0, tiled=True)
    their_local = theirs[:, TASKS].astype(jnp.int32)
    spread = (their_local[:, :, None] == 1 + jnp.arange(owned, dtype=jnp.int32)).astype(jnp.float32)
    totals = lax.dot_general(theirs[:, :TASKS], spread, (((0, 2), (0, 1)), ((), ())), precision=HIGH)
    return totals / jnp.sqrt(domain_tokens.astype(jnp.float32))[None, :]


def solution(mesh):
    return jax.shard_map(
        shards,
        mesh=mesh,
        in_specs=(
            P(("groups", "dp"), None),
            P(("groups", "dp"), None),
            P(None, "dp", None),
            P(("groups", "dp")),
            P(("groups", "dp"), None),
            P(("groups", "dp")),
            P(("groups", "dp")),
        ),
        out_specs=P(None, ("groups", "dp")),
        check_vma=False,
    )
```

```python
import jax
import jax.numpy as jnp
from jax import lax
from jax.sharding import PartitionSpec as P

TASKS = 16
AXES = ("groups", "dp")
HIGH = lax.Precision.HIGHEST


def scores(act, grad, rows):
    dims = (((1,), (1,)), ((), ()))
    left = lax.dot_general(rows[0], act, dims, preferred_element_type=jnp.float32)
    right = lax.dot_general(rows[1], grad, dims, preferred_element_type=jnp.float32)
    return left * right


def ring_products(act, grad, val):
    third = val.shape[1] // 3
    row_count = act.shape[0]
    g = lax.axis_index("groups")
    d = lax.axis_index("dp")
    z, y, c = d // 4, (d // 2) % 2, d % 2
    spot = jnp.where(y == 0, z, 7 - z)
    every = [(gg, pp, cc) for gg in range(2) for pp in range(8) for cc in range(2)]

    def flat(gg, pp, cc):
        pp = pp % 8
        zz, yy = (pp, 0) if pp < 4 else (7 - pp, 1)
        return gg * 16 + zz * 4 + yy * 2 + cc

    def ring(x, step):
        return lax.ppermute(x, AXES, [(flat(*e), flat(e[0], e[1] + step, e[2])) for e in every])

    def across(x):
        return lax.ppermute(x, AXES, [(flat(*e), flat(1 - e[0], e[1], e[2])) for e in every])

    def sibling(x):
        return lax.ppermute(x, AXES, [(flat(*e), flat(e[0], e[1], 1 - e[2])) for e in every])

    def source(step, core):
        pp = lax.rem(spot - step + 8, 8)
        zz = jnp.where(pp < 4, pp, 7 - pp)
        yy = jnp.where(pp < 4, 0, 1)
        return zz * 4 + yy * 2 + core

    def products(rows):
        count = rows.shape[1] // third
        return jnp.sum(scores(act, grad, rows).reshape(count, third, row_count), axis=1)

    tie = lax.optimization_barrier
    cat = lambda *xs: jnp.concatenate(xs, axis=1)

    a0 = val[:, :third]
    b0 = lax.dynamic_slice_in_dim(val, third * (1 + g), third, 1)
    ub1, db1 = ring(b0, 1), ring(b0, -1)
    ua1, da1 = ring(a0, 1), ring(a0, -1)
    ub2, db2 = ring(ub1, 1), ring(db1, -1)
    ua2, da2 = ring(ua1, 1), ring(da1, -1)
    x1 = across(cat(ub1, db1))
    s0 = sibling(val)
    ub1, db1, ua1, da1, ub2, db2, ua2, da2, x1, s0 = tie((ub1, db1, ua1, da1, ub2, db2, ua2, da2, x1, s0))

    x2 = across(cat(ub2, db2))
    ub3, db3 = ring(ub2, 1), ring(db2, -1)
    ua3, da3 = ring(ua2, 1), ring(da2, -1)
    db4 = ring(db3, -1)
    ua4 = ring(ua3, 1)
    x3 = across(cat(ub3, db3))
    h1 = cat(ua1, da1, ub1, db1, x1)
    s1 = sibling(h1)
    r1 = products(cat(val, s0, h1, s1))
    ub3, db3, ua3, da3, db4, ua4, x2, x3, r1 = tie((ub3, db3, ua3, da3, db4, ua4, x2, x3, r1))

    x4 = across(db4)
    h2 = cat(ua2, da2, ub2, db2, x2)
    s2 = sibling(h2)
    h3 = cat(ua3, da3, ub3, db3, x3)
    s3 = sibling(h3)
    h4 = cat(ua4, db4)
    s4 = sibling(h4)
    r2 = products(cat(h2, s2, h3, s3))
    x4, s4, r2 = tie((x4, s4, r2))
    s5 = sibling(x4)
    r3 = products(cat(h4, x4, s4, s5))

    near, far = c, 1 - c
    ids = [source(0, near)] * 3 + [source(0, far)] * 3
    for step in (1, 2, 3):
        for core in (near, far):
            ids += [source(step, core), source(-step, core)] * 3
    ids += [source(4, near)] * 3 + [source(4, far)] * 3
    return jnp.concatenate([r1, r2, r3]), jnp.stack(ids)


def shards(act, grad, val_panels, row_domain, block_tasks, block_live, domain_tokens):
    row_count, width = act.shape
    block_count = block_live.shape[0]
    block_rows = row_count // block_count
    n_dp = lax.axis_size("dp")
    owned = domain_tokens.shape[0]
    cap = 2 * row_count // n_dp
    task_ids = jnp.arange(TASKS, dtype=jnp.int32)

    owner = row_domain // owned
    local = row_domain % owned
    at_owner = (owner[:, None] == jnp.arange(n_dp, dtype=jnp.int32)[None, :])
    before = jnp.arange(row_count)[:, None] > jnp.arange(row_count)[None, :]
    rank = lax.dot_general(
        before.astype(jnp.bfloat16), at_owner.astype(jnp.bfloat16), (((1,), (0,)), ((), ())),
        preferred_element_type=jnp.float32,
    )
    rank = jnp.sum(jnp.where(at_owner, rank, 0.0), axis=1).astype(jnp.int32)
    place = owner * cap + rank
    pack = (place[:, None] == jnp.arange(n_dp * cap, dtype=jnp.int32)[None, :]).astype(jnp.float32)

    paired = jnp.sum((block_tasks[:, None, :] == task_ids[None, :, None]).astype(jnp.float32), axis=2)
    weights = paired * block_live.astype(jnp.float32)[:, None]
    weights = jnp.broadcast_to(weights.T[:, :, None], (TASKS, block_count, block_rows)).reshape(TASKS, row_count)

    if n_dp == 16 and lax.axis_size("groups") == 2:
        sums, ids = ring_products(act, grad, val_panels)
        to_task = (ids[None, :] == task_ids[:, None]).astype(jnp.float32)
        per_task = lax.dot_general(to_task, sums, (((1,), (0,)), ((), ())), precision=HIGH)
    else:
        rows = lax.all_gather(val_panels, "dp", axis=1, tiled=True)
        per_task = jnp.sum(scores(act, grad, rows).reshape(TASKS, -1, row_count), axis=1)
    row_task = per_task * (weights / width)

    sent = jnp.concatenate([row_task, (local + 1).astype(jnp.float32)[None, :]])
    packed = lax.dot_general(sent, pack, (((1,), (0,)), ((), ())), precision=HIGH)
    packed = packed.reshape(TASKS + 1, n_dp, cap).transpose(1, 0, 2)
    theirs = lax.all_to_all(packed, "dp", 0, 0, tiled=True)
    their_local = theirs[:, TASKS].astype(jnp.int32)
    spread = (their_local[:, :, None] == 1 + jnp.arange(owned, dtype=jnp.int32)).astype(jnp.float32)
    totals = lax.dot_general(theirs[:, :TASKS], spread, (((0, 2), (0, 1)), ((), ())), precision=HIGH)
    return totals / jnp.sqrt(domain_tokens.astype(jnp.float32))[None, :]


def solution(mesh):
    return jax.shard_map(
        shards,
        mesh=mesh,
        in_specs=(
            P(("groups", "dp"), None),
            P(("groups", "dp"), None),
            P(None, "dp", None),
            P(("groups", "dp")),
            P(("groups", "dp"), None),
            P(("groups", "dp")),
            P(("groups", "dp")),
        ),
        out_specs=P(None, ("groups", "dp")),
        check_vma=False,
    )
```

```python
import jax
import jax.numpy as jnp
from jax import lax
from jax.sharding import PartitionSpec as P

TASKS = 16
AXES = ("groups", "dp")
HIGH = lax.Precision.HIGHEST


def scores(act, grad, rows):
    dims = (((1,), (1,)), ((), ()))
    left = lax.dot_general(rows[0], act, dims, preferred_element_type=jnp.float32)
    right = lax.dot_general(rows[1], grad, dims, preferred_element_type=jnp.float32)
    return left * right


def ring_products(act, grad, val):
    third = val.shape[1] // 3
    row_count = act.shape[0]
    g = lax.axis_index("groups")
    d = lax.axis_index("dp")
    z, y, c = d // 4, (d // 2) % 2, d % 2
    spot = jnp.where(y == 0, z, 7 - z)
    every = [(gg, pp, cc) for gg in range(2) for pp in range(8) for cc in range(2)]

    def flat(gg, pp, cc):
        pp = pp % 8
        zz, yy = (pp, 0) if pp < 4 else (7 - pp, 1)
        return gg * 16 + zz * 4 + yy * 2 + cc

    def ring(x):
        perm = [(flat(gg, pp, cc), flat(gg, pp + 1 - 2 * cc, cc)) for gg, pp, cc in every]
        return lax.ppermute(x, AXES, perm)

    def across(x):
        return lax.ppermute(x, AXES, [(flat(*e), flat(1 - e[0], e[1], e[2])) for e in every])

    def sibling(x):
        return lax.ppermute(x, AXES, [(flat(*e), flat(e[0], e[1], 1 - e[2])) for e in every])

    def source(step, core):
        pp = lax.rem(spot + step + 8, 8)
        zz = jnp.where(pp < 4, pp, 7 - pp)
        yy = jnp.where(pp < 4, 0, 1)
        return zz * 4 + yy * 2 + core

    def products(rows):
        count = rows.shape[1] // third
        return jnp.sum(scores(act, grad, rows).reshape(count, third, row_count), axis=1)

    tie = lax.optimization_barrier
    cat = lambda *xs: jnp.concatenate(xs, axis=1)
    two = lambda v: cat(v[:, :third], lax.dynamic_slice_in_dim(v, third * (1 + g), third, 1))

    a1 = ring(two(val))
    s0 = sibling(val)
    b1 = ring(two(s0))
    xa1 = across(a1[:, third:])
    a2 = ring(a1)
    xb1 = across(b1[:, third:])
    b2 = ring(b1)
    a2, xa1 = tie((a2, xa1))
    xa2 = across(a2[:, third:])
    a3 = ring(a2)
    b2, xb1 = tie((b2, xb1))
    xb2 = across(b2[:, third:])
    b3 = ring(b2)
    h1 = cat(a1, xa1, b1, xb1)
    f1 = sibling(h1)
    r0 = products(cat(val, s0))
    r1 = products(cat(h1, f1))
    a3, xa2 = tie((a3, xa2))
    xa3 = across(a3[:, third:])
    a4 = ring(a3)
    b3, xb2, r0, r1 = tie((b3, xb2, r0, r1))
    xb3 = across(b3[:, third:])
    h2 = cat(a2, xa2, b2, xb2)
    f2 = sibling(h2)
    r2 = products(cat(h2, f2))
    c4 = ring(xa3)
    h3 = cat(a3, xa3, b3, xb3)
    f3 = sibling(h3)
    f4 = sibling(a4)
    c4, r2 = tie((c4, r2))
    e4 = sibling(c4)
    r3 = products(cat(h3, f3, a4, c4, f4, e4))

    near, far = c, 1 - c
    ahead, back = 2 * c - 1, 1 - 2 * c
    ids = [source(0, near)] * 3 + [source(0, far)] * 3
    for step in (1, 2, 3):
        ids += [source(step * ahead, near)] * 3 + [source(step * ahead, far)] * 3
        ids += [source(step * back, far)] * 3 + [source(step * back, near)] * 3
    ids += [source(4, near)] * 3 + [source(4, far)] * 3
    return jnp.concatenate([r0, r1, r2, r3]), jnp.stack(ids)


def shards(act, grad, val_panels, row_domain, block_tasks, block_live, domain_tokens):
    row_count, width = act.shape
    block_count = block_live.shape[0]
    block_rows = row_count // block_count
    n_dp = lax.axis_size("dp")
    owned = domain_tokens.shape[0]
    cap = 2 * row_count // n_dp
    task_ids = jnp.arange(TASKS, dtype=jnp.int32)

    owner = row_domain // owned
    local = row_domain % owned
    at_owner = (owner[:, None] == jnp.arange(n_dp, dtype=jnp.int32)[None, :])
    before = jnp.arange(row_count)[:, None] > jnp.arange(row_count)[None, :]
    rank = lax.dot_general(
        before.astype(jnp.bfloat16), at_owner.astype(jnp.bfloat16), (((1,), (0,)), ((), ())),
        preferred_element_type=jnp.float32,
    )
    rank = jnp.sum(jnp.where(at_owner, rank, 0.0), axis=1).astype(jnp.int32)
    place = owner * cap + rank
    pack = (place[:, None] == jnp.arange(n_dp * cap, dtype=jnp.int32)[None, :]).astype(jnp.float32)

    paired = jnp.sum((block_tasks[:, None, :] == task_ids[None, :, None]).astype(jnp.float32), axis=2)
    weights = paired * block_live.astype(jnp.float32)[:, None]
    weights = jnp.broadcast_to(weights.T[:, :, None], (TASKS, block_count, block_rows)).reshape(TASKS, row_count)

    if n_dp == 16 and lax.axis_size("groups") == 2:
        sums, ids = ring_products(act, grad, val_panels)
        to_task = (ids[None, :] == task_ids[:, None]).astype(jnp.float32)
        per_task = lax.dot_general(to_task, sums, (((1,), (0,)), ((), ())), precision=HIGH)
    else:
        rows = lax.all_gather(val_panels, "dp", axis=1, tiled=True)
        per_task = jnp.sum(scores(act, grad, rows).reshape(TASKS, -1, row_count), axis=1)
    row_task = per_task * (weights / width)

    sent = jnp.concatenate([row_task, (local + 1).astype(jnp.float32)[None, :]])
    packed = lax.dot_general(sent, pack, (((1,), (0,)), ((), ())), precision=HIGH)
    packed = packed.reshape(TASKS + 1, n_dp, cap).transpose(1, 0, 2)
    theirs = lax.all_to_all(packed, "dp", 0, 0, tiled=True)
    their_local = theirs[:, TASKS].astype(jnp.int32)
    spread = (their_local[:, :, None] == 1 + jnp.arange(owned, dtype=jnp.int32)).astype(jnp.float32)
    totals = lax.dot_general(theirs[:, :TASKS], spread, (((0, 2), (0, 1)), ((), ())), precision=HIGH)
    return totals / jnp.sqrt(domain_tokens.astype(jnp.float32))[None, :]


def solution(mesh):
    return jax.shard_map(
        shards,
        mesh=mesh,
        in_specs=(
            P(("groups", "dp"), None),
            P(("groups", "dp"), None),
            P(None, "dp", None),
            P(("groups", "dp")),
            P(("groups", "dp"), None),
            P(("groups", "dp")),
            P(("groups", "dp")),
        ),
        out_specs=P(None, ("groups", "dp")),
        check_vma=False,
    )
```

```python
import jax
import jax.numpy as jnp
from jax import lax
from jax.sharding import PartitionSpec as P

TASKS = 16
AXES = ("groups", "dp")
HIGH = lax.Precision.HIGHEST


def scores(act, grad, rows):
    dims = (((1,), (1,)), ((), ()))
    left = lax.dot_general(rows[0], act, dims, preferred_element_type=jnp.float32)
    right = lax.dot_general(rows[1], grad, dims, preferred_element_type=jnp.float32)
    return left * right


def ring_products(act, grad, val):
    third = val.shape[1] // 3
    row_count = act.shape[0]
    g = lax.axis_index("groups")
    d = lax.axis_index("dp")
    z, y, c = d // 4, (d // 2) % 2, d % 2
    spot = jnp.where(y == 0, z, 7 - z)
    every = [(gg, pp, cc) for gg in range(2) for pp in range(8) for cc in range(2)]

    def flat(gg, pp, cc):
        pp = pp % 8
        zz, yy = (pp, 0) if pp < 4 else (7 - pp, 1)
        return gg * 16 + zz * 4 + yy * 2 + cc

    def ring(x):
        perm = [(flat(gg, pp, cc), flat(gg, pp + 1 - 2 * cc, cc)) for gg, pp, cc in every]
        return lax.ppermute(x, AXES, perm)

    def across(x):
        return lax.ppermute(x, AXES, [(flat(*e), flat(1 - e[0], e[1], e[2])) for e in every])

    def sibling(x):
        return lax.ppermute(x, AXES, [(flat(*e), flat(e[0], e[1], 1 - e[2])) for e in every])

    def source(step, core):
        pp = lax.rem(spot + step + 8, 8)
        zz = jnp.where(pp < 4, pp, 7 - pp)
        yy = jnp.where(pp < 4, 0, 1)
        return zz * 4 + yy * 2 + core

    def products(rows):
        count = rows.shape[1] // third
        return jnp.sum(scores(act, grad, rows).reshape(count, third, row_count), axis=1)

    tie = lax.optimization_barrier
    cat = lambda *xs: jnp.concatenate(xs, axis=1)
    two = lambda v: cat(v[:, :third], lax.dynamic_slice_in_dim(v, third * (1 + g), third, 1))

    s0 = sibling(val)
    a1 = ring(val)
    b1 = ring(two(s0))
    a2 = ring(two(a1))
    xb1 = across(b1[:, third:])
    b2 = ring(b1)
    xa2 = across(a2[:, third:])
    a3 = ring(a2)
    b2, xb1 = tie((b2, xb1))
    xb2 = across(b2[:, third:])
    b3 = ring(b2)
    h1 = cat(a1, b1, xb1)
    f1 = sibling(h1)
    r1 = products(cat(val, s0, h1, f1))
    a3, xa2, r1 = tie((a3, xa2, r1))
    xa3 = across(a3[:, third:])
    a4 = ring(a3)
    b3, xb2, a3 = tie((b3, xb2, a3))
    xb3 = across(b3[:, third:])
    h2 = cat(a2, xa2, b2, xb2)
    f2 = sibling(h2)
    r2 = products(cat(h2, f2))
    xa3, b3 = tie((xa3, b3))
    c4 = ring(xa3)
    xb3, r2 = tie((xb3, r2))
    h3 = cat(a3, xa3, b3, xb3)
    f3 = sibling(h3)
    a4, r2 = tie((a4, r2))
    f4 = sibling(a4)
    e4 = sibling(c4)
    r3 = products(cat(h3, f3, a4, c4, f4, e4))

    near, far = c, 1 - c
    ahead, back = 2 * c - 1, 1 - 2 * c
    ids = [source(0, near)] * 3 + [source(0, far)] * 3
    for step in (1, 2, 3):
        ids += [source(step * ahead, near)] * 3 + [source(step * ahead, far)] * 3
        ids += [source(step * back, far)] * 3 + [source(step * back, near)] * 3
    ids += [source(4, near)] * 3 + [source(4, far)] * 3
    return jnp.concatenate([r1, r2, r3]), jnp.stack(ids)


def shards(act, grad, val_panels, row_domain, block_tasks, block_live, domain_tokens):
    row_count, width = act.shape
    block_count = block_live.shape[0]
    block_rows = row_count // block_count
    n_dp = lax.axis_size("dp")
    owned = domain_tokens.shape[0]
    cap = 2 * row_count // n_dp
    task_ids = jnp.arange(TASKS, dtype=jnp.int32)

    owner = row_domain // owned
    local = row_domain % owned
    at_owner = (owner[:, None] == jnp.arange(n_dp, dtype=jnp.int32)[None, :])
    before = jnp.arange(row_count)[:, None] > jnp.arange(row_count)[None, :]
    rank = lax.dot_general(
        before.astype(jnp.bfloat16), at_owner.astype(jnp.bfloat16), (((1,), (0,)), ((), ())),
        preferred_element_type=jnp.float32,
    )
    rank = jnp.sum(jnp.where(at_owner, rank, 0.0), axis=1).astype(jnp.int32)
    place = owner * cap + rank
    pack = (place[:, None] == jnp.arange(n_dp * cap, dtype=jnp.int32)[None, :]).astype(jnp.float32)

    paired = jnp.sum((block_tasks[:, None, :] == task_ids[None, :, None]).astype(jnp.float32), axis=2)
    weights = paired * block_live.astype(jnp.float32)[:, None]
    weights = jnp.broadcast_to(weights.T[:, :, None], (TASKS, block_count, block_rows)).reshape(TASKS, row_count)

    if n_dp == 16 and lax.axis_size("groups") == 2:
        sums, ids = ring_products(act, grad, val_panels)
        to_task = (ids[None, :] == task_ids[:, None]).astype(jnp.float32)
        per_task = lax.dot_general(to_task, sums, (((1,), (0,)), ((), ())), precision=HIGH)
    else:
        rows = lax.all_gather(val_panels, "dp", axis=1, tiled=True)
        per_task = jnp.sum(scores(act, grad, rows).reshape(TASKS, -1, row_count), axis=1)
    row_task = per_task * (weights / width)

    sent = jnp.concatenate([row_task, (local + 1).astype(jnp.float32)[None, :]])
    packed = lax.dot_general(sent, pack, (((1,), (0,)), ((), ())), precision=HIGH)
    packed = packed.reshape(TASKS + 1, n_dp, cap).transpose(1, 0, 2)
    theirs = lax.all_to_all(packed, "dp", 0, 0, tiled=True)
    their_local = theirs[:, TASKS].astype(jnp.int32)
    spread = (their_local[:, :, None] == 1 + jnp.arange(owned, dtype=jnp.int32)).astype(jnp.float32)
    totals = lax.dot_general(theirs[:, :TASKS], spread, (((0, 2), (0, 1)), ((), ())), precision=HIGH)
    return totals / jnp.sqrt(domain_tokens.astype(jnp.float32))[None, :]


def solution(mesh):
    return jax.shard_map(
        shards,
        mesh=mesh,
        in_specs=(
            P(("groups", "dp"), None),
            P(("groups", "dp"), None),
            P(None, "dp", None),
            P(("groups", "dp")),
            P(("groups", "dp"), None),
            P(("groups", "dp")),
            P(("groups", "dp")),
        ),
        out_specs=P(None, ("groups", "dp")),
        check_vma=False,
    )
```

```python
import jax
import jax.numpy as jnp
from jax import lax
from jax.sharding import PartitionSpec as P

TASKS = 16
AXES = ("groups", "dp")
HIGH = lax.Precision.HIGHEST


def scores(act, grad, rows):
    dims = (((1,), (1,)), ((), ()))
    left = lax.dot_general(rows[0], act, dims, preferred_element_type=jnp.float32)
    right = lax.dot_general(rows[1], grad, dims, preferred_element_type=jnp.float32)
    return left * right


def ring_products(act, grad, val, small):
    third = val.shape[1] // 3
    row_count = act.shape[0]
    g = lax.axis_index("groups")
    d = lax.axis_index("dp")
    z, y, c = d // 4, (d // 2) % 2, d % 2
    spot = jnp.where(y == 0, z, 7 - z)
    every = [(gg, pp, cc) for gg in range(2) for pp in range(8) for cc in range(2)]

    def flat(gg, pp, cc):
        pp = pp % 8
        zz, yy = (pp, 0) if pp < 4 else (7 - pp, 1)
        return gg * 16 + zz * 4 + yy * 2 + cc

    def ring(x):
        perm = [(flat(gg, pp, cc), flat(gg, pp + 1 - 2 * cc, cc)) for gg, pp, cc in every]
        return lax.ppermute(x, AXES, perm)

    def across(x):
        return lax.ppermute(x, AXES, [(flat(*e), flat(1 - e[0], e[1], e[2])) for e in every])

    def sibling(x):
        return lax.ppermute(x, AXES, [(flat(*e), flat(e[0], e[1], 1 - e[2])) for e in every])

    def source(step, core):
        pp = lax.rem(spot + step + 8, 8)
        zz = jnp.where(pp < 4, pp, 7 - pp)
        yy = jnp.where(pp < 4, 0, 1)
        return zz * 4 + yy * 2 + core

    def products(rows):
        count = rows.shape[1] // third
        return jnp.sum(scores(act, grad, rows).reshape(count, third, row_count), axis=1)

    tie = lax.optimization_barrier
    cat = lambda *xs: jnp.concatenate(xs, axis=1)
    two = lambda v: cat(v[:, :third], lax.dynamic_slice_in_dim(v, third * (1 + g), third, 1))

    s0 = sibling(val)
    a1 = ring(val)
    b1 = ring(two(s0))
    b1, *small = tie((b1, *small))

    p1 = cat(a1[:, :third], b1[:, :third], lax.dynamic_slice_in_dim(a1, third * (1 + g), third, 1), b1[:, third:])
    p2 = ring(p1)
    x1 = across(b1[:, third:])
    p2, x1 = tie((p2, x1))
    p3 = ring(p2)
    x2 = across(p2[:, 2 * third:])
    h1 = cat(a1, b1, x1)
    f1 = sibling(h1)
    r1 = products(cat(val, s0, h1, f1))
    x2, r1 = tie((x2, r1))
    p3, r1 = tie((p3, r1))
    xa3 = across(p3[:, 2 * third:3 * third])
    a4 = ring(cat(p3[:, :third], p3[:, 2 * third:3 * third]))
    c3 = ring(x2[:, third:])
    h2 = cat(p2, x2)
    f2 = sibling(h2)
    r2 = products(cat(h2, f2))
    xa3, a4, r2 = tie((xa3, a4, r2))
    c4 = ring(xa3)
    h3 = cat(p3, xa3, c3)
    f3 = sibling(h3)
    f4 = sibling(a4)
    e4 = sibling(c4)
    r3 = products(cat(h3, f3, a4, c4, f4, e4))

    near, far = c, 1 - c
    ahead, back = 2 * c - 1, 1 - 2 * c
    ids = [source(0, near)] * 3 + [source(0, far)] * 3
    for step in (1, 2, 3):
        for first, second in ((source(step * ahead, near), source(step * ahead, far)), (source(step * back, far), source(step * back, near))):
            ids += [first] * 3 + [second] * 3 if step == 1 else [first, second] * 3
    ids += [source(4, near)] * 3 + [source(4, far)] * 3
    return jnp.concatenate([r1, r2, r3]), jnp.stack(ids), small


def shards(act, grad, val_panels, row_domain, block_tasks, block_live, domain_tokens):
    row_count, width = act.shape
    block_count = block_live.shape[0]
    block_rows = row_count // block_count
    n_dp = lax.axis_size("dp")
    owned = domain_tokens.shape[0]
    cap = 2 * row_count // n_dp
    task_ids = jnp.arange(TASKS, dtype=jnp.int32)

    if n_dp == 16 and lax.axis_size("groups") == 2:
        small = (row_domain, block_tasks, block_live, domain_tokens)
        sums, ids, small = ring_products(act, grad, val_panels, small)
        row_domain, block_tasks, block_live, domain_tokens = small
        to_task = (ids[None, :] == task_ids[:, None]).astype(jnp.float32)
        per_task = lax.dot_general(to_task, sums, (((1,), (0,)), ((), ())), precision=HIGH)
    else:
        rows = lax.all_gather(val_panels, "dp", axis=1, tiled=True)
        per_task = jnp.sum(scores(act, grad, rows).reshape(TASKS, -1, row_count), axis=1)

    paired = jnp.sum((block_tasks[:, None, :] == task_ids[None, :, None]).astype(jnp.float32), axis=2)
    weights = paired * block_live.astype(jnp.float32)[:, None]
    weights = jnp.broadcast_to(weights.T[:, :, None], (TASKS, block_count, block_rows)).reshape(TASKS, row_count)

    owner = row_domain // owned
    local = row_domain % owned
    at_owner = (owner[:, None] == jnp.arange(n_dp, dtype=jnp.int32)[None, :])
    before = jnp.arange(row_count)[:, None] > jnp.arange(row_count)[None, :]
    rank = lax.dot_general(
        before.astype(jnp.bfloat16), at_owner.astype(jnp.bfloat16), (((1,), (0,)), ((), ())),
        preferred_element_type=jnp.float32,
    )
    rank = jnp.sum(jnp.where(at_owner, rank, 0.0), axis=1).astype(jnp.int32)
    place = owner * cap + rank
    pack = (place[:, None] == jnp.arange(n_dp * cap, dtype=jnp.int32)[None, :]).astype(jnp.float32)

    row_task = per_task * (weights / width)
    sent = jnp.concatenate([row_task, (local + 1).astype(jnp.float32)[None, :]])
    packed = lax.dot_general(sent, pack, (((1,), (0,)), ((), ())), precision=HIGH)
    packed = packed.reshape(TASKS + 1, n_dp, cap).transpose(1, 0, 2)
    theirs = lax.all_to_all(packed, "dp", 0, 0, tiled=True)
    their_local = theirs[:, TASKS].astype(jnp.int32)
    spread = (their_local[:, :, None] == 1 + jnp.arange(owned, dtype=jnp.int32)).astype(jnp.float32)
    totals = lax.dot_general(theirs[:, :TASKS], spread, (((0, 2), (0, 1)), ((), ())), precision=HIGH)
    return totals / jnp.sqrt(domain_tokens.astype(jnp.float32))[None, :]


def solution(mesh):
    return jax.shard_map(
        shards,
        mesh=mesh,
        in_specs=(
            P(("groups", "dp"), None),
            P(("groups", "dp"), None),
            P(None, "dp", None),
            P(("groups", "dp")),
            P(("groups", "dp"), None),
            P(("groups", "dp")),
            P(("groups", "dp")),
        ),
        out_specs=P(None, ("groups", "dp")),
        check_vma=False,
    )
```

```python
import jax
import jax.numpy as jnp
from jax import lax
from jax.sharding import PartitionSpec as P

TASKS = 16
AXES = ("groups", "dp")
HIGH = lax.Precision.HIGHEST


def row_products(left, right):
    return lax.dot_general(left, right, (((1,), (1,)), ((), ())), preferred_element_type=jnp.float32)


def ring_products(act, grad, val, small):
    shard_rows, width = val.shape[1:]
    row_count = act.shape[0]
    flipped = width // 128 // 3 * 128
    ringed = width - flipped
    g = lax.axis_index("groups")
    d = lax.axis_index("dp")
    z, y, c = d // 4, (d // 2) % 2, d % 2
    spot = jnp.where(y == 0, z, 7 - z)
    every = [(gg, pp, cc) for gg in range(2) for pp in range(8) for cc in range(2)]

    def flat(gg, pp, cc):
        pp = pp % 8
        zz, yy = (pp, 0) if pp < 4 else (7 - pp, 1)
        return gg * 16 + zz * 4 + yy * 2 + cc

    def ring(x):
        perm = [(flat(gg, pp, cc), flat(gg, pp + 1 - 2 * cc, cc)) for gg, pp, cc in every]
        return lax.ppermute(x, AXES, perm)

    def across(x):
        return lax.ppermute(x, AXES, [(flat(*e), flat(1 - e[0], e[1], e[2])) for e in every])

    def sibling(x):
        return lax.ppermute(x, AXES, [(flat(*e), flat(e[0], e[1], 1 - e[2])) for e in every])

    def source(step, core):
        pp = lax.rem(spot + step + 8, 8)
        zz = jnp.where(pp < 4, pp, 7 - pp)
        yy = jnp.where(pp < 4, 0, 1)
        return zz * 4 + yy * 2 + core

    def ring_part(v):
        return lax.dynamic_slice_in_dim(v, flipped * g, ringed, 2)

    def flip_part(v):
        return lax.dynamic_slice_in_dim(v, ringed * (1 - g), flipped, 2)

    def to_flip(v):
        return lax.dynamic_slice_in_dim(v, (ringed - flipped) * g, flipped, 2)

    act_ring = lax.dynamic_slice_in_dim(act, flipped * g, ringed, 1)
    act_flip = lax.dynamic_slice_in_dim(act, ringed * (1 - g), flipped, 1)
    grad_ring = lax.dynamic_slice_in_dim(grad, flipped * g, ringed, 1)
    grad_flip = lax.dynamic_slice_in_dim(grad, ringed * (1 - g), flipped, 1)

    def ring_dots(rows):
        return row_products(rows[0], act_ring), row_products(rows[1], grad_ring)

    def shard_sums(dots, rows):
        left = dots[0] + row_products(rows[0], act_flip)
        right = dots[1] + row_products(rows[1], grad_flip)
        return jnp.sum((left * right).reshape(-1, shard_rows, row_count), axis=1)

    tie = lax.optimization_barrier
    cat = lambda *xs: jnp.concatenate(xs, axis=1)

    s0 = sibling(val)
    p0 = cat(ring_part(val), ring_part(s0))
    p1 = ring(p0)
    p1, *small = tie((p1, *small))
    p2 = ring(p1)
    x1 = across(to_flip(p1))
    p2, x1 = tie((p2, x1))
    p3 = ring(p2)
    send2 = to_flip(p2)
    x2a = across(send2[:, :shard_rows])
    f1, g1 = sibling(p1), sibling(x1)
    send2b, g1 = tie((send2[:, shard_rows:], g1))
    x2b = across(send2b)
    r1 = shard_sums(ring_dots(cat(p0, p1, f1)), cat(flip_part(val), flip_part(s0), x1, g1))
    f2 = sibling(p2)
    d2 = ring_dots(cat(p2, f2))
    x2a, r1, d2 = tie((x2a, r1, d2))
    c3a = ring(x2a)
    p3, x2a = tie((p3, x2a))
    a4 = ring(p3[:, :shard_rows])
    f3 = sibling(p3)
    d3 = ring_dots(cat(p3, f3))
    c3a, p3, x2b = tie((c3a, p3, x2b))
    c4 = ring(c3a)
    c3b = ring(x2b)
    f4 = sibling(a4)
    d4 = ring_dots(cat(a4, f4))
    early = cat(x2a, x2b, c3a)
    c4, d3 = tie((c4, d3))
    c3b, d4 = tie((c3b, d4))
    late = c3b
    g2, g3, g4 = sibling(early), sibling(late), sibling(c4)
    rows = cat(early[:, :2 * shard_rows], g2[:, :2 * shard_rows], early[:, 2 * shard_rows:], late, g2[:, 2 * shard_rows:], g3, c4, g4)
    dots = [jnp.concatenate(d) for d in zip(d2, d3, d4)]
    r2 = shard_sums(dots, rows)

    near, far = c, 1 - c
    ahead, back = 2 * c - 1, 1 - 2 * c
    ids = [source(0, near), source(0, far)]
    for step in (1, 2, 3):
        ids += [source(step * ahead, near), source(step * ahead, far), source(step * back, far), source(step * back, near)]
    ids += [source(4, near), source(4, far)]
    return jnp.concatenate([r1, r2]), jnp.stack(ids), small


def shards(act, grad, val_panels, row_domain, block_tasks, block_live, domain_tokens):
    row_count, width = act.shape
    block_count = block_live.shape[0]
    block_rows = row_count // block_count
    n_dp = lax.axis_size("dp")
    owned = domain_tokens.shape[0]
    cap = 2 * row_count // n_dp
    task_ids = jnp.arange(TASKS, dtype=jnp.int32)

    if n_dp == 16 and lax.axis_size("groups") == 2:
        small = (row_domain, block_tasks, block_live, domain_tokens)
        sums, ids, small = ring_products(act, grad, val_panels, small)
        row_domain, block_tasks, block_live, domain_tokens = small
        to_task = (ids[None, :] == task_ids[:, None]).astype(jnp.float32)
        per_task = lax.dot_general(to_task, sums, (((1,), (0,)), ((), ())), precision=HIGH)
    else:
        rows = lax.all_gather(val_panels, "dp", axis=1, tiled=True)
        ghost = row_products(rows[0], act) * row_products(rows[1], grad)
        per_task = jnp.sum(ghost.reshape(TASKS, -1, row_count), axis=1)

    paired = jnp.sum((block_tasks[:, None, :] == task_ids[None, :, None]).astype(jnp.float32), axis=2)
    weights = paired * block_live.astype(jnp.float32)[:, None]
    weights = jnp.broadcast_to(weights.T[:, :, None], (TASKS, block_count, block_rows)).reshape(TASKS, row_count)

    owner = row_domain // owned
    local = row_domain % owned
    at_owner = (owner[:, None] == jnp.arange(n_dp, dtype=jnp.int32)[None, :])
    before = jnp.arange(row_count)[:, None] > jnp.arange(row_count)[None, :]
    rank = lax.dot_general(
        before.astype(jnp.bfloat16), at_owner.astype(jnp.bfloat16), (((1,), (0,)), ((), ())),
        preferred_element_type=jnp.float32,
    )
    rank = jnp.sum(jnp.where(at_owner, rank, 0.0), axis=1).astype(jnp.int32)
    place = owner * cap + rank
    pack = (place[:, None] == jnp.arange(n_dp * cap, dtype=jnp.int32)[None, :]).astype(jnp.float32)

    row_task = per_task * (weights / width)
    sent = jnp.concatenate([row_task, (local + 1).astype(jnp.float32)[None, :]])
    packed = lax.dot_general(sent, pack, (((1,), (0,)), ((), ())), precision=HIGH)
    packed = packed.reshape(TASKS + 1, n_dp, cap).transpose(1, 0, 2)
    theirs = lax.all_to_all(packed, "dp", 0, 0, tiled=True)
    their_local = theirs[:, TASKS].astype(jnp.int32)
    spread = (their_local[:, :, None] == 1 + jnp.arange(owned, dtype=jnp.int32)).astype(jnp.float32)
    totals = lax.dot_general(theirs[:, :TASKS], spread, (((0, 2), (0, 1)), ((), ())), precision=HIGH)
    return totals / jnp.sqrt(domain_tokens.astype(jnp.float32))[None, :]


def solution(mesh):
    return jax.shard_map(
        shards,
        mesh=mesh,
        in_specs=(
            P(("groups", "dp"), None),
            P(("groups", "dp"), None),
            P(None, "dp", None),
            P(("groups", "dp")),
            P(("groups", "dp"), None),
            P(("groups", "dp")),
            P(("groups", "dp")),
        ),
        out_specs=P(None, ("groups", "dp")),
        check_vma=False,
    )
```

```python
import functools

import jax
import jax.numpy as jnp
from jax import lax
from jax.experimental import pallas as pl
from jax.experimental.pallas import tpu as pltpu
from jax.sharding import PartitionSpec as P

TASKS = 16
AXES = ("groups", "dp")
HIGH = lax.Precision.HIGHEST
SLOTS = 3


def row_products(left, right):
    return lax.dot_general(left, right, (((1,), (1,)), ((), ())), preferred_element_type=jnp.float32)


def dots_kernel(plan, *refs):
    places, rows, chunk, steps, begin, group, adds, sums = plan
    count = len(places)
    spots, refs = refs[0], refs[1:]
    pieces, refs = refs[:count], refs[count:]
    sides, refs = refs[:2], refs[2:]
    if adds:
        before, refs = refs[:2], refs[2:]
    outs, refs = (refs[:1], refs[1:]) if sums else (refs[:2], refs[2:])
    held, slots, totals, piece_sems, slot_sems = refs
    base = 0 if begin is None else pl.multiple_of(spots[begin], 128)

    def piece_copy(i):
        row, column, panel, size = places[i]
        columns = pl.ds(pl.multiple_of(spots[column], 128), pieces[i].shape[-1])
        where = held.at[:, pl.ds(row, size), columns] if panel is None else held.at[spots[panel], pl.ds(row, size), columns]
        return pltpu.make_async_copy(pieces[i], where, piece_sems.at[i])

    def side_copy(step):
        side, part = step // steps, step % steps
        columns = pl.ds(pl.multiple_of(base + part * chunk, 128), chunk)
        return pltpu.make_async_copy(sides[side].at[:, columns], slots.at[step % SLOTS], slot_sems.at[step % SLOTS])

    for i in range(count):
        piece_copy(i).start()
    for step in range(min(SLOTS, 2 * steps)):
        side_copy(step).start()
    for i in range(count):
        piece_copy(i).wait()
    for step in range(2 * steps):
        side, part = step // steps, step % steps
        side_copy(step).wait()
        product = row_products(held[side, :, part * chunk:(part + 1) * chunk], slots[step % SLOTS])
        if part > 0:
            totals[side] += product
        elif adds:
            totals[side] = before[side][...] + product
        else:
            totals[side] = product
        if step + SLOTS < 2 * steps:
            side_copy(step + SLOTS).start()
    if sums:
        ghost = totals[0] * totals[1]
        outs[0][...] = jnp.sum(ghost.reshape(rows // group, group, ghost.shape[1]), axis=1)
    else:
        outs[0][...] = totals[0]
        outs[1][...] = totals[1]


def dots(spots, act, grad, pieces, rows, width, chunk, begin, group, before=None, sums=True):
    row_count = act.shape[0]
    places = tuple((row, column, panel, array.shape[-2]) for array, row, column, panel in pieces)
    steps = width // chunk
    plan = (places, rows, chunk, steps, begin, group, before is not None, sums)
    total = jax.ShapeDtypeStruct((rows, row_count), jnp.float32)
    anywhere = pl.BlockSpec(memory_space=pl.ANY)
    inside = pl.BlockSpec(memory_space=pltpu.VMEM)
    out = [jax.ShapeDtypeStruct((rows // group, row_count), jnp.float32)] if sums else [total, total]
    extra = [] if before is None else list(before)
    result = pl.pallas_call(
        functools.partial(dots_kernel, plan),
        out_shape=out,
        in_specs=[pl.BlockSpec(memory_space=pltpu.SMEM)] + [anywhere] * (len(pieces) + 2) + [inside] * len(extra),
        out_specs=[inside] * len(out),
        scratch_shapes=[
            pltpu.VMEM((2, rows, width), jnp.bfloat16),
            pltpu.VMEM((SLOTS, row_count, chunk), jnp.bfloat16),
            pltpu.VMEM((2, rows, row_count), jnp.float32),
            pltpu.SemaphoreType.DMA((len(pieces),)),
            pltpu.SemaphoreType.DMA((SLOTS,)),
        ],
        compiler_params=pltpu.CompilerParams(vmem_limit_bytes=24 * 1024 * 1024),
        cost_estimate=pl.CostEstimate(
            flops=4 * rows * width * row_count, bytes_accessed=4 * (rows + row_count) * width, transcendentals=0
        ),
    )(spots, *[piece[0] for piece in pieces], act, grad, *extra)
    return result[0] if sums else result


def ring_products(act, grad, val, small):
    shard_rows, width = val.shape[1:]
    pair = 2 * shard_rows
    lent = width // 128 * 3 // 10 * 128
    shared = width - 2 * lent
    g = lax.axis_index("groups")
    d = lax.axis_index("dp")
    z, y, c = d // 4, (d // 2) % 2, d % 2
    spot = jnp.where(y == 0, z, 7 - z)
    every = [(gg, pp, cc) for gg in range(2) for pp in range(8) for cc in range(2)]

    def flat(gg, pp, cc):
        pp = pp % 8
        zz, yy = (pp, 0) if pp < 4 else (7 - pp, 1)
        return gg * 16 + zz * 4 + yy * 2 + cc

    def ring(x):
        perm = [(flat(gg, pp, cc), flat(gg, pp + 1 - 2 * cc, cc)) for gg, pp, cc in every]
        return lax.ppermute(x, AXES, perm)

    def across(x):
        return lax.ppermute(x, AXES, [(flat(*e), flat(1 - e[0], e[1], e[2])) for e in every])

    def sibling(x):
        return lax.ppermute(x, AXES, [(flat(*e), flat(e[0], e[1], 1 - e[2])) for e in every])

    def sources(step):
        pp = lax.rem(spot + step + 8, 8)
        zz = jnp.where(pp < 4, pp, 7 - pp)
        yy = jnp.where(pp < 4, 0, 1)
        return [zz * 4 + yy * 2, zz * 4 + yy * 2 + 1]

    tie = lax.optimization_barrier
    mine = lambda x: lax.dynamic_index_in_dim(x, c, 0, keepdims=False)
    spots = jnp.stack([
        (width - lent) * g, lent + 0 * g, (width - lent) * (1 - g),
        lent * g, shared * g, lent * (1 - g), 0 * g, c, 1 - c,
    ]).astype(jnp.int32)
    U, M, X, RING, RING_U, RING_M, ZERO, PANEL, OTHER = range(9)
    compute = functools.partial(dots, spots, act, grad, group=shard_rows)

    s0 = sibling(val)
    both = jnp.concatenate([jnp.where(c == 0, val, s0), jnp.where(c == 0, s0, val)], axis=1)
    u0 = lax.dynamic_slice_in_dim(both, (width - lent) * g, lent, 2)
    m0 = both[:, :, lent:width - lent]
    x0 = lax.dynamic_slice_in_dim(both, (width - lent) * (1 - g), lent, 2)
    blocks = lambda row, u, m, x: [(u, row, U, None), (m, row, M, None), (x, row, X, None)]
    u1 = ring(u0)
    m1 = ring(m0)
    x1, u2, fu1 = across(u1), ring(u1), sibling(u1)
    m1, *small = tie((m1, *small))
    m2, fm1 = ring(m1), sibling(m1)
    x2, u3, fu2 = across(u2), ring(u2), sibling(u2)
    m3, fm2 = ring(m2), sibling(m2)
    fx1 = sibling(x1)
    k1 = compute(
        pieces=blocks(0, u0, m0, x0) + blocks(pair, u1, m1, x1) + blocks(2 * pair, fu1, fm1, fx1),
        rows=3 * pair, width=width, chunk=width // 8, begin=None,
    )
    u3, k1 = tie((u3, k1))
    x3, u4, fu3 = across(u3), ring(mine(u3)), sibling(u3)
    m4, fm3 = ring(mine(m3)), sibling(m3)
    fx2 = sibling(x2)
    k2 = compute(
        pieces=blocks(0, u2, m2, x2) + blocks(pair, fu2, fm2, fx2),
        rows=2 * pair, width=width, chunk=width // 8, begin=None,
    )
    x3, k2 = tie((x3, k2))
    c4, fx3 = ring(mine(x3)), sibling(x3)
    fu4, fm4 = sibling(u4), sibling(m4)
    early = [(0, u3, m3, None), (pair, fu3, fm3, None), (2 * pair, u4, m4, PANEL), (2 * pair, fu4, fm4, OTHER)]
    part = compute(
        pieces=[p for row, u, m, panel in early for p in ((u, row, RING_U, panel), (m, row, RING_M, panel))],
        rows=3 * pair, width=width - lent, chunk=(width - lent) // 5, begin=RING, sums=False,
    )
    c4, *part = tie((c4, *part))
    fc4 = sibling(c4)
    k3 = compute(
        pieces=[(x3, 0, ZERO, None), (fx3, pair, ZERO, None), (c4, 2 * pair, ZERO, PANEL), (fc4, 2 * pair, ZERO, OTHER)],
        rows=3 * pair, width=lent, chunk=lent, begin=X, before=part,
    )
    ahead, back = 2 * c - 1, 1 - 2 * c
    ids = sources(0)
    for step in (1, 2, 3):
        ids += sources(step * ahead) + sources(step * back)
    ids += sources(4)
    return jnp.concatenate([k1, k2, k3]), jnp.stack(ids), small


def shards(act, grad, val_panels, row_domain, block_tasks, block_live, domain_tokens):
    row_count, width = act.shape
    block_count = block_live.shape[0]
    block_rows = row_count // block_count
    n_dp = lax.axis_size("dp")
    owned = domain_tokens.shape[0]
    cap = 2 * row_count // n_dp
    task_ids = jnp.arange(TASKS, dtype=jnp.int32)

    if n_dp == 16 and lax.axis_size("groups") == 2:
        small = (row_domain, block_tasks, block_live, domain_tokens)
        sums, ids, small = ring_products(act, grad, val_panels, small)
        row_domain, block_tasks, block_live, domain_tokens = small
        to_task = (ids[None, :] == task_ids[:, None]).astype(jnp.float32)
        per_task = lax.dot_general(to_task, sums, (((1,), (0,)), ((), ())), precision=HIGH)
    else:
        rows = lax.all_gather(val_panels, "dp", axis=1, tiled=True)
        ghost = row_products(rows[0], act) * row_products(rows[1], grad)
        per_task = jnp.sum(ghost.reshape(TASKS, -1, row_count), axis=1)

    paired = jnp.sum((block_tasks[:, None, :] == task_ids[None, :, None]).astype(jnp.float32), axis=2)
    weights = paired * block_live.astype(jnp.float32)[:, None]
    weights = jnp.broadcast_to(weights.T[:, :, None], (TASKS, block_count, block_rows)).reshape(TASKS, row_count)

    owner = row_domain // owned
    local = row_domain % owned
    at_owner = (owner[:, None] == jnp.arange(n_dp, dtype=jnp.int32)[None, :])
    before = jnp.arange(row_count)[:, None] > jnp.arange(row_count)[None, :]
    rank = lax.dot_general(
        before.astype(jnp.bfloat16), at_owner.astype(jnp.bfloat16), (((1,), (0,)), ((), ())),
        preferred_element_type=jnp.float32,
    )
    rank = jnp.sum(jnp.where(at_owner, rank, 0.0), axis=1).astype(jnp.int32)
    place = owner * cap + rank
    pack = (place[:, None] == jnp.arange(n_dp * cap, dtype=jnp.int32)[None, :]).astype(jnp.float32)

    row_task = per_task * (weights / width)
    sent = jnp.concatenate([row_task, (local + 1).astype(jnp.float32)[None, :]])
    packed = lax.dot_general(sent, pack, (((1,), (0,)), ((), ())), precision=HIGH)
    packed = packed.reshape(TASKS + 1, n_dp, cap).transpose(1, 0, 2)
    theirs = lax.all_to_all(packed, "dp", 0, 0, tiled=True)
    their_local = theirs[:, TASKS].astype(jnp.int32)
    spread = (their_local[:, :, None] == 1 + jnp.arange(owned, dtype=jnp.int32)).astype(jnp.float32)
    totals = lax.dot_general(theirs[:, :TASKS], spread, (((0, 2), (0, 1)), ((), ())), precision=HIGH)
    return totals / jnp.sqrt(domain_tokens.astype(jnp.float32))[None, :]


def solution(mesh):
    return jax.shard_map(
        shards,
        mesh=mesh,
        in_specs=(
            P(("groups", "dp"), None),
            P(("groups", "dp"), None),
            P(None, "dp", None),
            P(("groups", "dp")),
            P(("groups", "dp"), None),
            P(("groups", "dp")),
            P(("groups", "dp")),
        ),
        out_specs=P(None, ("groups", "dp")),
        check_vma=False,
    )
```

```python
import jax
import jax.numpy as jnp
from jax import lax
from jax.sharding import PartitionSpec as P

TASKS = 16
AXES = ("groups", "dp")
HIGH = lax.Precision.HIGHEST


def scores(act, grad, rows):
    dims = (((1,), (1,)), ((), ()))
    left = lax.dot_general(rows[0], act, dims, preferred_element_type=jnp.float32)
    right = lax.dot_general(rows[1], grad, dims, preferred_element_type=jnp.float32)
    return left * right


def ring_products(act, grad, val, small):
    third = val.shape[1] // 3
    row_count = act.shape[0]
    g = lax.axis_index("groups")
    d = lax.axis_index("dp")
    z, y, c = d // 4, (d // 2) % 2, d % 2
    spot = jnp.where(y == 0, z, 7 - z)
    every = [(gg, pp, cc) for gg in range(2) for pp in range(8) for cc in range(2)]

    def flat(gg, pp, cc):
        pp = pp % 8
        zz, yy = (pp, 0) if pp < 4 else (7 - pp, 1)
        return gg * 16 + zz * 4 + yy * 2 + cc

    def ring(x):
        perm = [(flat(gg, pp, cc), flat(gg, pp + 1 - 2 * cc, cc)) for gg, pp, cc in every]
        return lax.ppermute(x, AXES, perm)

    def across(x):
        return lax.ppermute(x, AXES, [(flat(*e), flat(1 - e[0], e[1], e[2])) for e in every])

    def sibling(x):
        return lax.ppermute(x, AXES, [(flat(*e), flat(e[0], e[1], 1 - e[2])) for e in every])

    def source(step, core):
        pp = lax.rem(spot + step + 8, 8)
        zz = jnp.where(pp < 4, pp, 7 - pp)
        yy = jnp.where(pp < 4, 0, 1)
        return zz * 4 + yy * 2 + core

    def products(rows):
        count = rows.shape[1] // third
        return jnp.sum(scores(act, grad, rows).reshape(count, third, row_count), axis=1)

    tie = lax.optimization_barrier
    cat = lambda *xs: jnp.concatenate(xs, axis=1)
    two = lambda v: cat(v[:, :third], lax.dynamic_slice_in_dim(v, third * (1 + g), third, 1))

    *small, token = small

    def seen(x):
        nonlocal token
        x, token = tie((x, token))
        return x

    def cross(x):
        perm = [(flat(gg, pp, cc), flat(gg, pp - 1 + 2 * cc, 1 - cc)) for gg, pp, cc in every]
        return lax.ppermute(x, AXES, perm)

    own = cat(val[:, :third], jnp.where(g == 0, val[:, third:2 * third], val[:, 2 * third:]))
    a1 = ring(own)
    a1 = seen(a1)
    b1 = cross(own)
    b1 = seen(b1)
    xa1 = across(a1[:, third:])
    xa1 = seen(xa1)
    *small, token = tie((*small, token))
    a2 = ring(a1)
    a2 = seen(a2)
    xb1 = across(b1[:, third:])
    xb1 = seen(xb1)
    a3 = ring(a2)
    a3 = seen(a3)
    xa2 = across(a2[:, third:])
    xa2 = seen(xa2)
    h1 = cat(a1, xa1, b1, xb1)
    f1 = sibling(h1)
    f1 = seen(f1)
    s0 = sibling(val)
    r1 = products(cat(val, s0, h1, f1))
    r1 = seen(r1)
    b2 = ring(b1)
    xb2 = across(b2[:, third:])
    xb2 = seen(xb2)
    b3 = ring(b2)
    b3 = seen(b3)
    h2 = cat(a2, xa2, b2, xb2)
    f2 = sibling(h2)
    f2 = seen(f2)
    r2 = products(cat(h2, f2))
    r2 = seen(r2)
    a4 = ring(a3)
    a4 = seen(a4)
    xa3 = across(a3[:, third:])
    xa3 = seen(xa3)
    c3 = ring(xb2)
    c3 = seen(c3)
    h3 = cat(a3, xa3, b3, c3)
    f3 = sibling(h3)
    c4 = ring(xa3)
    f4 = sibling(a4)
    e4 = sibling(c4)
    r3 = products(cat(h3, f3, a4, c4, f4, e4))
    small = [*small, token]

    near, far = c, 1 - c
    ahead, back = 2 * c - 1, 1 - 2 * c
    ids = [source(0, near)] * 3 + [source(0, far)] * 3
    for step in (1, 2, 3):
        ids += [source(step * ahead, near)] * 3 + [source(step * ahead, far)] * 3
        ids += [source(step * back, far)] * 3 + [source(step * back, near)] * 3
    ids += [source(4, near)] * 3 + [source(4, far)] * 3
    return jnp.concatenate([r1, r2, r3]), jnp.stack(ids), small


def shards(act, grad, val_panels, row_domain, block_tasks, block_live, domain_tokens):
    row_count, width = act.shape
    block_count = block_live.shape[0]
    block_rows = row_count // block_count
    n_dp = lax.axis_size("dp")
    owned = domain_tokens.shape[0]
    cap = 2 * row_count // n_dp
    task_ids = jnp.arange(TASKS, dtype=jnp.int32)

    if n_dp == 16 and lax.axis_size("groups") == 2:
        small = (row_domain, block_tasks, block_live, domain_tokens)
        sums, ids, small = ring_products(act, grad, val_panels, small)
        row_domain, block_tasks, block_live, domain_tokens = small
        to_task = (ids[None, :] == task_ids[:, None]).astype(jnp.float32)
        per_task = lax.dot_general(to_task, sums, (((1,), (0,)), ((), ())), precision=HIGH)
    else:
        rows = lax.all_gather(val_panels, "dp", axis=1, tiled=True)
        per_task = jnp.sum(scores(act, grad, rows).reshape(TASKS, -1, row_count), axis=1)

    paired = jnp.sum((block_tasks[:, None, :] == task_ids[None, :, None]).astype(jnp.float32), axis=2)
    weights = paired * block_live.astype(jnp.float32)[:, None]
    weights = jnp.broadcast_to(weights.T[:, :, None], (TASKS, block_count, block_rows)).reshape(TASKS, row_count)

    owner = row_domain // owned
    local = row_domain % owned
    at_owner = (owner[:, None] == jnp.arange(n_dp, dtype=jnp.int32)[None, :])
    before = jnp.arange(row_count)[:, None] > jnp.arange(row_count)[None, :]
    rank = lax.dot_general(
        before.astype(jnp.bfloat16), at_owner.astype(jnp.bfloat16), (((1,), (0,)), ((), ())),
        preferred_element_type=jnp.float32,
    )
    rank = jnp.sum(jnp.where(at_owner, rank, 0.0), axis=1).astype(jnp.int32)
    place = owner * cap + rank
    pack = (place[:, None] == jnp.arange(n_dp * cap, dtype=jnp.int32)[None, :]).astype(jnp.float32)

    row_task = per_task * (weights / width)
    sent = jnp.concatenate([row_task, (local + 1).astype(jnp.float32)[None, :]])
    packed = lax.dot_general(sent, pack, (((1,), (0,)), ((), ())), precision=HIGH)
    packed = packed.reshape(TASKS + 1, n_dp, cap).transpose(1, 0, 2)
    theirs = lax.all_to_all(packed, "dp", 0, 0, tiled=True)
    their_local = theirs[:, TASKS].astype(jnp.int32)
    spread = (their_local[:, :, None] == 1 + jnp.arange(owned, dtype=jnp.int32)).astype(jnp.float32)
    totals = lax.dot_general(theirs[:, :TASKS], spread, (((0, 2), (0, 1)), ((), ())), precision=HIGH)
    return totals / jnp.sqrt(domain_tokens.astype(jnp.float32))[None, :]


def solution(mesh):
    return jax.shard_map(
        shards,
        mesh=mesh,
        in_specs=(
            P(("groups", "dp"), None),
            P(("groups", "dp"), None),
            P(None, "dp", None),
            P(("groups", "dp")),
            P(("groups", "dp"), None),
            P(("groups", "dp")),
            P(("groups", "dp")),
        ),
        out_specs=P(None, ("groups", "dp")),
        check_vma=False,
    )
```

```python
import functools

import jax
import jax.numpy as jnp
from jax import lax
from jax.experimental import pallas as pl
from jax.experimental.pallas import tpu as pltpu
from jax.sharding import PartitionSpec as P

TASKS = 16
AXES = ("groups", "dp")
HALF = 64


def three_parts(values):
    top = values.astype(jnp.bfloat16)
    rest = values - top.astype(jnp.float32)
    middle = rest.astype(jnp.bfloat16)
    last = (rest - middle.astype(jnp.float32)).astype(jnp.bfloat16)
    return jnp.concatenate([top, middle, last])


def choose(values, choice):
    m = values.shape[0]
    product = lax.dot_general(
        three_parts(values), choice.astype(jnp.bfloat16), (((1,), (1,)), ((), ())), preferred_element_type=jnp.float32
    )
    return product[:m] + product[m:2 * m] + product[2 * m:]


def pack_kernel(each, arrays, tasks_ref, *refs):
    sums, (weights, place, marks, out, by_task) = refs[:arrays], refs[arrays:]
    position = 0
    for ref in sums:
        for k in range(0, ref.shape[0], each):
            by_task[pl.ds(tasks_ref[position], 1), :] = jnp.sum(ref[k:k + each, :], axis=0, keepdims=True)
            position += 1
    row_task = by_task[...] * weights[...]
    owners, half_tasks, lanes = out.shape
    low = lax.broadcasted_iota(jnp.int32, (half_tasks, lanes), 1) < HALF
    slot = lax.broadcasted_iota(jnp.int32, (2 * lanes, place.shape[1]), 0)
    slot = slot // lanes * HALF + slot % HALF
    for owner in range(0, owners, 2):
        packed = choose(row_task, (place[...] == slot + owner * HALF).astype(jnp.float32))
        for k in range(2):
            part = packed[:, k * lanes:(k + 1) * lanes]
            out[owner + k] = jnp.where(low, part[:half_tasks], part[half_tasks:]) + marks[owner + k]


def pack(sums, tasks, weights, place, marks):
    each = sum(s.shape[0] for s in sums) // tasks.shape[0]
    inside = pl.BlockSpec(memory_space=pltpu.VMEM)
    return pl.pallas_call(
        functools.partial(pack_kernel, each, len(sums)),
        out_shape=jax.ShapeDtypeStruct(marks.shape, jnp.float32),
        in_specs=[pl.BlockSpec(memory_space=pltpu.SMEM)] + [inside] * (len(sums) + 3),
        out_specs=inside,
        scratch_shapes=[pltpu.VMEM(weights.shape, jnp.float32)],
    )(tasks, *sums, weights, place, marks)


def finish_kernel(cap, theirs, tokens, out):
    senders, half_tasks, lanes = theirs.shape
    owned = out.shape[1]
    spare = HALF - cap
    lane = lax.broadcasted_iota(jnp.int32, (senders, lanes), 1)
    domain = jnp.zeros((senders, lanes), jnp.float32)
    for line in range(-(-cap // spare)):
        first = line * spare
        moved = pltpu.roll(theirs[:, line, :], (first - cap) % lanes, 1)
        domain = jnp.where((lane >= first) & (lane < min(cap, first + spare)), moved, domain)
    domain = domain + pltpu.roll(domain, HALF, 1)
    low = lax.broadcasted_iota(jnp.int32, (half_tasks, lanes), 1) < HALF
    mine = lax.broadcasted_iota(jnp.int32, (owned, lanes), 0).astype(jnp.float32) + 1.0
    total = jnp.zeros((2 * half_tasks, owned), jnp.float32)
    for sender in range(0, senders, 2):
        values, choice = [], []
        for k in (sender, sender + 1):
            tile = theirs[k]
            values.append(jnp.concatenate([jnp.where(low, tile, 0.0), jnp.where(low, 0.0, tile)]))
            choice.append((domain[k:k + 1, :] == mine).astype(jnp.float32))
        total += choose(jnp.concatenate(values, axis=1), jnp.concatenate(choice, axis=1))
    out[...] = total / jnp.sqrt(tokens[...].astype(jnp.float32))


def finish(theirs, tokens, cap):
    inside = pl.BlockSpec(memory_space=pltpu.VMEM)
    return pl.pallas_call(
        functools.partial(finish_kernel, cap),
        out_shape=jax.ShapeDtypeStruct((TASKS, tokens.shape[0]), jnp.float32),
        in_specs=[inside] * 2,
        out_specs=inside,
    )(theirs, tokens[None, :])


def scores(act, grad, rows):
    dims = (((1,), (1,)), ((), ()))
    left = lax.dot_general(rows[0], act, dims, preferred_element_type=jnp.float32)
    right = lax.dot_general(rows[1], grad, dims, preferred_element_type=jnp.float32)
    return left * right


def ring_products(act, grad, val, small):
    third = val.shape[1] // 3
    row_count = act.shape[0]
    g = lax.axis_index("groups")
    d = lax.axis_index("dp")
    z, y, c = d // 4, (d // 2) % 2, d % 2
    spot = jnp.where(y == 0, z, 7 - z)
    every = [(gg, pp, cc) for gg in range(2) for pp in range(8) for cc in range(2)]

    def flat(gg, pp, cc):
        pp = pp % 8
        zz, yy = (pp, 0) if pp < 4 else (7 - pp, 1)
        return gg * 16 + zz * 4 + yy * 2 + cc

    def ring(x):
        perm = [(flat(gg, pp, cc), flat(gg, pp + 1 - 2 * cc, cc)) for gg, pp, cc in every]
        return lax.ppermute(x, AXES, perm)

    def across(x):
        return lax.ppermute(x, AXES, [(flat(*e), flat(1 - e[0], e[1], e[2])) for e in every])

    def sibling(x):
        return lax.ppermute(x, AXES, [(flat(*e), flat(e[0], e[1], 1 - e[2])) for e in every])

    def source(step, core):
        pp = lax.rem(spot + step + 8, 8)
        zz = jnp.where(pp < 4, pp, 7 - pp)
        yy = jnp.where(pp < 4, 0, 1)
        return zz * 4 + yy * 2 + core

    def products(rows):
        return jnp.sum(scores(act, grad, rows).reshape(-1, third, row_count), axis=1)

    tie = lax.optimization_barrier
    cat = lambda *xs: jnp.concatenate(xs, axis=1)

    *small, token = small

    def seen(x):
        nonlocal token
        x, token = tie((x, token))
        return x

    def cross(x):
        perm = [(flat(gg, pp, cc), flat(gg, pp - 1 + 2 * cc, 1 - cc)) for gg, pp, cc in every]
        return lax.ppermute(x, AXES, perm)

    two = lambda v: cat(v[:, :third], jnp.where(g == 0, v[:, third:2 * third], v[:, 2 * third:]))
    own = two(val)
    a1 = ring(own)
    a1 = seen(a1)
    xa1 = across(a1[:, third:])
    xa1 = seen(xa1)
    a2 = ring(a1)
    a2 = seen(a2)
    b1 = cross(own)
    xb1 = across(b1[:, third:])
    xb1 = seen(xb1)
    a3 = ring(a2)
    a3 = seen(a3)
    xa2 = across(a2[:, third:])
    xa2 = seen(xa2)
    s0 = sibling(val)
    h1 = cat(a1, xa1, b1, xb1)
    f1 = sibling(h1)
    r1 = products(cat(val, s0, h1, f1))
    r1 = seen(r1)
    b2 = ring(b1)
    xb2 = across(b2[:, third:])
    xb2 = seen(xb2)
    b3 = ring(b2)
    b3 = seen(b3)
    h2 = cat(a2, xa2, b2, xb2)
    f2 = sibling(h2)
    f2 = seen(f2)
    xa3 = across(a3[:, third:])
    xa3 = seen(xa3)
    r2 = products(cat(h2, f2))
    r2 = seen(r2)
    c3 = ring(xb2)
    h3 = cat(a3, xa3, b3, c3)
    f3 = sibling(h3)
    a4 = ring(a3)
    c4 = ring(xa3)
    f4 = sibling(a4)
    e4 = sibling(c4)
    r3 = products(cat(h3, f3, a4, c4, f4, e4))
    small = [*small, token]

    near, far = c, 1 - c
    ahead, back = 2 * c - 1, 1 - 2 * c
    ids = []
    ids += [source(0, near), source(0, far)]
    for step in (1, 2, 3):
        ids += [source(step * ahead, near), source(step * ahead, far)]
        ids += [source(step * back, far), source(step * back, near)]
    ids += [source(4, near), source(4, far)]
    return [r1, r2, r3], jnp.stack(ids), small


def shards(act, grad, val_panels, row_domain, block_tasks, block_live, domain_tokens):
    row_count, width = act.shape
    block_count = block_live.shape[0]
    block_rows = row_count // block_count
    n_dp = lax.axis_size("dp")
    owned = domain_tokens.shape[0]
    cap = 2 * row_count // n_dp
    task_ids = jnp.arange(TASKS, dtype=jnp.int32)

    if n_dp == 16 and lax.axis_size("groups") == 2:
        small = (row_domain, block_tasks, block_live, domain_tokens)
        sums, ids, small = ring_products(act, grad, val_panels, small)
        row_domain, block_tasks, block_live, domain_tokens = small
    else:
        rows = lax.all_gather(val_panels, "dp", axis=1, tiled=True)
        sums, ids = [jnp.sum(scores(act, grad, rows).reshape(TASKS, -1, row_count), axis=1)], task_ids

    paired = jnp.sum((block_tasks[:, None, :] == task_ids[None, :, None]).astype(jnp.float32), axis=2)
    weights = paired * block_live.astype(jnp.float32)[:, None]
    weights = jnp.broadcast_to(weights.T[:, :, None], (TASKS, block_count, block_rows)).reshape(TASKS, row_count)

    owner = row_domain // owned
    local = row_domain % owned
    at_owner = (owner[:, None] == jnp.arange(n_dp, dtype=jnp.int32)[None, :])
    before = jnp.arange(row_count)[:, None] > jnp.arange(row_count)[None, :]
    rank = lax.dot_general(
        before.astype(jnp.bfloat16), at_owner.astype(jnp.bfloat16), (((1,), (0,)), ((), ())),
        preferred_element_type=jnp.float32,
    )
    rank = jnp.sum(jnp.where(at_owner, rank, 0.0), axis=1).astype(jnp.int32)
    place = (owner * HALF + rank)[None, :]
    spare = HALF - cap
    lines = -(-cap // spare)
    home = at_owner[:, :, None] & (rank[:, None, None] == jnp.arange(lines * spare, dtype=jnp.int32))
    marks = jnp.sum(jnp.where(home, (local + 1).astype(jnp.float32)[:, None, None], 0.0), axis=0)
    marks = jnp.pad(marks.reshape(n_dp, lines, spare), ((0, 0), (0, TASKS // 2 - lines), (cap, HALF)))

    packed = pack(sums, ids, weights / width, place, marks)
    theirs = lax.all_to_all(packed, "dp", 0, 0, tiled=True)
    return finish(theirs, domain_tokens, cap)


def solution(mesh):
    return jax.shard_map(
        shards,
        mesh=mesh,
        in_specs=(
            P(("groups", "dp"), None),
            P(("groups", "dp"), None),
            P(None, "dp", None),
            P(("groups", "dp")),
            P(("groups", "dp"), None),
            P(("groups", "dp")),
            P(("groups", "dp")),
        ),
        out_specs=P(None, ("groups", "dp")),
        check_vma=False,
    )
```

```python
import functools

import jax
import jax.numpy as jnp
from jax import lax
from jax.experimental import pallas as pl
from jax.experimental.pallas import tpu as pltpu
from jax.sharding import PartitionSpec as P

TASKS = 16
AXES = ("groups", "dp")
HALF = 64


def three_parts(values):
    top = values.astype(jnp.bfloat16)
    rest = values - top.astype(jnp.float32)
    middle = rest.astype(jnp.bfloat16)
    last = (rest - middle.astype(jnp.float32)).astype(jnp.bfloat16)
    return jnp.concatenate([top, middle, last])


def choose(values, choice):
    m = values.shape[0]
    product = lax.dot_general(
        three_parts(values), choice.astype(jnp.bfloat16), (((1,), (1,)), ((), ())), preferred_element_type=jnp.float32
    )
    return product[:m] + product[m:2 * m] + product[2 * m:]


def pack_kernel(each, arrays, tasks_ref, *refs):
    sums, (weights, place, marks, out, by_task) = refs[:arrays], refs[arrays:]
    position = 0
    for ref in sums:
        for k in range(0, ref.shape[0], each):
            by_task[pl.ds(tasks_ref[position], 1), :] = jnp.sum(ref[k:k + each, :], axis=0, keepdims=True)
            position += 1
    row_task = by_task[...] * weights[...]
    owners, half_tasks, lanes = out.shape
    low = lax.broadcasted_iota(jnp.int32, (half_tasks, lanes), 1) < HALF
    slot = lax.broadcasted_iota(jnp.int32, (2 * lanes, place.shape[1]), 0)
    slot = slot // lanes * HALF + slot % HALF
    for owner in range(0, owners, 2):
        packed = choose(row_task, (place[...] == slot + owner * HALF).astype(jnp.float32))
        for k in range(2):
            part = packed[:, k * lanes:(k + 1) * lanes]
            out[owner + k] = jnp.where(low, part[:half_tasks], part[half_tasks:]) + marks[owner + k]


def pack(sums, tasks, weights, place, marks):
    each = sum(s.shape[0] for s in sums) // tasks.shape[0]
    inside = pl.BlockSpec(memory_space=pltpu.VMEM)
    return pl.pallas_call(
        functools.partial(pack_kernel, each, len(sums)),
        out_shape=jax.ShapeDtypeStruct(marks.shape, jnp.float32),
        in_specs=[pl.BlockSpec(memory_space=pltpu.SMEM)] + [inside] * (len(sums) + 3),
        out_specs=inside,
        scratch_shapes=[pltpu.VMEM(weights.shape, jnp.float32)],
        compiler_params=pltpu.CompilerParams(vmem_limit_bytes=8 * 1024 * 1024),
    )(tasks, *sums, weights, place, marks)


def finish_kernel(cap, theirs, tokens, out):
    senders, half_tasks, lanes = theirs.shape
    owned = out.shape[1]
    spare = HALF - cap
    lane = lax.broadcasted_iota(jnp.int32, (senders, lanes), 1)
    domain = jnp.zeros((senders, lanes), jnp.float32)
    for line in range(-(-cap // spare)):
        first = line * spare
        moved = pltpu.roll(theirs[:, line, :], (first - cap) % lanes, 1)
        domain = jnp.where((lane >= first) & (lane < min(cap, first + spare)), moved, domain)
    domain = domain + pltpu.roll(domain, HALF, 1)
    low = lax.broadcasted_iota(jnp.int32, (half_tasks, lanes), 1) < HALF
    mine = lax.broadcasted_iota(jnp.int32, (owned, lanes), 0).astype(jnp.float32) + 1.0
    total = jnp.zeros((2 * half_tasks, owned), jnp.float32)
    for sender in range(0, senders, 2):
        values, choice = [], []
        for k in (sender, sender + 1):
            tile = theirs[k]
            values.append(jnp.concatenate([jnp.where(low, tile, 0.0), jnp.where(low, 0.0, tile)]))
            choice.append((domain[k:k + 1, :] == mine).astype(jnp.float32))
        total += choose(jnp.concatenate(values, axis=1), jnp.concatenate(choice, axis=1))
    out[...] = total / jnp.sqrt(tokens[...].astype(jnp.float32))


def finish(theirs, tokens, cap):
    inside = pl.BlockSpec(memory_space=pltpu.VMEM)
    return pl.pallas_call(
        functools.partial(finish_kernel, cap),
        out_shape=jax.ShapeDtypeStruct((TASKS, tokens.shape[0]), jnp.float32),
        in_specs=[inside] * 2,
        out_specs=inside,
        compiler_params=pltpu.CompilerParams(vmem_limit_bytes=8 * 1024 * 1024),
    )(theirs, tokens[None, :])


def scores(act, grad, rows):
    dims = (((1,), (1,)), ((), ()))
    left = lax.dot_general(rows[0], act, dims, preferred_element_type=jnp.float32)
    right = lax.dot_general(rows[1], grad, dims, preferred_element_type=jnp.float32)
    return left * right


def ring_products(act, grad, val, small):
    third = val.shape[1] // 3
    row_count = act.shape[0]
    g = lax.axis_index("groups")
    d = lax.axis_index("dp")
    z, y, c = d // 4, (d // 2) % 2, d % 2
    spot = jnp.where(y == 0, z, 7 - z)
    every = [(gg, pp, cc) for gg in range(2) for pp in range(8) for cc in range(2)]

    def flat(gg, pp, cc):
        pp = pp % 8
        zz, yy = (pp, 0) if pp < 4 else (7 - pp, 1)
        return gg * 16 + zz * 4 + yy * 2 + cc

    def ring(x):
        perm = [(flat(gg, pp, cc), flat(gg, pp + 1 - 2 * cc, cc)) for gg, pp, cc in every]
        return lax.ppermute(x, AXES, perm)

    def across(x):
        return lax.ppermute(x, AXES, [(flat(*e), flat(1 - e[0], e[1], e[2])) for e in every])

    def sibling(x):
        return lax.ppermute(x, AXES, [(flat(*e), flat(e[0], e[1], 1 - e[2])) for e in every])

    def source(step, core):
        pp = lax.rem(spot + step + 8, 8)
        zz = jnp.where(pp < 4, pp, 7 - pp)
        yy = jnp.where(pp < 4, 0, 1)
        return zz * 4 + yy * 2 + core

    def products(rows):
        return jnp.sum(scores(act, grad, rows).reshape(-1, third, row_count), axis=1)

    tie = lax.optimization_barrier
    cat = lambda *xs: jnp.concatenate(xs, axis=1)

    *small, token = small

    def seen(x):
        nonlocal token
        x, token = tie((x, token))
        return x

    def cross(x):
        perm = [(flat(gg, pp, cc), flat(gg, pp - 1 + 2 * cc, 1 - cc)) for gg, pp, cc in every]
        return lax.ppermute(x, AXES, perm)

    two = lambda v: cat(v[:, :third], jnp.where(g == 0, v[:, third:2 * third], v[:, 2 * third:]))
    own = two(val)
    a1 = ring(own)
    a1 = seen(a1)
    xa1 = across(a1[:, third:])
    xa1 = seen(xa1)
    a2 = ring(a1)
    a2 = seen(a2)
    b1 = cross(own)
    xb1 = across(b1[:, third:])
    xb1 = seen(xb1)
    a3 = ring(a2)
    a3 = seen(a3)
    xa2 = across(a2[:, third:])
    xa2 = seen(xa2)
    s0 = sibling(val)
    h1 = cat(a1, xa1, b1, xb1)
    f1 = sibling(h1)
    r1 = products(cat(val, s0, h1, f1))
    r1 = seen(r1)
    b2 = ring(b1)
    xb2 = across(b2[:, third:])
    xb2 = seen(xb2)
    b3 = ring(b2)
    b3 = seen(b3)
    h2 = cat(a2, xa2, b2, xb2)
    f2 = sibling(h2)
    f2 = seen(f2)
    xa3 = across(a3[:, third:])
    xa3 = seen(xa3)
    r2 = products(cat(h2, f2))
    r2 = seen(r2)
    c3 = ring(xb2)
    h3 = cat(a3, xa3, b3, c3)
    f3 = sibling(h3)
    a4 = ring(a3)
    c4 = ring(xa3)
    f4 = sibling(a4)
    e4 = sibling(c4)
    r3 = products(cat(h3, f3, a4, c4, f4, e4))
    small = [*small, token]

    near, far = c, 1 - c
    ahead, back = 2 * c - 1, 1 - 2 * c
    ids = []
    ids += [source(0, near), source(0, far)]
    for step in (1, 2, 3):
        ids += [source(step * ahead, near), source(step * ahead, far)]
        ids += [source(step * back, far), source(step * back, near)]
    ids += [source(4, near), source(4, far)]
    return [r1, r2, r3], jnp.stack(ids), small


def shards(act, grad, val_panels, row_domain, block_tasks, block_live, domain_tokens):
    row_count, width = act.shape
    block_count = block_live.shape[0]
    block_rows = row_count // block_count
    n_dp = lax.axis_size("dp")
    owned = domain_tokens.shape[0]
    cap = 2 * row_count // n_dp
    task_ids = jnp.arange(TASKS, dtype=jnp.int32)

    if n_dp == 16 and lax.axis_size("groups") == 2:
        small = (row_domain, block_tasks, block_live, domain_tokens)
        sums, ids, small = ring_products(act, grad, val_panels, small)
        row_domain, block_tasks, block_live, domain_tokens = small
    else:
        rows = lax.all_gather(val_panels, "dp", axis=1, tiled=True)
        sums, ids = [jnp.sum(scores(act, grad, rows).reshape(TASKS, -1, row_count), axis=1)], task_ids

    paired = jnp.sum((block_tasks[:, None, :] == task_ids[None, :, None]).astype(jnp.float32), axis=2)
    weights = paired * block_live.astype(jnp.float32)[:, None]
    weights = jnp.broadcast_to(weights.T[:, :, None], (TASKS, block_count, block_rows)).reshape(TASKS, row_count)

    owner = row_domain // owned
    local = row_domain % owned
    at_owner = (owner[:, None] == jnp.arange(n_dp, dtype=jnp.int32)[None, :])
    before = jnp.arange(row_count)[:, None] > jnp.arange(row_count)[None, :]
    rank = lax.dot_general(
        before.astype(jnp.bfloat16), at_owner.astype(jnp.bfloat16), (((1,), (0,)), ((), ())),
        preferred_element_type=jnp.float32,
    )
    rank = jnp.sum(jnp.where(at_owner, rank, 0.0), axis=1).astype(jnp.int32)
    place = (owner * HALF + rank)[None, :]
    spare = HALF - cap
    lines = -(-cap // spare)
    home = at_owner[:, :, None] & (rank[:, None, None] == jnp.arange(lines * spare, dtype=jnp.int32))
    marks = jnp.sum(jnp.where(home, (local + 1).astype(jnp.float32)[:, None, None], 0.0), axis=0)
    marks = jnp.pad(marks.reshape(n_dp, lines, spare), ((0, 0), (0, TASKS // 2 - lines), (cap, HALF)))

    packed = pack(sums, ids, weights / width, place, marks)
    inner, outer = 4, n_dp // 4
    near = [[q * inner + r for r in range(inner)] for q in range(outer)]
    far = [[q * inner + r for q in range(outer)] for r in range(inner)]
    tiles = packed.shape[1:]
    packed = packed.reshape(outer, inner, *tiles).swapaxes(0, 1)
    packed = lax.all_to_all(packed, "dp", 0, 0, axis_index_groups=near, tiled=True)
    packed = packed.swapaxes(0, 1)
    theirs = lax.all_to_all(packed, "dp", 0, 0, axis_index_groups=far, tiled=True).reshape(n_dp, *tiles)
    return finish(theirs, domain_tokens, cap)


def solution(mesh):
    return jax.shard_map(
        shards,
        mesh=mesh,
        in_specs=(
            P(("groups", "dp"), None),
            P(("groups", "dp"), None),
            P(None, "dp", None),
            P(("groups", "dp")),
            P(("groups", "dp"), None),
            P(("groups", "dp")),
            P(("groups", "dp")),
        ),
        out_specs=P(None, ("groups", "dp")),
        check_vma=False,
    )
```

```python
import functools

import jax
import jax.numpy as jnp
from jax import lax
from jax.experimental import pallas as pl
from jax.experimental.pallas import tpu as pltpu
from jax.sharding import PartitionSpec as P

TASKS = 16
AXES = ("groups", "dp")
HALF = 64


def three_parts(values):
    top = values.astype(jnp.bfloat16)
    rest = values - top.astype(jnp.float32)
    middle = rest.astype(jnp.bfloat16)
    last = (rest - middle.astype(jnp.float32)).astype(jnp.bfloat16)
    return jnp.concatenate([top, middle, last])


def choose(values, choice):
    m = values.shape[0]
    product = lax.dot_general(
        three_parts(values), choice.astype(jnp.bfloat16), (((1,), (1,)), ((), ())), preferred_element_type=jnp.float32
    )
    return product[:m] + product[m:2 * m] + product[2 * m:]


def pack_kernel(each, arrays, tasks_ref, *refs):
    sums, (weights, place, marks, out, by_task) = refs[:arrays], refs[arrays:]
    position = 0
    for ref in sums:
        for k in range(0, ref.shape[0], each):
            by_task[pl.ds(tasks_ref[position], 1), :] = jnp.sum(ref[k:k + each, :], axis=0, keepdims=True)
            position += 1
    row_task = by_task[...] * weights[...]
    owners, half_tasks, lanes = out.shape
    low = lax.broadcasted_iota(jnp.int32, (half_tasks, lanes), 1) < HALF
    slot = lax.broadcasted_iota(jnp.int32, (2 * lanes, place.shape[1]), 0)
    slot = slot // lanes * HALF + slot % HALF
    for owner in range(0, owners, 2):
        packed = choose(row_task, (place[...] == slot + owner * HALF).astype(jnp.float32))
        for k in range(2):
            part = packed[:, k * lanes:(k + 1) * lanes]
            out[owner + k] = jnp.where(low, part[:half_tasks], part[half_tasks:]) + marks[owner + k]


def pack(sums, tasks, weights, place, marks):
    each = sum(s.shape[0] for s in sums) // tasks.shape[0]
    inside = pl.BlockSpec(memory_space=pltpu.VMEM)
    return pl.pallas_call(
        functools.partial(pack_kernel, each, len(sums)),
        out_shape=jax.ShapeDtypeStruct(marks.shape, jnp.float32),
        in_specs=[pl.BlockSpec(memory_space=pltpu.SMEM)] + [inside] * (len(sums) + 3),
        out_specs=inside,
        scratch_shapes=[pltpu.VMEM(weights.shape, jnp.float32)],
        compiler_params=pltpu.CompilerParams(vmem_limit_bytes=8 * 1024 * 1024),
    )(tasks, *sums, weights, place, marks)


def finish_kernel(cap, theirs, tokens, out):
    senders, half_tasks, lanes = theirs.shape
    owned = out.shape[1]
    spare = HALF - cap
    lane = lax.broadcasted_iota(jnp.int32, (senders, lanes), 1)
    domain = jnp.zeros((senders, lanes), jnp.float32)
    for line in range(-(-cap // spare)):
        first = line * spare
        moved = pltpu.roll(theirs[:, line, :], (first - cap) % lanes, 1)
        domain = jnp.where((lane >= first) & (lane < min(cap, first + spare)), moved, domain)
    domain = domain + pltpu.roll(domain, HALF, 1)
    low = lax.broadcasted_iota(jnp.int32, (half_tasks, lanes), 1) < HALF
    mine = lax.broadcasted_iota(jnp.int32, (owned, lanes), 0).astype(jnp.float32) + 1.0
    total = jnp.zeros((2 * half_tasks, owned), jnp.float32)
    for sender in range(0, senders, 2):
        values, choice = [], []
        for k in (sender, sender + 1):
            tile = theirs[k]
            values.append(jnp.concatenate([jnp.where(low, tile, 0.0), jnp.where(low, 0.0, tile)]))
            choice.append((domain[k:k + 1, :] == mine).astype(jnp.float32))
        total += choose(jnp.concatenate(values, axis=1), jnp.concatenate(choice, axis=1))
    out[...] = total / jnp.sqrt(tokens[...].astype(jnp.float32))


def finish(theirs, tokens, cap):
    inside = pl.BlockSpec(memory_space=pltpu.VMEM)
    return pl.pallas_call(
        functools.partial(finish_kernel, cap),
        out_shape=jax.ShapeDtypeStruct((TASKS, tokens.shape[0]), jnp.float32),
        in_specs=[inside] * 2,
        out_specs=inside,
        compiler_params=pltpu.CompilerParams(vmem_limit_bytes=8 * 1024 * 1024),
    )(theirs, tokens[None, :])


def scores(act, grad, rows):
    dims = (((1,), (1,)), ((), ()))
    left = lax.dot_general(rows[0], act, dims, preferred_element_type=jnp.float32)
    right = lax.dot_general(rows[1], grad, dims, preferred_element_type=jnp.float32)
    return left * right


def ring_products(act, grad, val, small):
    third = val.shape[1] // 3
    row_count = act.shape[0]
    g = lax.axis_index("groups")
    d = lax.axis_index("dp")
    z, y, c = d // 4, (d // 2) % 2, d % 2
    spot = jnp.where(y == 0, z, 7 - z)
    every = [(gg, pp, cc) for gg in range(2) for pp in range(8) for cc in range(2)]

    def flat(gg, pp, cc):
        pp = pp % 8
        zz, yy = (pp, 0) if pp < 4 else (7 - pp, 1)
        return gg * 16 + zz * 4 + yy * 2 + cc

    def ring(x):
        perm = [(flat(gg, pp, cc), flat(gg, pp + 1 - 2 * cc, cc)) for gg, pp, cc in every]
        return lax.ppermute(x, AXES, perm)

    def across(x):
        return lax.ppermute(x, AXES, [(flat(*e), flat(1 - e[0], e[1], e[2])) for e in every])

    def sibling(x):
        return lax.ppermute(x, AXES, [(flat(*e), flat(e[0], e[1], 1 - e[2])) for e in every])

    def source(step, core):
        pp = lax.rem(spot + step + 8, 8)
        zz = jnp.where(pp < 4, pp, 7 - pp)
        yy = jnp.where(pp < 4, 0, 1)
        return zz * 4 + yy * 2 + core

    def products(rows):
        return jnp.sum(scores(act, grad, rows).reshape(-1, third, row_count), axis=1)

    tie = lax.optimization_barrier
    cat = lambda *xs: jnp.concatenate(xs, axis=1)

    *small, token = small

    def seen(x):
        nonlocal token
        x, token = tie((x, token))
        return x

    def cross(x):
        perm = [(flat(gg, pp, cc), flat(gg, pp - 1 + 2 * cc, 1 - cc)) for gg, pp, cc in every]
        return lax.ppermute(x, AXES, perm)

    two = lambda v: cat(v[:, :third], jnp.where(g == 0, v[:, third:2 * third], v[:, 2 * third:]))
    own = two(val)
    a1 = ring(own)
    a1 = seen(a1)
    xa1 = across(a1[:, third:])
    xa1 = seen(xa1)
    a2 = ring(a1)
    a2 = seen(a2)
    b1 = cross(own)
    xb1 = across(b1[:, third:])
    xb1 = seen(xb1)
    a3 = ring(a2)
    a3 = seen(a3)
    xa2 = across(a2[:, third:])
    xa2 = seen(xa2)
    s0 = sibling(val)
    h1 = cat(a1, xa1, b1, xb1)
    f1 = sibling(h1)
    r1 = products(cat(val, s0, h1, f1))
    r1 = seen(r1)
    b2 = ring(b1)
    xb2 = across(b2[:, third:])
    xb2 = seen(xb2)
    b3 = ring(b2)
    b3 = seen(b3)
    h2 = cat(a2, xa2, b2, xb2)
    f2 = sibling(h2)
    f2 = seen(f2)
    xa3 = across(a3[:, third:])
    xa3 = seen(xa3)
    r2 = products(cat(h2, f2))
    r2 = seen(r2)
    c3 = ring(xb2)
    h3 = cat(a3, xa3, b3, c3)
    f3 = sibling(h3)
    a4 = ring(a3)
    c4 = ring(xa3)
    f4 = sibling(a4)
    e4 = sibling(c4)
    r3 = products(cat(h3, f3, a4, c4, f4, e4))
    small = [*small, token]

    near, far = c, 1 - c
    ahead, back = 2 * c - 1, 1 - 2 * c
    ids = []
    ids += [source(0, near), source(0, far)]
    for step in (1, 2, 3):
        ids += [source(step * ahead, near), source(step * ahead, far)]
        ids += [source(step * back, far), source(step * back, near)]
    ids += [source(4, near), source(4, far)]
    return [r1, r2, r3], jnp.stack(ids), small


def shards(act, grad, val_panels, row_domain, block_tasks, block_live, domain_tokens):
    row_count, width = act.shape
    block_count = block_live.shape[0]
    block_rows = row_count // block_count
    n_dp = lax.axis_size("dp")
    owned = domain_tokens.shape[0]
    cap = 2 * row_count // n_dp
    task_ids = jnp.arange(TASKS, dtype=jnp.int32)

    if n_dp == 16 and lax.axis_size("groups") == 2:
        small = (row_domain, block_tasks, block_live, domain_tokens)
        sums, ids, small = ring_products(act, grad, val_panels, small)
        row_domain, block_tasks, block_live, domain_tokens = small
    else:
        rows = lax.all_gather(val_panels, "dp", axis=1, tiled=True)
        sums, ids = [jnp.sum(scores(act, grad, rows).reshape(TASKS, -1, row_count), axis=1)], task_ids

    paired = jnp.sum((block_tasks[:, None, :] == task_ids[None, :, None]).astype(jnp.float32), axis=2)
    weights = paired * block_live.astype(jnp.float32)[:, None]
    weights = jnp.broadcast_to(weights.T[:, :, None], (TASKS, block_count, block_rows)).reshape(TASKS, row_count)

    owner = row_domain // owned
    local = row_domain % owned
    at_owner = (owner[:, None] == jnp.arange(n_dp, dtype=jnp.int32)[None, :])
    before = jnp.arange(row_count)[:, None] > jnp.arange(row_count)[None, :]
    rank = lax.dot_general(
        before.astype(jnp.bfloat16), at_owner.astype(jnp.bfloat16), (((1,), (0,)), ((), ())),
        preferred_element_type=jnp.float32,
    )
    rank = jnp.sum(jnp.where(at_owner, rank, 0.0), axis=1).astype(jnp.int32)
    place = (owner * HALF + rank)[None, :]
    spare = HALF - cap
    lines = -(-cap // spare)
    home = at_owner[:, :, None] & (rank[:, None, None] == jnp.arange(lines * spare, dtype=jnp.int32))
    marks = jnp.sum(jnp.where(home, (local + 1).astype(jnp.float32)[:, None, None], 0.0), axis=0)
    marks = jnp.pad(marks.reshape(n_dp, lines, spare), ((0, 0), (0, TASKS // 2 - lines), (cap, HALF)))

    packed = pack(sums, ids, weights / width, place, marks)
    theirs = lax.all_to_all(packed, "dp", 0, 0, tiled=True)
    return finish(theirs, domain_tokens, cap)


def solution(mesh):
    return jax.shard_map(
        shards,
        mesh=mesh,
        in_specs=(
            P(("groups", "dp"), None),
            P(("groups", "dp"), None),
            P(None, "dp", None),
            P(("groups", "dp")),
            P(("groups", "dp"), None),
            P(("groups", "dp")),
            P(("groups", "dp")),
        ),
        out_specs=P(None, ("groups", "dp")),
        check_vma=False,
    )
```

```python
import functools

import jax
import jax.numpy as jnp
from jax import lax
from jax.experimental import pallas as pl
from jax.experimental.pallas import tpu as pltpu
from jax.sharding import PartitionSpec as P

TASKS = 16
AXES = ("groups", "dp")
HALF = 64


def three_parts(values):
    top = values.astype(jnp.bfloat16)
    rest = values - top.astype(jnp.float32)
    middle = rest.astype(jnp.bfloat16)
    last = (rest - middle.astype(jnp.float32)).astype(jnp.bfloat16)
    return jnp.concatenate([top, middle, last])


def choose(values, choice):
    m = values.shape[0]
    product = lax.dot_general(
        three_parts(values), choice.astype(jnp.bfloat16), (((1,), (1,)), ((), ())), preferred_element_type=jnp.float32
    )
    return product[:m] + product[m:2 * m] + product[2 * m:]


def pack_kernel(each, arrays, tasks_ref, *refs):
    sums, (weights, place, marks, out, by_task) = refs[:arrays], refs[arrays:]
    position = 0
    for ref in sums:
        for k in range(0, ref.shape[0], each):
            by_task[pl.ds(tasks_ref[position], 1), :] = jnp.sum(ref[k:k + each, :], axis=0, keepdims=True)
            position += 1
    row_task = by_task[...] * weights[...]
    owners, half_tasks, lanes = out.shape
    low = lax.broadcasted_iota(jnp.int32, (half_tasks, lanes), 1) < HALF
    slot = lax.broadcasted_iota(jnp.int32, (2 * lanes, place.shape[1]), 0)
    slot = slot // lanes * HALF + slot % HALF
    for owner in range(0, owners, 2):
        packed = choose(row_task, (place[...] == slot + owner * HALF).astype(jnp.float32))
        for k in range(2):
            part = packed[:, k * lanes:(k + 1) * lanes]
            out[owner + k] = jnp.where(low, part[:half_tasks], part[half_tasks:]) + marks[owner + k]


def pack(sums, tasks, weights, place, marks):
    each = sum(s.shape[0] for s in sums) // tasks.shape[0]
    inside = pl.BlockSpec(memory_space=pltpu.VMEM)
    return pl.pallas_call(
        functools.partial(pack_kernel, each, len(sums)),
        out_shape=jax.ShapeDtypeStruct(marks.shape, jnp.float32),
        in_specs=[pl.BlockSpec(memory_space=pltpu.SMEM)] + [inside] * (len(sums) + 3),
        out_specs=inside,
        scratch_shapes=[pltpu.VMEM(weights.shape, jnp.float32)],
        compiler_params=pltpu.CompilerParams(vmem_limit_bytes=8 * 1024 * 1024),
    )(tasks, *sums, weights, place, marks)


def finish_kernel(cap, theirs, tokens, out):
    senders, half_tasks, lanes = theirs.shape
    owned = out.shape[1]
    spare = HALF - cap
    lane = lax.broadcasted_iota(jnp.int32, (senders, lanes), 1)
    domain = jnp.zeros((senders, lanes), jnp.float32)
    for line in range(-(-cap // spare)):
        first = line * spare
        moved = pltpu.roll(theirs[:, line, :], (first - cap) % lanes, 1)
        domain = jnp.where((lane >= first) & (lane < min(cap, first + spare)), moved, domain)
    domain = domain + pltpu.roll(domain, HALF, 1)
    low = lax.broadcasted_iota(jnp.int32, (half_tasks, lanes), 1) < HALF
    mine = lax.broadcasted_iota(jnp.int32, (owned, lanes), 0).astype(jnp.float32) + 1.0
    total = jnp.zeros((2 * half_tasks, owned), jnp.float32)
    for sender in range(0, senders, 2):
        values, choice = [], []
        for k in (sender, sender + 1):
            tile = theirs[k]
            values.append(jnp.concatenate([jnp.where(low, tile, 0.0), jnp.where(low, 0.0, tile)]))
            choice.append((domain[k:k + 1, :] == mine).astype(jnp.float32))
        total += choose(jnp.concatenate(values, axis=1), jnp.concatenate(choice, axis=1))
    out[...] = total / jnp.sqrt(tokens[...].astype(jnp.float32))


def finish(theirs, tokens, cap):
    inside = pl.BlockSpec(memory_space=pltpu.VMEM)
    return pl.pallas_call(
        functools.partial(finish_kernel, cap),
        out_shape=jax.ShapeDtypeStruct((TASKS, tokens.shape[0]), jnp.float32),
        in_specs=[inside] * 2,
        out_specs=inside,
        compiler_params=pltpu.CompilerParams(vmem_limit_bytes=8 * 1024 * 1024),
    )(theirs, tokens[None, :])


def scores(act, grad, rows):
    dims = (((1,), (1,)), ((), ()))
    left = lax.dot_general(rows[0], act, dims, preferred_element_type=jnp.float32)
    right = lax.dot_general(rows[1], grad, dims, preferred_element_type=jnp.float32)
    return left * right


def ring_products(act, grad, val, small):
    row_count = act.shape[0]
    g = lax.axis_index("groups")
    d = lax.axis_index("dp")
    z, y, c = d // 4, (d // 2) % 2, d % 2
    spot = jnp.where(y == 0, z, 7 - z)
    every = [(gg, pp, cc) for gg in range(2) for pp in range(8) for cc in range(2)]

    def flat(gg, pp, cc):
        pp = pp % 8
        zz, yy = (pp, 0) if pp < 4 else (7 - pp, 1)
        return gg * 16 + zz * 4 + yy * 2 + cc

    def ring(x):
        perm = [(flat(gg, pp, cc), flat(gg, pp + 1 - 2 * cc, cc)) for gg, pp, cc in every]
        return lax.ppermute(x, AXES, perm)

    def across(x):
        return lax.ppermute(x, AXES, [(flat(*e), flat(1 - e[0], e[1], e[2])) for e in every])

    def sibling(x):
        return lax.ppermute(x, AXES, [(flat(*e), flat(e[0], e[1], 1 - e[2])) for e in every])

    def source(step, core):
        pp = lax.rem(spot + step + 8, 8)
        zz = jnp.where(pp < 4, pp, 7 - pp)
        yy = jnp.where(pp < 4, 0, 1)
        return zz * 4 + yy * 2 + core

    def products(rows):
        return jnp.sum(scores(act, grad, rows).reshape(-1, val.shape[1] // 3, row_count), axis=1)

    tie = lax.optimization_barrier
    cat = lambda *xs: jnp.concatenate(xs, axis=1)

    *small, token = small

    def seen(x):
        nonlocal token
        x, token = tie((x, token))
        return x

    def pair(*parts):
        left = [jnp.where(g == 0, p, q) for p, q in parts]
        right = [jnp.where(g == 0, q, p) for p, q in parts]
        return jnp.stack([jnp.concatenate(left), jnp.concatenate(right)])

    def later(rows):
        zero = jnp.zeros((rows.shape[1] // val.shape[1], row_count), jnp.float32)
        return lax.fori_loop(0, jnp.minimum(token[0], 1), lambda i, total: total + products(rows), zero)

    mine = lax.dynamic_index_in_dim(val, g, 0, keepdims=False)
    s1 = sibling(mine)
    s1 = seen(s1)
    a1 = ring(mine)
    a1 = seen(a1)
    b1 = ring(s1)
    b1 = seen(b1)
    xa1 = across(a1)
    xa1 = seen(xa1)
    *small, token = tie((*small, token))
    b2 = ring(b1)
    b2 = seen(b2)
    a2 = ring(a1)
    a3 = ring(a2)
    a3 = seen(a3)
    b3 = ring(b2)
    b3 = seen(b3)
    xb1 = across(b1)
    xb1 = seen(xb1)
    a4 = ring(a3)
    a4 = seen(a4)
    xa2 = across(a2)
    xa2 = seen(xa2)
    xb2 = ring(xb1)
    xb2 = seen(xb2)
    c3a = ring(xa2)
    c3a = seen(c3a)
    h1 = pair((a1, xa1), (b1, xb1))
    f1 = sibling(h1)
    f1 = seen(f1)
    c3b = ring(xb2)
    c3b = seen(c3b)
    h2 = pair((a2, xa2), (b2, xb2))
    f2 = sibling(h2)
    f2 = seen(f2)
    h3 = pair((a3, c3a), (b3, c3b))
    f3 = sibling(h3)
    f3 = seen(f3)
    c4 = ring(c3a)
    c4 = seen(c4)
    f4 = sibling(a4)
    f4 = seen(f4)
    r1 = products(cat(*tie((h1, f1, h2, f2))))
    r1 = seen(r1)
    e4 = sibling(c4)
    e4 = seen(e4)
    s0 = sibling(val)
    r3 = products(cat(h3, f3, pair((a4, c4), (f4, e4)), val, s0))
    small = [*small, token]

    near, far = c, 1 - c
    ahead, back = 2 * c - 1, 1 - 2 * c
    ids = []
    for step in (1, 2, 3):
        ids += [source(step * ahead, near), source(step * ahead, far), source(step * back, far), source(step * back, near)]
    ids += [source(4, near), source(4, far)]
    ids += [source(0, near), source(0, far)]
    return [r1, r3], jnp.stack(ids), small


def shards(act, grad, val_panels, row_domain, block_tasks, block_live, domain_tokens):
    row_count, width = act.shape
    block_count = block_live.shape[0]
    block_rows = row_count // block_count
    n_dp = lax.axis_size("dp")
    owned = domain_tokens.shape[0]
    cap = 2 * row_count // n_dp
    task_ids = jnp.arange(TASKS, dtype=jnp.int32)

    if n_dp == 16 and lax.axis_size("groups") == 2:
        small = (row_domain, block_tasks, block_live, domain_tokens)
        sums, ids, small = ring_products(act, grad, val_panels, small)
        row_domain, block_tasks, block_live, domain_tokens = small
    else:
        rows = lax.all_gather(val_panels, "dp", axis=1, tiled=True)
        sums, ids = [jnp.sum(scores(act, grad, rows).reshape(TASKS, -1, row_count), axis=1)], task_ids

    paired = jnp.sum((block_tasks[:, None, :] == task_ids[None, :, None]).astype(jnp.float32), axis=2)
    weights = paired * block_live.astype(jnp.float32)[:, None]
    weights = jnp.broadcast_to(weights.T[:, :, None], (TASKS, block_count, block_rows)).reshape(TASKS, row_count)

    owner = row_domain // owned
    local = row_domain % owned
    at_owner = (owner[:, None] == jnp.arange(n_dp, dtype=jnp.int32)[None, :])
    before = jnp.arange(row_count)[:, None] > jnp.arange(row_count)[None, :]
    rank = lax.dot_general(
        before.astype(jnp.bfloat16), at_owner.astype(jnp.bfloat16), (((1,), (0,)), ((), ())),
        preferred_element_type=jnp.float32,
    )
    rank = jnp.sum(jnp.where(at_owner, rank, 0.0), axis=1).astype(jnp.int32)
    place = (owner * HALF + rank)[None, :]
    spare = HALF - cap
    lines = -(-cap // spare)
    home = at_owner[:, :, None] & (rank[:, None, None] == jnp.arange(lines * spare, dtype=jnp.int32))
    marks = jnp.sum(jnp.where(home, (local + 1).astype(jnp.float32)[:, None, None], 0.0), axis=0)
    marks = jnp.pad(marks.reshape(n_dp, lines, spare), ((0, 0), (0, TASKS // 2 - lines), (cap, HALF)))

    packed = pack(sums, ids, weights / width, place, marks)
    theirs = lax.all_to_all(packed, "dp", 0, 0, tiled=True)
    return finish(theirs, domain_tokens, cap)


def solution(mesh):
    return jax.shard_map(
        shards,
        mesh=mesh,
        in_specs=(
            P(("groups", "dp"), None),
            P(("groups", "dp"), None),
            P(None, "dp", None),
            P(("groups", "dp")),
            P(("groups", "dp"), None),
            P(("groups", "dp")),
            P(("groups", "dp")),
        ),
        out_specs=P(None, ("groups", "dp")),
        check_vma=False,
    )
```

```python
import functools

import jax
import jax.numpy as jnp
from jax import lax
from jax.experimental import pallas as pl
from jax.experimental.pallas import tpu as pltpu
from jax.sharding import PartitionSpec as P

TASKS = 16
AXES = ("groups", "dp")
HALF = 64


def load_kernel(act, grad, act_out, grad_out, sems):
    copies = [pltpu.make_async_copy(act, act_out, sems.at[0]), pltpu.make_async_copy(grad, grad_out, sems.at[1])]
    for copy in copies:
        copy.start()
    for copy in copies:
        copy.wait()


def load(act, grad):
    return pl.pallas_call(
        load_kernel,
        out_shape=[pltpu.VMEM(act.shape, act.dtype), pltpu.VMEM(grad.shape, grad.dtype)],
        in_specs=[pl.BlockSpec(memory_space=pl.ANY)] * 2,
        out_specs=[pl.BlockSpec(memory_space=pltpu.VMEM)] * 2,
        scratch_shapes=[pltpu.SemaphoreType.DMA((2,))],
        compiler_params=pltpu.CompilerParams(vmem_limit_bytes=40 * 1024 * 1024),
    )(act, grad)


def three_parts(values):
    top = values.astype(jnp.bfloat16)
    rest = values - top.astype(jnp.float32)
    middle = rest.astype(jnp.bfloat16)
    last = (rest - middle.astype(jnp.float32)).astype(jnp.bfloat16)
    return jnp.concatenate([top, middle, last])


def choose(values, choice):
    m = values.shape[0]
    product = lax.dot_general(
        three_parts(values), choice.astype(jnp.bfloat16), (((1,), (1,)), ((), ())), preferred_element_type=jnp.float32
    )
    return product[:m] + product[m:2 * m] + product[2 * m:]


def pack_kernel(each, arrays, tasks_ref, *refs):
    sums, (weights, place, marks, out, by_task) = refs[:arrays], refs[arrays:]
    position = 0
    for ref in sums:
        for k in range(0, ref.shape[0], each):
            by_task[pl.ds(tasks_ref[position], 1), :] = jnp.sum(ref[k:k + each, :], axis=0, keepdims=True)
            position += 1
    row_task = by_task[...] * weights[...]
    owners, half_tasks, lanes = out.shape
    low = lax.broadcasted_iota(jnp.int32, (half_tasks, lanes), 1) < HALF
    slot = lax.broadcasted_iota(jnp.int32, (2 * lanes, place.shape[1]), 0)
    slot = slot // lanes * HALF + slot % HALF
    for owner in range(0, owners, 2):
        packed = choose(row_task, (place[...] == slot + owner * HALF).astype(jnp.float32))
        for k in range(2):
            part = packed[:, k * lanes:(k + 1) * lanes]
            out[owner + k] = jnp.where(low, part[:half_tasks], part[half_tasks:]) + marks[owner + k]


def pack(sums, tasks, weights, place, marks):
    each = sum(s.shape[0] for s in sums) // tasks.shape[0]
    inside = pl.BlockSpec(memory_space=pltpu.VMEM)
    return pl.pallas_call(
        functools.partial(pack_kernel, each, len(sums)),
        out_shape=jax.ShapeDtypeStruct(marks.shape, jnp.float32),
        in_specs=[pl.BlockSpec(memory_space=pltpu.SMEM)] + [inside] * (len(sums) + 3),
        out_specs=inside,
        scratch_shapes=[pltpu.VMEM(weights.shape, jnp.float32)],
        compiler_params=pltpu.CompilerParams(vmem_limit_bytes=8 * 1024 * 1024),
    )(tasks, *sums, weights, place, marks)


def finish_kernel(cap, theirs, tokens, out):
    senders, half_tasks, lanes = theirs.shape
    owned = out.shape[1]
    spare = HALF - cap
    lane = lax.broadcasted_iota(jnp.int32, (senders, lanes), 1)
    domain = jnp.zeros((senders, lanes), jnp.float32)
    for line in range(-(-cap // spare)):
        first = line * spare
        moved = pltpu.roll(theirs[:, line, :], (first - cap) % lanes, 1)
        domain = jnp.where((lane >= first) & (lane < min(cap, first + spare)), moved, domain)
    domain = domain + pltpu.roll(domain, HALF, 1)
    low = lax.broadcasted_iota(jnp.int32, (half_tasks, lanes), 1) < HALF
    mine = lax.broadcasted_iota(jnp.int32, (owned, lanes), 0).astype(jnp.float32) + 1.0
    total = jnp.zeros((2 * half_tasks, owned), jnp.float32)
    for sender in range(0, senders, 2):
        values, choice = [], []
        for k in (sender, sender + 1):
            tile = theirs[k]
            values.append(jnp.concatenate([jnp.where(low, tile, 0.0), jnp.where(low, 0.0, tile)]))
            choice.append((domain[k:k + 1, :] == mine).astype(jnp.float32))
        total += choose(jnp.concatenate(values, axis=1), jnp.concatenate(choice, axis=1))
    out[...] = total / jnp.sqrt(tokens[...].astype(jnp.float32))


def finish(theirs, tokens, cap):
    inside = pl.BlockSpec(memory_space=pltpu.VMEM)
    return pl.pallas_call(
        functools.partial(finish_kernel, cap),
        out_shape=jax.ShapeDtypeStruct((TASKS, tokens.shape[0]), jnp.float32),
        in_specs=[inside] * 2,
        out_specs=inside,
        compiler_params=pltpu.CompilerParams(vmem_limit_bytes=8 * 1024 * 1024),
    )(theirs, tokens[None, :])


def scores(act, grad, rows):
    dims = (((1,), (1,)), ((), ()))
    left = lax.dot_general(rows[0], act, dims, preferred_element_type=jnp.float32)
    right = lax.dot_general(rows[1], grad, dims, preferred_element_type=jnp.float32)
    return left * right


def ring_products(act, grad, val, small):
    third = val.shape[1] // 3
    row_count = act.shape[0]
    g = lax.axis_index("groups")
    d = lax.axis_index("dp")
    z, y, c = d // 4, (d // 2) % 2, d % 2
    spot = jnp.where(y == 0, z, 7 - z)
    every = [(gg, pp, cc) for gg in range(2) for pp in range(8) for cc in range(2)]

    def flat(gg, pp, cc):
        pp = pp % 8
        zz, yy = (pp, 0) if pp < 4 else (7 - pp, 1)
        return gg * 16 + zz * 4 + yy * 2 + cc

    def ring(x):
        perm = [(flat(gg, pp, cc), flat(gg, pp + 1 - 2 * cc, cc)) for gg, pp, cc in every]
        return lax.ppermute(x, AXES, perm)

    def across(x):
        return lax.ppermute(x, AXES, [(flat(*e), flat(1 - e[0], e[1], e[2])) for e in every])

    def sibling(x):
        return lax.ppermute(x, AXES, [(flat(*e), flat(e[0], e[1], 1 - e[2])) for e in every])

    def source(step, core):
        pp = lax.rem(spot + step + 8, 8)
        zz = jnp.where(pp < 4, pp, 7 - pp)
        yy = jnp.where(pp < 4, 0, 1)
        return zz * 4 + yy * 2 + core

    def products(rows):
        return jnp.sum(scores(act, grad, rows).reshape(-1, val.shape[1] // 3, row_count), axis=1)

    tie = lax.optimization_barrier
    cat = lambda *xs: jnp.concatenate(xs, axis=1)

    *small, token = small

    def seen(x):
        nonlocal token
        x, token = tie((x, token))
        return x

    def cross(x):
        perm = [(flat(gg, pp, cc), flat(gg, pp - 1 + 2 * cc, 1 - cc)) for gg, pp, cc in every]
        return lax.ppermute(x, AXES, perm)

    two = lambda v: cat(v[:, :third], jnp.where(g == 0, v[:, third:2 * third], v[:, 2 * third:]))
    own = two(val)
    act, grad = load(act, grad)
    act = seen(act)
    a1 = ring(own)
    a1 = seen(a1)
    xa1 = across(a1[:, third:])
    xa1 = seen(xa1)
    a2 = ring(a1)
    a2 = seen(a2)
    b1 = cross(own)
    xb1 = across(b1[:, third:])
    xb1 = seen(xb1)
    a3 = ring(a2)
    a3 = seen(a3)
    xa2 = across(a2[:, third:])
    xa2 = seen(xa2)
    s0 = sibling(val)
    h1 = cat(a1, xa1, b1, xb1)
    f1 = sibling(h1)
    r1 = products(cat(val, s0, h1, f1))
    r1 = seen(r1)
    b2 = ring(b1)
    xb2 = across(b2[:, third:])
    xb2 = seen(xb2)
    b3 = ring(b2)
    b3 = seen(b3)
    h2 = cat(a2, xa2, b2, xb2)
    f2 = sibling(h2)
    f2 = seen(f2)
    xa3 = across(a3[:, third:])
    xa3 = seen(xa3)
    r2 = products(cat(h2, f2))
    r2 = seen(r2)
    c3 = ring(xb2)
    h3 = cat(a3, xa3, b3, c3)
    f3 = sibling(h3)
    a4 = ring(a3)
    c4 = ring(xa3)
    f4 = sibling(a4)
    e4 = sibling(c4)
    r3 = products(cat(h3, f3, a4, c4, f4, e4))
    small = [*small, token]

    near, far = c, 1 - c
    ahead, back = 2 * c - 1, 1 - 2 * c
    ids = []
    ids += [source(0, near), source(0, far)]
    for step in (1, 2, 3):
        ids += [source(step * ahead, near), source(step * ahead, far)]
        ids += [source(step * back, far), source(step * back, near)]
    ids += [source(4, near), source(4, far)]
    return [r1, r2, r3], jnp.stack(ids), small


def shards(act, grad, val_panels, row_domain, block_tasks, block_live, domain_tokens):
    row_count, width = act.shape
    block_count = block_live.shape[0]
    block_rows = row_count // block_count
    n_dp = lax.axis_size("dp")
    owned = domain_tokens.shape[0]
    cap = 2 * row_count // n_dp
    task_ids = jnp.arange(TASKS, dtype=jnp.int32)

    if n_dp == 16 and lax.axis_size("groups") == 2:
        small = (row_domain, block_tasks, block_live, domain_tokens)
        sums, ids, small = ring_products(act, grad, val_panels, small)
        row_domain, block_tasks, block_live, domain_tokens = small
    else:
        rows = lax.all_gather(val_panels, "dp", axis=1, tiled=True)
        sums, ids = [jnp.sum(scores(act, grad, rows).reshape(TASKS, -1, row_count), axis=1)], task_ids

    paired = jnp.sum((block_tasks[:, None, :] == task_ids[None, :, None]).astype(jnp.float32), axis=2)
    weights = paired * block_live.astype(jnp.float32)[:, None]
    weights = jnp.broadcast_to(weights.T[:, :, None], (TASKS, block_count, block_rows)).reshape(TASKS, row_count)

    owner = row_domain // owned
    local = row_domain % owned
    at_owner = (owner[:, None] == jnp.arange(n_dp, dtype=jnp.int32)[None, :])
    before = jnp.arange(row_count)[:, None] > jnp.arange(row_count)[None, :]
    rank = lax.dot_general(
        before.astype(jnp.bfloat16), at_owner.astype(jnp.bfloat16), (((1,), (0,)), ((), ())),
        preferred_element_type=jnp.float32,
    )
    rank = jnp.sum(jnp.where(at_owner, rank, 0.0), axis=1).astype(jnp.int32)
    place = (owner * HALF + rank)[None, :]
    spare = HALF - cap
    lines = -(-cap // spare)
    home = at_owner[:, :, None] & (rank[:, None, None] == jnp.arange(lines * spare, dtype=jnp.int32))
    marks = jnp.sum(jnp.where(home, (local + 1).astype(jnp.float32)[:, None, None], 0.0), axis=0)
    marks = jnp.pad(marks.reshape(n_dp, lines, spare), ((0, 0), (0, TASKS // 2 - lines), (cap, HALF)))

    packed = pack(sums, ids, weights / width, place, marks)
    theirs = lax.all_to_all(packed, "dp", 0, 0, tiled=True)
    return finish(theirs, domain_tokens, cap)


def solution(mesh):
    return jax.shard_map(
        shards,
        mesh=mesh,
        in_specs=(
            P(("groups", "dp"), None),
            P(("groups", "dp"), None),
            P(None, "dp", None),
            P(("groups", "dp")),
            P(("groups", "dp"), None),
            P(("groups", "dp")),
            P(("groups", "dp")),
        ),
        out_specs=P(None, ("groups", "dp")),
        check_vma=False,
    )
```

```python
import functools

import jax
import jax.numpy as jnp
from jax import lax
from jax.experimental import pallas as pl
from jax.experimental.pallas import tpu as pltpu
from jax.sharding import PartitionSpec as P

TASKS = 16
AXES = ("groups", "dp")
HALF = 64


def three_parts(values):
    top = values.astype(jnp.bfloat16)
    rest = values - top.astype(jnp.float32)
    middle = rest.astype(jnp.bfloat16)
    last = (rest - middle.astype(jnp.float32)).astype(jnp.bfloat16)
    return jnp.concatenate([top, middle, last])


def choose(values, choice):
    m = values.shape[0]
    product = lax.dot_general(
        three_parts(values), choice.astype(jnp.bfloat16), (((1,), (1,)), ((), ())), preferred_element_type=jnp.float32
    )
    return product[:m] + product[m:2 * m] + product[2 * m:]


def pack_kernel(each, arrays, tasks_ref, *refs):
    sums, (weights, place, marks, out, by_task) = refs[:arrays], refs[arrays:]
    position = 0
    for ref in sums:
        for k in range(0, ref.shape[0], each):
            by_task[pl.ds(tasks_ref[position], 1), :] = jnp.sum(ref[k:k + each, :], axis=0, keepdims=True)
            position += 1
    row_task = by_task[...] * weights[...]
    owners, half_tasks, lanes = out.shape
    low = lax.broadcasted_iota(jnp.int32, (half_tasks, lanes), 1) < HALF
    slot = lax.broadcasted_iota(jnp.int32, (2 * lanes, place.shape[1]), 0)
    slot = slot // lanes * HALF + slot % HALF
    for owner in range(0, owners, 2):
        packed = choose(row_task, (place[...] == slot + owner * HALF).astype(jnp.float32))
        for k in range(2):
            part = packed[:, k * lanes:(k + 1) * lanes]
            out[owner + k] = jnp.where(low, part[:half_tasks], part[half_tasks:]) + marks[owner + k]


def pack(sums, tasks, weights, place, marks):
    each = sum(s.shape[0] for s in sums) // tasks.shape[0]
    inside = pl.BlockSpec(memory_space=pltpu.VMEM)
    return pl.pallas_call(
        functools.partial(pack_kernel, each, len(sums)),
        out_shape=jax.ShapeDtypeStruct(marks.shape, jnp.float32),
        in_specs=[pl.BlockSpec(memory_space=pltpu.SMEM)] + [inside] * (len(sums) + 3),
        out_specs=inside,
        scratch_shapes=[pltpu.VMEM(weights.shape, jnp.float32)],
        compiler_params=pltpu.CompilerParams(vmem_limit_bytes=8 * 1024 * 1024),
    )(tasks, *sums, weights, place, marks)


def finish_kernel(cap, theirs, tokens, out):
    senders, half_tasks, lanes = theirs.shape
    owned = out.shape[1]
    spare = HALF - cap
    lane = lax.broadcasted_iota(jnp.int32, (senders, lanes), 1)
    domain = jnp.zeros((senders, lanes), jnp.float32)
    for line in range(-(-cap // spare)):
        first = line * spare
        moved = pltpu.roll(theirs[:, line, :], (first - cap) % lanes, 1)
        domain = jnp.where((lane >= first) & (lane < min(cap, first + spare)), moved, domain)
    domain = domain + pltpu.roll(domain, HALF, 1)
    low = lax.broadcasted_iota(jnp.int32, (half_tasks, lanes), 1) < HALF
    mine = lax.broadcasted_iota(jnp.int32, (owned, lanes), 0).astype(jnp.float32) + 1.0
    total = jnp.zeros((2 * half_tasks, owned), jnp.float32)
    for sender in range(0, senders, 2):
        values, choice = [], []
        for k in (sender, sender + 1):
            tile = theirs[k]
            values.append(jnp.concatenate([jnp.where(low, tile, 0.0), jnp.where(low, 0.0, tile)]))
            choice.append((domain[k:k + 1, :] == mine).astype(jnp.float32))
        total += choose(jnp.concatenate(values, axis=1), jnp.concatenate(choice, axis=1))
    out[...] = total / jnp.sqrt(tokens[...].astype(jnp.float32))


def finish(theirs, tokens, cap):
    inside = pl.BlockSpec(memory_space=pltpu.VMEM)
    return pl.pallas_call(
        functools.partial(finish_kernel, cap),
        out_shape=jax.ShapeDtypeStruct((TASKS, tokens.shape[0]), jnp.float32),
        in_specs=[inside] * 2,
        out_specs=inside,
        compiler_params=pltpu.CompilerParams(vmem_limit_bytes=8 * 1024 * 1024),
    )(theirs, tokens[None, :])


def scores(act, grad, rows):
    dims = (((1,), (1,)), ((), ()))
    left = lax.dot_general(rows[0], act, dims, preferred_element_type=jnp.float32)
    right = lax.dot_general(rows[1], grad, dims, preferred_element_type=jnp.float32)
    return left * right


def ring_products(act, grad, val, small):
    third = val.shape[1] // 3
    row_count = act.shape[0]
    g = lax.axis_index("groups")
    d = lax.axis_index("dp")
    z, y, c = d // 4, (d // 2) % 2, d % 2
    spot = jnp.where(y == 0, z, 7 - z)
    every = [(gg, pp, cc) for gg in range(2) for pp in range(8) for cc in range(2)]

    def flat(gg, pp, cc):
        pp = pp % 8
        zz, yy = (pp, 0) if pp < 4 else (7 - pp, 1)
        return gg * 16 + zz * 4 + yy * 2 + cc

    def ring(x):
        perm = [(flat(gg, pp, cc), flat(gg, pp + 1 - 2 * cc, cc)) for gg, pp, cc in every]
        return lax.ppermute(x, AXES, perm)

    def across(x):
        return lax.ppermute(x, AXES, [(flat(*e), flat(1 - e[0], e[1], e[2])) for e in every])

    def sibling(x):
        return lax.ppermute(x, AXES, [(flat(*e), flat(e[0], e[1], 1 - e[2])) for e in every])

    def source(step, core):
        pp = lax.rem(spot + step + 8, 8)
        zz = jnp.where(pp < 4, pp, 7 - pp)
        yy = jnp.where(pp < 4, 0, 1)
        return zz * 4 + yy * 2 + core

    def products(rows):
        return jnp.sum(scores(act, grad, rows).reshape(-1, val.shape[1] // 3, row_count), axis=1)

    tie = lax.optimization_barrier
    cat = lambda *xs: jnp.concatenate(xs, axis=1)

    *small, token = small

    def seen(x):
        nonlocal token
        x, token = tie((x, token))
        return x

    def cross(x):
        perm = [(flat(gg, pp, cc), flat(gg, pp - 1 + 2 * cc, 1 - cc)) for gg, pp, cc in every]
        return lax.ppermute(x, AXES, perm)

    two = lambda v: cat(v[:, :third], jnp.where(g == 0, v[:, third:2 * third], v[:, 2 * third:]))
    own = two(val)
    a1 = ring(own)
    a1 = seen(a1)
    xa1 = across(a1[:, third:])
    xa1 = seen(xa1)
    a2 = ring(a1)
    a2 = seen(a2)
    b1 = cross(own)
    xb1 = across(b1[:, third:])
    xb1 = seen(xb1)
    a3 = ring(a2)
    a3 = seen(a3)
    xa2 = across(a2[:, third:])
    xa2 = seen(xa2)
    s0 = sibling(val)
    s0 = seen(s0)
    h1 = cat(a1, xa1, b1, xb1)
    f1 = sibling(h1)
    r1 = products(cat(*tie((val, s0, h1, f1))))
    r1 = seen(r1)
    b2 = ring(b1)
    xb2 = across(b2[:, third:])
    xb2 = seen(xb2)
    h2 = cat(a2, xa2, b2, xb2)
    f2 = sibling(h2)
    f2 = seen(f2)
    b3 = ring(b2)
    b3 = seen(b3)
    a4 = ring(a3)
    a4 = seen(a4)
    xa3 = across(a3[:, third:])
    xa3 = seen(xa3)
    r2 = products(cat(h2, f2))
    r2 = seen(r2)
    c3 = ring(xb2)
    h3 = cat(a3, xa3, b3, c3)
    f3 = sibling(h3)
    c4 = ring(xa3)
    f4 = sibling(a4)
    e4 = sibling(c4)
    r3 = products(cat(h3, f3, a4, c4, f4, e4))
    small = [*small, token]

    near, far = c, 1 - c
    ahead, back = 2 * c - 1, 1 - 2 * c
    ids = []
    ids += [source(0, near), source(0, far)]
    for step in (1, 2, 3):
        ids += [source(step * ahead, near), source(step * ahead, far)]
        ids += [source(step * back, far), source(step * back, near)]
    ids += [source(4, near), source(4, far)]
    return [r1, r2, r3], jnp.stack(ids), small


def shards(act, grad, val_panels, row_domain, block_tasks, block_live, domain_tokens):
    row_count, width = act.shape
    block_count = block_live.shape[0]
    block_rows = row_count // block_count
    n_dp = lax.axis_size("dp")
    owned = domain_tokens.shape[0]
    cap = 2 * row_count // n_dp
    task_ids = jnp.arange(TASKS, dtype=jnp.int32)

    if n_dp == 16 and lax.axis_size("groups") == 2:
        small = (row_domain, block_tasks, block_live, domain_tokens)
        sums, ids, small = ring_products(act, grad, val_panels, small)
        row_domain, block_tasks, block_live, domain_tokens = small
    else:
        rows = lax.all_gather(val_panels, "dp", axis=1, tiled=True)
        sums, ids = [jnp.sum(scores(act, grad, rows).reshape(TASKS, -1, row_count), axis=1)], task_ids

    paired = jnp.sum((block_tasks[:, None, :] == task_ids[None, :, None]).astype(jnp.float32), axis=2)
    weights = paired * block_live.astype(jnp.float32)[:, None]
    weights = jnp.broadcast_to(weights.T[:, :, None], (TASKS, block_count, block_rows)).reshape(TASKS, row_count)

    owner = row_domain // owned
    local = row_domain % owned
    at_owner = (owner[:, None] == jnp.arange(n_dp, dtype=jnp.int32)[None, :])
    before = jnp.arange(row_count)[:, None] > jnp.arange(row_count)[None, :]
    rank = lax.dot_general(
        before.astype(jnp.bfloat16), at_owner.astype(jnp.bfloat16), (((1,), (0,)), ((), ())),
        preferred_element_type=jnp.float32,
    )
    rank = jnp.sum(jnp.where(at_owner, rank, 0.0), axis=1).astype(jnp.int32)
    place = (owner * HALF + rank)[None, :]
    spare = HALF - cap
    lines = -(-cap // spare)
    home = at_owner[:, :, None] & (rank[:, None, None] == jnp.arange(lines * spare, dtype=jnp.int32))
    marks = jnp.sum(jnp.where(home, (local + 1).astype(jnp.float32)[:, None, None], 0.0), axis=0)
    marks = jnp.pad(marks.reshape(n_dp, lines, spare), ((0, 0), (0, TASKS // 2 - lines), (cap, HALF)))

    packed = pack(sums, ids, weights / width, place, marks)
    theirs = lax.all_to_all(packed, "dp", 0, 0, tiled=True)
    return finish(theirs, domain_tokens, cap)


def solution(mesh):
    return jax.shard_map(
        shards,
        mesh=mesh,
        in_specs=(
            P(("groups", "dp"), None),
            P(("groups", "dp"), None),
            P(None, "dp", None),
            P(("groups", "dp")),
            P(("groups", "dp"), None),
            P(("groups", "dp")),
            P(("groups", "dp")),
        ),
        out_specs=P(None, ("groups", "dp")),
        check_vma=False,
    )
```

```python
import functools

import jax
import jax.numpy as jnp
from jax import lax
from jax.experimental import pallas as pl
from jax.experimental.pallas import tpu as pltpu
from jax.sharding import PartitionSpec as P

TASKS = 16
AXES = ("groups", "dp")
HALF = 64


def three_parts(values):
    top = values.astype(jnp.bfloat16)
    rest = values - top.astype(jnp.float32)
    middle = rest.astype(jnp.bfloat16)
    last = (rest - middle.astype(jnp.float32)).astype(jnp.bfloat16)
    return jnp.concatenate([top, middle, last])


def choose(values, choice):
    m = values.shape[0]
    product = lax.dot_general(
        three_parts(values), choice.astype(jnp.bfloat16), (((1,), (1,)), ((), ())), preferred_element_type=jnp.float32
    )
    return product[:m] + product[m:2 * m] + product[2 * m:]


def pack_kernel(each, arrays, tasks_ref, *refs):
    sums, (weights, place, marks, out, by_task) = refs[:arrays], refs[arrays:]
    position = 0
    for ref in sums:
        for k in range(0, ref.shape[0], each):
            by_task[pl.ds(tasks_ref[position], 1), :] = jnp.sum(ref[k:k + each, :], axis=0, keepdims=True)
            position += 1
    row_task = by_task[...] * weights[...]
    owners, half_tasks, lanes = out.shape
    low = lax.broadcasted_iota(jnp.int32, (half_tasks, lanes), 1) < HALF
    slot = lax.broadcasted_iota(jnp.int32, (2 * lanes, place.shape[1]), 0)
    slot = slot // lanes * HALF + slot % HALF
    for owner in range(0, owners, 2):
        packed = choose(row_task, (place[...] == slot + owner * HALF).astype(jnp.float32))
        for k in range(2):
            part = packed[:, k * lanes:(k + 1) * lanes]
            out[owner + k] = jnp.where(low, part[:half_tasks], part[half_tasks:]) + marks[owner + k]


def pack(sums, tasks, weights, place, marks):
    each = sum(s.shape[0] for s in sums) // tasks.shape[0]
    inside = pl.BlockSpec(memory_space=pltpu.VMEM)
    return pl.pallas_call(
        functools.partial(pack_kernel, each, len(sums)),
        out_shape=jax.ShapeDtypeStruct(marks.shape, jnp.float32),
        in_specs=[pl.BlockSpec(memory_space=pltpu.SMEM)] + [inside] * (len(sums) + 3),
        out_specs=inside,
        scratch_shapes=[pltpu.VMEM(weights.shape, jnp.float32)],
        compiler_params=pltpu.CompilerParams(vmem_limit_bytes=8 * 1024 * 1024),
    )(tasks, *sums, weights, place, marks)


def finish_kernel(cap, theirs, tokens, out):
    senders, half_tasks, lanes = theirs.shape
    owned = out.shape[1]
    spare = HALF - cap
    lane = lax.broadcasted_iota(jnp.int32, (senders, lanes), 1)
    domain = jnp.zeros((senders, lanes), jnp.float32)
    for line in range(-(-cap // spare)):
        first = line * spare
        moved = pltpu.roll(theirs[:, line, :], (first - cap) % lanes, 1)
        domain = jnp.where((lane >= first) & (lane < min(cap, first + spare)), moved, domain)
    domain = domain + pltpu.roll(domain, HALF, 1)
    low = lax.broadcasted_iota(jnp.int32, (half_tasks, lanes), 1) < HALF
    mine = lax.broadcasted_iota(jnp.int32, (owned, lanes), 0).astype(jnp.float32) + 1.0
    total = jnp.zeros((2 * half_tasks, owned), jnp.float32)
    for sender in range(0, senders, 2):
        values, choice = [], []
        for k in (sender, sender + 1):
            tile = theirs[k]
            values.append(jnp.concatenate([jnp.where(low, tile, 0.0), jnp.where(low, 0.0, tile)]))
            choice.append((domain[k:k + 1, :] == mine).astype(jnp.float32))
        total += choose(jnp.concatenate(values, axis=1), jnp.concatenate(choice, axis=1))
    out[...] = total / jnp.sqrt(tokens[...].astype(jnp.float32))


def finish(theirs, tokens, cap):
    inside = pl.BlockSpec(memory_space=pltpu.VMEM)
    return pl.pallas_call(
        functools.partial(finish_kernel, cap),
        out_shape=jax.ShapeDtypeStruct((TASKS, tokens.shape[0]), jnp.float32),
        in_specs=[inside] * 2,
        out_specs=inside,
        compiler_params=pltpu.CompilerParams(vmem_limit_bytes=8 * 1024 * 1024),
    )(theirs, tokens[None, :])


def scores(act, grad, rows):
    return row_products(rows[0], act) * row_products(rows[1], grad)


def row_products(left, right):
    return lax.dot_general(left, right, (((1,), (1,)), ((), ())), preferred_element_type=jnp.float32)


def ring_products(act, grad, val, small):
    third = val.shape[1] // 3
    row_count = act.shape[0]
    g = lax.axis_index("groups")
    d = lax.axis_index("dp")
    z, y, c = d // 4, (d // 2) % 2, d % 2
    spot = jnp.where(y == 0, z, 7 - z)
    every = [(gg, pp, cc) for gg in range(2) for pp in range(8) for cc in range(2)]

    def flat(gg, pp, cc):
        pp = pp % 8
        zz, yy = (pp, 0) if pp < 4 else (7 - pp, 1)
        return gg * 16 + zz * 4 + yy * 2 + cc

    def ring(x):
        perm = [(flat(gg, pp, cc), flat(gg, pp + 1 - 2 * cc, cc)) for gg, pp, cc in every]
        return lax.ppermute(x, AXES, perm)

    def across(x):
        return lax.ppermute(x, AXES, [(flat(*e), flat(1 - e[0], e[1], e[2])) for e in every])

    def sibling(x):
        return lax.ppermute(x, AXES, [(flat(*e), flat(e[0], e[1], 1 - e[2])) for e in every])

    def source(step, core):
        pp = lax.rem(spot + step + 8, 8)
        zz = jnp.where(pp < 4, pp, 7 - pp)
        yy = jnp.where(pp < 4, 0, 1)
        return zz * 4 + yy * 2 + core

    def products(left, rows):
        return jnp.sum((left * row_products(rows[1], grad)).reshape(-1, third, row_count), axis=1)

    def left_dots(rows):
        return row_products(rows[0], act)

    tie = lax.optimization_barrier
    cat = lambda *xs: jnp.concatenate(xs, axis=1)

    *small, token = small

    def seen(x):
        nonlocal token
        x, token = tie((x, token))
        return x

    def cross(x):
        perm = [(flat(gg, pp, cc), flat(gg, pp - 1 + 2 * cc, 1 - cc)) for gg, pp, cc in every]
        return lax.ppermute(x, AXES, perm)

    two = lambda v: cat(v[:, :third], jnp.where(g == 0, v[:, third:2 * third], v[:, 2 * third:]))
    own = two(val)
    a1 = ring(own)
    a1 = seen(a1)
    xa1 = across(a1[:, third:])
    xa1 = seen(xa1)
    a2 = ring(a1)
    a2 = seen(a2)
    b1 = cross(own)
    xb1 = across(b1[:, third:])
    xb1 = seen(xb1)
    a3 = ring(a2)
    a3 = seen(a3)
    xa2 = across(a2[:, third:])
    xa2 = seen(xa2)
    s0 = sibling(val)
    s0 = seen(s0)
    h1 = cat(a1, xa1, b1, xb1)
    f1 = sibling(h1)
    q1 = cat(*tie((val, s0, h1, f1)))
    r1l = left_dots(q1)
    r1 = products(r1l, q1)
    r1 = seen(r1)
    b2 = ring(b1)
    xb2 = across(b2[:, third:])
    xb2 = seen(xb2)
    h2 = cat(a2, xa2, b2, xb2)
    f2 = sibling(h2)
    f2 = seen(f2)
    b3 = ring(b2)
    b3 = seen(b3)
    a4 = ring(a3)
    a4 = seen(a4)
    xa3 = across(a3[:, third:])
    xa3 = seen(xa3)
    q2 = cat(h2, f2)
    r2l = left_dots(q2)
    r2l = seen(r2l)
    c3 = ring(xb2)
    c3 = seen(c3)
    h3 = cat(a3, xa3, b3)
    f3 = sibling(h3)
    f3 = seen(f3)
    f4 = sibling(a4)
    f4 = seen(f4)
    c4 = ring(xa3)
    c4 = seen(c4)
    r2 = products(*tie((r2l, q2, token))[:2])
    r2 = seen(r2)
    g3 = sibling(c3)
    e4 = sibling(c4)
    q3 = cat(h3, c3, f3, g3, a4, c4, f4, e4)
    r3 = products(left_dots(q3), q3)
    small = [*small, token]

    near, far = c, 1 - c
    ahead, back = 2 * c - 1, 1 - 2 * c
    ids = []
    ids += [source(0, near), source(0, far)]
    for step in (1, 2, 3):
        ids += [source(step * ahead, near), source(step * ahead, far)]
        ids += [source(step * back, far), source(step * back, near)]
    ids += [source(4, near), source(4, far)]
    return [r1, r2, r3], jnp.stack(ids), small


def shards(act, grad, val_panels, row_domain, block_tasks, block_live, domain_tokens):
    row_count, width = act.shape
    block_count = block_live.shape[0]
    block_rows = row_count // block_count
    n_dp = lax.axis_size("dp")
    owned = domain_tokens.shape[0]
    cap = 2 * row_count // n_dp
    task_ids = jnp.arange(TASKS, dtype=jnp.int32)

    if n_dp == 16 and lax.axis_size("groups") == 2:
        small = (row_domain, block_tasks, block_live, domain_tokens)
        sums, ids, small = ring_products(act, grad, val_panels, small)
        row_domain, block_tasks, block_live, domain_tokens = small
    else:
        rows = lax.all_gather(val_panels, "dp", axis=1, tiled=True)
        sums, ids = [jnp.sum(scores(act, grad, rows).reshape(TASKS, -1, row_count), axis=1)], task_ids

    paired = jnp.sum((block_tasks[:, None, :] == task_ids[None, :, None]).astype(jnp.float32), axis=2)
    weights = paired * block_live.astype(jnp.float32)[:, None]
    weights = jnp.broadcast_to(weights.T[:, :, None], (TASKS, block_count, block_rows)).reshape(TASKS, row_count)

    owner = row_domain // owned
    local = row_domain % owned
    at_owner = (owner[:, None] == jnp.arange(n_dp, dtype=jnp.int32)[None, :])
    before = jnp.arange(row_count)[:, None] > jnp.arange(row_count)[None, :]
    rank = lax.dot_general(
        before.astype(jnp.bfloat16), at_owner.astype(jnp.bfloat16), (((1,), (0,)), ((), ())),
        preferred_element_type=jnp.float32,
    )
    rank = jnp.sum(jnp.where(at_owner, rank, 0.0), axis=1).astype(jnp.int32)
    place = (owner * HALF + rank)[None, :]
    spare = HALF - cap
    lines = -(-cap // spare)
    home = at_owner[:, :, None] & (rank[:, None, None] == jnp.arange(lines * spare, dtype=jnp.int32))
    marks = jnp.sum(jnp.where(home, (local + 1).astype(jnp.float32)[:, None, None], 0.0), axis=0)
    marks = jnp.pad(marks.reshape(n_dp, lines, spare), ((0, 0), (0, TASKS // 2 - lines), (cap, HALF)))

    packed = pack(sums, ids, weights / width, place, marks)
    theirs = lax.all_to_all(packed, "dp", 0, 0, tiled=True)
    return finish(theirs, domain_tokens, cap)


def solution(mesh):
    return jax.shard_map(
        shards,
        mesh=mesh,
        in_specs=(
            P(("groups", "dp"), None),
            P(("groups", "dp"), None),
            P(None, "dp", None),
            P(("groups", "dp")),
            P(("groups", "dp"), None),
            P(("groups", "dp")),
            P(("groups", "dp")),
        ),
        out_specs=P(None, ("groups", "dp")),
        check_vma=False,
    )
```

```python
import functools

import jax
import jax.numpy as jnp
from jax import lax
from jax.experimental import pallas as pl
from jax.experimental.pallas import tpu as pltpu
from jax.sharding import PartitionSpec as P

TASKS = 16
AXES = ("groups", "dp")
HALF = 64


def three_parts(values):
    top = values.astype(jnp.bfloat16)
    rest = values - top.astype(jnp.float32)
    middle = rest.astype(jnp.bfloat16)
    last = (rest - middle.astype(jnp.float32)).astype(jnp.bfloat16)
    return jnp.concatenate([top, middle, last])


def choose(values, choice):
    m = values.shape[0]
    product = lax.dot_general(
        three_parts(values), choice.astype(jnp.bfloat16), (((1,), (1,)), ((), ())), preferred_element_type=jnp.float32
    )
    return product[:m] + product[m:2 * m] + product[2 * m:]


def pack_kernel(each, arrays, tasks_ref, *refs):
    sums, (weights, place, marks, out, by_task) = refs[:arrays], refs[arrays:]
    position = 0
    for ref in sums:
        for k in range(0, ref.shape[0], each):
            by_task[pl.ds(tasks_ref[position], 1), :] = jnp.sum(ref[k:k + each, :], axis=0, keepdims=True)
            position += 1
    row_task = by_task[...] * weights[...]
    owners, half_tasks, lanes = out.shape
    low = lax.broadcasted_iota(jnp.int32, (half_tasks, lanes), 1) < HALF
    slot = lax.broadcasted_iota(jnp.int32, (2 * lanes, place.shape[1]), 0)
    slot = slot // lanes * HALF + slot % HALF
    for owner in range(0, owners, 2):
        packed = choose(row_task, (place[...] == slot + owner * HALF).astype(jnp.float32))
        for k in range(2):
            part = packed[:, k * lanes:(k + 1) * lanes]
            out[owner + k] = jnp.where(low, part[:half_tasks], part[half_tasks:]) + marks[owner + k]


def pack(sums, tasks, weights, place, marks):
    each = sum(s.shape[0] for s in sums) // tasks.shape[0]
    inside = pl.BlockSpec(memory_space=pltpu.VMEM)
    return pl.pallas_call(
        functools.partial(pack_kernel, each, len(sums)),
        out_shape=jax.ShapeDtypeStruct(marks.shape, jnp.float32),
        in_specs=[pl.BlockSpec(memory_space=pltpu.SMEM)] + [inside] * (len(sums) + 3),
        out_specs=inside,
        scratch_shapes=[pltpu.VMEM(weights.shape, jnp.float32)],
        compiler_params=pltpu.CompilerParams(vmem_limit_bytes=8 * 1024 * 1024),
    )(tasks, *sums, weights, place, marks)


def finish_kernel(cap, theirs, tokens, out):
    senders, half_tasks, lanes = theirs.shape
    owned = out.shape[1]
    spare = HALF - cap
    lane = lax.broadcasted_iota(jnp.int32, (senders, lanes), 1)
    domain = jnp.zeros((senders, lanes), jnp.float32)
    for line in range(-(-cap // spare)):
        first = line * spare
        moved = pltpu.roll(theirs[:, line, :], (first - cap) % lanes, 1)
        domain = jnp.where((lane >= first) & (lane < min(cap, first + spare)), moved, domain)
    domain = domain + pltpu.roll(domain, HALF, 1)
    low = lax.broadcasted_iota(jnp.int32, (half_tasks, lanes), 1) < HALF
    mine = lax.broadcasted_iota(jnp.int32, (owned, lanes), 0).astype(jnp.float32) + 1.0
    total = jnp.zeros((2 * half_tasks, owned), jnp.float32)
    for sender in range(0, senders, 2):
        values, choice = [], []
        for k in (sender, sender + 1):
            tile = theirs[k]
            values.append(jnp.concatenate([jnp.where(low, tile, 0.0), jnp.where(low, 0.0, tile)]))
            choice.append((domain[k:k + 1, :] == mine).astype(jnp.float32))
        total += choose(jnp.concatenate(values, axis=1), jnp.concatenate(choice, axis=1))
    out[...] = total / jnp.sqrt(tokens[...].astype(jnp.float32))


def finish(theirs, tokens, cap):
    inside = pl.BlockSpec(memory_space=pltpu.VMEM)
    return pl.pallas_call(
        functools.partial(finish_kernel, cap),
        out_shape=jax.ShapeDtypeStruct((TASKS, tokens.shape[0]), jnp.float32),
        in_specs=[inside] * 2,
        out_specs=inside,
        compiler_params=pltpu.CompilerParams(vmem_limit_bytes=8 * 1024 * 1024),
    )(theirs, tokens[None, :])


def scores(act, grad, rows):
    return row_products(rows[0], act) * row_products(rows[1], grad)


def row_products(left, right):
    return lax.dot_general(left, right, (((1,), (1,)), ((), ())), preferred_element_type=jnp.float32)


def ring_products(act, grad, val, small):
    third = val.shape[1] // 3
    row_count = act.shape[0]
    g = lax.axis_index("groups")
    d = lax.axis_index("dp")
    z, y, c = d // 4, (d // 2) % 2, d % 2
    spot = jnp.where(y == 0, z, 7 - z)
    every = [(gg, pp, cc) for gg in range(2) for pp in range(8) for cc in range(2)]

    def flat(gg, pp, cc):
        pp = pp % 8
        zz, yy = (pp, 0) if pp < 4 else (7 - pp, 1)
        return gg * 16 + zz * 4 + yy * 2 + cc

    def ring(x):
        perm = [(flat(gg, pp, cc), flat(gg, pp + 1 - 2 * cc, cc)) for gg, pp, cc in every]
        return lax.ppermute(x, AXES, perm)

    def across(x):
        return lax.ppermute(x, AXES, [(flat(*e), flat(1 - e[0], e[1], e[2])) for e in every])

    def sibling(x):
        return lax.ppermute(x, AXES, [(flat(*e), flat(e[0], e[1], 1 - e[2])) for e in every])

    def source(step, core):
        pp = lax.rem(spot + step + 8, 8)
        zz = jnp.where(pp < 4, pp, 7 - pp)
        yy = jnp.where(pp < 4, 0, 1)
        return zz * 4 + yy * 2 + core

    def products(left, rows):
        return jnp.sum((left * row_products(rows[1], grad)).reshape(-1, third, row_count), axis=1)

    def left_dots(rows):
        return row_products(rows[0], act)

    tie = lax.optimization_barrier
    cat = lambda *xs: jnp.concatenate(xs, axis=1)

    *small, token = small

    def seen(x):
        nonlocal token
        x, token = tie((x, token))
        return x

    def cross(x):
        perm = [(flat(gg, pp, cc), flat(gg, pp - 1 + 2 * cc, 1 - cc)) for gg, pp, cc in every]
        return lax.ppermute(x, AXES, perm)

    two = lambda v: cat(v[:, :third], jnp.where(g == 0, v[:, third:2 * third], v[:, 2 * third:]))
    own = two(val)
    a1 = ring(own)
    a1 = seen(a1)
    xa1 = across(a1[:, third:])
    xa1 = seen(xa1)
    a2 = ring(a1)
    a2 = seen(a2)
    b1 = cross(own)
    xb1 = across(b1[:, third:])
    xb1 = seen(xb1)
    a3 = ring(a2)
    a3 = seen(a3)
    xa2 = across(a2[:, third:])
    xa2 = seen(xa2)
    s0 = sibling(val)
    s0 = seen(s0)
    h1 = cat(a1, xa1, b1, xb1)
    f1 = sibling(h1)
    q1 = cat(*tie((val, s0, h1, f1)))
    r1l = left_dots(q1)
    r1 = products(r1l, q1)
    r1 = seen(r1)
    b2 = ring(b1)
    xb2 = across(b2[:, third:])
    xb2 = seen(xb2)
    xa3 = across(a3[:, third:])
    xa3 = seen(xa3)
    h2 = cat(a2, xa2, b2, xb2)
    f2 = sibling(h2)
    f2 = seen(f2)
    b3 = ring(b2)
    b3 = seen(b3)
    a4 = ring(a3)
    a4 = seen(a4)
    q2 = cat(h2, f2)
    r2l = left_dots(q2)
    r2l = seen(r2l)
    c3 = ring(xb2)
    c3 = seen(c3)
    h3 = cat(a3, xa3, b3)
    f3 = sibling(h3)
    f3 = seen(f3)
    f4 = sibling(a4)
    f4 = seen(f4)
    c4 = ring(xa3)
    c4 = seen(c4)
    r2 = products(*tie((r2l, q2, token))[:2])
    r2 = seen(r2)
    g3 = sibling(c3)
    e4 = sibling(c4)
    q3 = cat(h3, c3, f3, g3, a4, c4, f4, e4)
    r3 = products(left_dots(q3), q3)
    small = [*small, token]

    near, far = c, 1 - c
    ahead, back = 2 * c - 1, 1 - 2 * c
    ids = []
    ids += [source(0, near), source(0, far)]
    for step in (1, 2, 3):
        ids += [source(step * ahead, near), source(step * ahead, far)]
        ids += [source(step * back, far), source(step * back, near)]
    ids += [source(4, near), source(4, far)]
    return [r1, r2, r3], jnp.stack(ids), small


def shards(act, grad, val_panels, row_domain, block_tasks, block_live, domain_tokens):
    row_count, width = act.shape
    block_count = block_live.shape[0]
    block_rows = row_count // block_count
    n_dp = lax.axis_size("dp")
    owned = domain_tokens.shape[0]
    cap = 2 * row_count // n_dp
    task_ids = jnp.arange(TASKS, dtype=jnp.int32)

    if n_dp == 16 and lax.axis_size("groups") == 2:
        small = (row_domain, block_tasks, block_live, domain_tokens)
        sums, ids, small = ring_products(act, grad, val_panels, small)
        row_domain, block_tasks, block_live, domain_tokens = small
    else:
        rows = lax.all_gather(val_panels, "dp", axis=1, tiled=True)
        sums, ids = [jnp.sum(scores(act, grad, rows).reshape(TASKS, -1, row_count), axis=1)], task_ids

    paired = jnp.sum((block_tasks[:, None, :] == task_ids[None, :, None]).astype(jnp.float32), axis=2)
    weights = paired * block_live.astype(jnp.float32)[:, None]
    weights = jnp.broadcast_to(weights.T[:, :, None], (TASKS, block_count, block_rows)).reshape(TASKS, row_count)

    owner = row_domain // owned
    local = row_domain % owned
    at_owner = (owner[:, None] == jnp.arange(n_dp, dtype=jnp.int32)[None, :])
    before = jnp.arange(row_count)[:, None] > jnp.arange(row_count)[None, :]
    rank = lax.dot_general(
        before.astype(jnp.bfloat16), at_owner.astype(jnp.bfloat16), (((1,), (0,)), ((), ())),
        preferred_element_type=jnp.float32,
    )
    rank = jnp.sum(jnp.where(at_owner, rank, 0.0), axis=1).astype(jnp.int32)
    place = (owner * HALF + rank)[None, :]
    spare = HALF - cap
    lines = -(-cap // spare)
    home = at_owner[:, :, None] & (rank[:, None, None] == jnp.arange(lines * spare, dtype=jnp.int32))
    marks = jnp.sum(jnp.where(home, (local + 1).astype(jnp.float32)[:, None, None], 0.0), axis=0)
    marks = jnp.pad(marks.reshape(n_dp, lines, spare), ((0, 0), (0, TASKS // 2 - lines), (cap, HALF)))

    packed = pack(sums, ids, weights / width, place, marks)
    theirs = lax.all_to_all(packed, "dp", 0, 0, tiled=True)
    return finish(theirs, domain_tokens, cap)


def solution(mesh):
    return jax.shard_map(
        shards,
        mesh=mesh,
        in_specs=(
            P(("groups", "dp"), None),
            P(("groups", "dp"), None),
            P(None, "dp", None),
            P(("groups", "dp")),
            P(("groups", "dp"), None),
            P(("groups", "dp")),
            P(("groups", "dp")),
        ),
        out_specs=P(None, ("groups", "dp")),
        check_vma=False,
    )
```

```python
import functools

import jax
import jax.numpy as jnp
from jax import lax
from jax.experimental import pallas as pl
from jax.experimental.pallas import tpu as pltpu
from jax.sharding import PartitionSpec as P

TASKS = 16
AXES = ("groups", "dp")
HALF = 64


def three_parts(values):
    top = values.astype(jnp.bfloat16)
    rest = values - top.astype(jnp.float32)
    middle = rest.astype(jnp.bfloat16)
    last = (rest - middle.astype(jnp.float32)).astype(jnp.bfloat16)
    return jnp.concatenate([top, middle, last])


def choose(values, choice):
    m = values.shape[0]
    product = lax.dot_general(
        three_parts(values), choice.astype(jnp.bfloat16), (((1,), (1,)), ((), ())), preferred_element_type=jnp.float32
    )
    return product[:m] + product[m:2 * m] + product[2 * m:]


def pack_kernel(each, arrays, tasks_ref, *refs):
    sums, (weights, place, marks, out, by_task) = refs[:arrays], refs[arrays:]
    position = 0
    for ref in sums:
        for k in range(0, ref.shape[0], each):
            by_task[pl.ds(tasks_ref[position], 1), :] = jnp.sum(ref[k:k + each, :], axis=0, keepdims=True)
            position += 1
    row_task = by_task[...] * weights[...]
    owners, half_tasks, lanes = out.shape
    low = lax.broadcasted_iota(jnp.int32, (half_tasks, lanes), 1) < HALF
    slot = lax.broadcasted_iota(jnp.int32, (2 * lanes, place.shape[1]), 0)
    slot = slot // lanes * HALF + slot % HALF
    for owner in range(0, owners, 2):
        packed = choose(row_task, (place[...] == slot + owner * HALF).astype(jnp.float32))
        for k in range(2):
            part = packed[:, k * lanes:(k + 1) * lanes]
            out[owner + k] = jnp.where(low, part[:half_tasks], part[half_tasks:]) + marks[owner + k]


def pack(sums, tasks, weights, place, marks):
    each = sum(s.shape[0] for s in sums) // tasks.shape[0]
    inside = pl.BlockSpec(memory_space=pltpu.VMEM)
    return pl.pallas_call(
        functools.partial(pack_kernel, each, len(sums)),
        out_shape=jax.ShapeDtypeStruct(marks.shape, jnp.float32),
        in_specs=[pl.BlockSpec(memory_space=pltpu.SMEM)] + [inside] * (len(sums) + 3),
        out_specs=inside,
        scratch_shapes=[pltpu.VMEM(weights.shape, jnp.float32)],
        compiler_params=pltpu.CompilerParams(vmem_limit_bytes=8 * 1024 * 1024),
    )(tasks, *sums, weights, place, marks)


def finish_kernel(cap, theirs, tokens, out):
    senders, half_tasks, lanes = theirs.shape
    owned = out.shape[1]
    spare = HALF - cap
    lane = lax.broadcasted_iota(jnp.int32, (senders, lanes), 1)
    domain = jnp.zeros((senders, lanes), jnp.float32)
    for line in range(-(-cap // spare)):
        first = line * spare
        moved = pltpu.roll(theirs[:, line, :], (first - cap) % lanes, 1)
        domain = jnp.where((lane >= first) & (lane < min(cap, first + spare)), moved, domain)
    domain = domain + pltpu.roll(domain, HALF, 1)
    low = lax.broadcasted_iota(jnp.int32, (half_tasks, lanes), 1) < HALF
    mine = lax.broadcasted_iota(jnp.int32, (owned, lanes), 0).astype(jnp.float32) + 1.0
    total = jnp.zeros((2 * half_tasks, owned), jnp.float32)
    for sender in range(0, senders, 2):
        values, choice = [], []
        for k in (sender, sender + 1):
            tile = theirs[k]
            values.append(jnp.concatenate([jnp.where(low, tile, 0.0), jnp.where(low, 0.0, tile)]))
            choice.append((domain[k:k + 1, :] == mine).astype(jnp.float32))
        total += choose(jnp.concatenate(values, axis=1), jnp.concatenate(choice, axis=1))
    out[...] = total / jnp.sqrt(tokens[...].astype(jnp.float32))


def finish(theirs, tokens, cap):
    inside = pl.BlockSpec(memory_space=pltpu.VMEM)
    return pl.pallas_call(
        functools.partial(finish_kernel, cap),
        out_shape=jax.ShapeDtypeStruct((TASKS, tokens.shape[0]), jnp.float32),
        in_specs=[inside] * 2,
        out_specs=inside,
        compiler_params=pltpu.CompilerParams(vmem_limit_bytes=8 * 1024 * 1024),
    )(theirs, tokens[None, :])


def scores(act, grad, rows):
    return row_products(rows[0], act) * row_products(rows[1], grad)


def row_products(left, right):
    return lax.dot_general(left, right, (((1,), (1,)), ((), ())), preferred_element_type=jnp.float32)


def ring_products(act, grad, val, small):
    third = val.shape[1] // 3
    row_count = act.shape[0]
    g = lax.axis_index("groups")
    d = lax.axis_index("dp")
    z, y, c = d // 4, (d // 2) % 2, d % 2
    spot = jnp.where(y == 0, z, 7 - z)
    every = [(gg, pp, cc) for gg in range(2) for pp in range(8) for cc in range(2)]

    def flat(gg, pp, cc):
        pp = pp % 8
        zz, yy = (pp, 0) if pp < 4 else (7 - pp, 1)
        return gg * 16 + zz * 4 + yy * 2 + cc

    def ring(x):
        perm = [(flat(gg, pp, cc), flat(gg, pp + 1 - 2 * cc, cc)) for gg, pp, cc in every]
        return lax.ppermute(x, AXES, perm)

    def across(x):
        return lax.ppermute(x, AXES, [(flat(*e), flat(1 - e[0], e[1], e[2])) for e in every])

    def sibling(x):
        return lax.ppermute(x, AXES, [(flat(*e), flat(e[0], e[1], 1 - e[2])) for e in every])

    def source(step, core):
        pp = lax.rem(spot + step + 8, 8)
        zz = jnp.where(pp < 4, pp, 7 - pp)
        yy = jnp.where(pp < 4, 0, 1)
        return zz * 4 + yy * 2 + core

    def products(left, rows):
        return jnp.sum((left * row_products(rows[1], grad)).reshape(-1, third, row_count), axis=1)

    def left_dots(rows):
        return row_products(rows[0], act)

    tie = lax.optimization_barrier
    cat = lambda *xs: jnp.concatenate(xs, axis=1)

    *small, token = small

    def seen(x):
        nonlocal token
        x, token = tie((x, token))
        return x

    def cross(x):
        perm = [(flat(gg, pp, cc), flat(gg, pp - 1 + 2 * cc, 1 - cc)) for gg, pp, cc in every]
        return lax.ppermute(x, AXES, perm)

    two = lambda v: cat(v[:, :third], jnp.where(g == 0, v[:, third:2 * third], v[:, 2 * third:]))
    own = two(val)
    a1 = ring(own)
    a1 = seen(a1)
    xa1 = across(a1[:, third:])
    xa1 = seen(xa1)
    a2 = ring(a1)
    a2 = seen(a2)
    b1 = cross(own)
    xb1 = across(b1[:, third:])
    xb1 = seen(xb1)
    a3 = ring(a2)
    a3 = seen(a3)
    xa2 = across(a2[:, third:])
    xa2 = seen(xa2)
    s0 = sibling(val)
    s0 = seen(s0)
    h1 = cat(a1, xa1, b1, xb1)
    f1 = sibling(h1)
    q1 = cat(*tie((val, s0, h1, f1)))
    r1l = left_dots(q1)
    r1 = products(r1l, q1)
    r1 = seen(r1)
    b2 = ring(b1)
    xb2 = across(b2[:, third:])
    xb2 = seen(xb2)
    xa3 = across(a3[:, third:])
    xa3 = seen(xa3)
    h2 = cat(a2, xa2, b2, xb2)
    f2 = sibling(h2)
    f2 = seen(f2)
    b3 = ring(b2)
    b3 = seen(b3)
    a4 = ring(a3)
    a4 = seen(a4)
    q2 = cat(h2, f2)
    r2l = left_dots(q2)
    r2l = seen(r2l)
    c3 = ring(xb2)
    c3 = seen(c3)
    h3 = cat(a3, xa3, b3)
    f3 = sibling(h3)
    f3 = seen(f3)
    f4 = sibling(a4)
    f4 = seen(f4)
    c4 = ring(xa3)
    c4 = seen(c4)
    r2 = products(*tie((r2l, q2, token))[:2])
    r2 = seen(r2)
    g3 = sibling(c3)
    e4 = sibling(c4)
    q3 = cat(h3, c3, f3, g3, a4, c4, f4, e4)
    r3 = products(left_dots(q3), q3)
    small = [*small, token]

    near, far = c, 1 - c
    ahead, back = 2 * c - 1, 1 - 2 * c
    ids = []
    ids += [source(0, near), source(0, far)]
    for step in (1, 2, 3):
        ids += [source(step * ahead, near), source(step * ahead, far)]
        ids += [source(step * back, far), source(step * back, near)]
    ids += [source(4, near), source(4, far)]
    return [r1, r2, r3], jnp.stack(ids), small


def shards(act, grad, val_panels, row_domain, block_tasks, block_live, domain_tokens):
    row_count, width = act.shape
    block_count = block_live.shape[0]
    block_rows = row_count // block_count
    n_dp = lax.axis_size("dp")
    owned = domain_tokens.shape[0]
    cap = 2 * row_count // n_dp
    task_ids = jnp.arange(TASKS, dtype=jnp.int32)

    if n_dp == 16 and lax.axis_size("groups") == 2:
        small = (row_domain, block_tasks, block_live, domain_tokens)
        sums, ids, small = ring_products(act, grad, val_panels, small)
        row_domain, block_tasks, block_live, domain_tokens = small
    else:
        rows = lax.all_gather(val_panels, "dp", axis=1, tiled=True)
        sums, ids = [jnp.sum(scores(act, grad, rows).reshape(TASKS, -1, row_count), axis=1)], task_ids

    paired = jnp.sum((block_tasks[:, None, :] == task_ids[None, :, None]).astype(jnp.float32), axis=2)
    weights = paired * block_live.astype(jnp.float32)[:, None]
    weights = jnp.broadcast_to(weights.T[:, :, None], (TASKS, block_count, block_rows)).reshape(TASKS, row_count)

    owner = row_domain // owned
    local = row_domain % owned
    at_owner = (owner[:, None] == jnp.arange(n_dp, dtype=jnp.int32)[None, :])
    before = jnp.arange(row_count)[:, None] > jnp.arange(row_count)[None, :]
    rank = lax.dot_general(
        before.astype(jnp.bfloat16), at_owner.astype(jnp.bfloat16), (((1,), (0,)), ((), ())),
        preferred_element_type=jnp.float32,
    )
    rank = jnp.sum(jnp.where(at_owner, rank, 0.0), axis=1).astype(jnp.int32)
    place = (owner * HALF + rank)[None, :]
    spare = HALF - cap
    lines = -(-cap // spare)
    home = at_owner[:, :, None] & (rank[:, None, None] == jnp.arange(lines * spare, dtype=jnp.int32))
    marks = jnp.sum(jnp.where(home, (local + 1).astype(jnp.float32)[:, None, None], 0.0), axis=0)
    marks = jnp.pad(marks.reshape(n_dp, lines, spare), ((0, 0), (0, TASKS // 2 - lines), (cap, HALF)))

    packed = pack(sums, ids, weights / width, place, marks)
    theirs = lax.all_to_all(packed.reshape(n_dp, 1, -1), "dp", 0, 0, tiled=True)
    return finish(theirs.reshape(packed.shape), domain_tokens, cap)


def solution(mesh):
    return jax.shard_map(
        shards,
        mesh=mesh,
        in_specs=(
            P(("groups", "dp"), None),
            P(("groups", "dp"), None),
            P(None, "dp", None),
            P(("groups", "dp")),
            P(("groups", "dp"), None),
            P(("groups", "dp")),
            P(("groups", "dp")),
        ),
        out_specs=P(None, ("groups", "dp")),
        check_vma=False,
    )
```

```python
import functools

import jax
import jax.numpy as jnp
from jax import lax
from jax.experimental import pallas as pl
from jax.experimental.pallas import tpu as pltpu
from jax.sharding import PartitionSpec as P

TASKS = 16
AXES = ("groups", "dp")
HALF = 64


def three_parts(values):
    top = values.astype(jnp.bfloat16)
    rest = values - top.astype(jnp.float32)
    middle = rest.astype(jnp.bfloat16)
    last = (rest - middle.astype(jnp.float32)).astype(jnp.bfloat16)
    return jnp.concatenate([top, middle, last])


def choose(values, choice):
    m = values.shape[0]
    product = lax.dot_general(
        three_parts(values), choice.astype(jnp.bfloat16), (((1,), (1,)), ((), ())), preferred_element_type=jnp.float32
    )
    return product[:m] + product[m:2 * m] + product[2 * m:]


def pack_kernel(each, arrays, tasks_ref, *refs):
    sums, (weights, place, marks, out, by_task) = refs[:arrays], refs[arrays:]
    position = 0
    for ref in sums:
        for k in range(0, ref.shape[0], each):
            by_task[pl.ds(tasks_ref[position], 1), :] = jnp.sum(ref[k:k + each, :], axis=0, keepdims=True)
            position += 1
    row_task = by_task[...] * weights[...]
    owners, half_tasks, lanes = out.shape
    low = lax.broadcasted_iota(jnp.int32, (half_tasks, lanes), 1) < HALF
    slot = lax.broadcasted_iota(jnp.int32, (2 * lanes, place.shape[1]), 0)
    slot = slot // lanes * HALF + slot % HALF
    for owner in range(0, owners, 2):
        packed = choose(row_task, (place[...] == slot + owner * HALF).astype(jnp.float32))
        for k in range(2):
            part = packed[:, k * lanes:(k + 1) * lanes]
            out[owner + k] = jnp.where(low, part[:half_tasks], part[half_tasks:]) + marks[owner + k]


def pack(sums, tasks, weights, place, marks):
    each = sum(s.shape[0] for s in sums) // tasks.shape[0]
    inside = pl.BlockSpec(memory_space=pltpu.VMEM)
    return pl.pallas_call(
        functools.partial(pack_kernel, each, len(sums)),
        out_shape=jax.ShapeDtypeStruct(marks.shape, jnp.float32),
        in_specs=[pl.BlockSpec(memory_space=pltpu.SMEM)] + [inside] * (len(sums) + 3),
        out_specs=inside,
        scratch_shapes=[pltpu.VMEM(weights.shape, jnp.float32)],
        compiler_params=pltpu.CompilerParams(vmem_limit_bytes=8 * 1024 * 1024),
    )(tasks, *sums, weights, place, marks)


def finish_kernel(cap, theirs, tokens, out):
    senders, half_tasks, lanes = theirs.shape
    owned = out.shape[1]
    spare = HALF - cap
    lane = lax.broadcasted_iota(jnp.int32, (senders, lanes), 1)
    domain = jnp.zeros((senders, lanes), jnp.float32)
    for line in range(-(-cap // spare)):
        first = line * spare
        moved = pltpu.roll(theirs[:, line, :], (first - cap) % lanes, 1)
        domain = jnp.where((lane >= first) & (lane < min(cap, first + spare)), moved, domain)
    domain = domain + pltpu.roll(domain, HALF, 1)
    low = lax.broadcasted_iota(jnp.int32, (half_tasks, lanes), 1) < HALF
    mine = lax.broadcasted_iota(jnp.int32, (owned, lanes), 0).astype(jnp.float32) + 1.0
    total = jnp.zeros((2 * half_tasks, owned), jnp.float32)
    for sender in range(0, senders, 2):
        values, choice = [], []
        for k in (sender, sender + 1):
            tile = theirs[k]
            values.append(jnp.concatenate([jnp.where(low, tile, 0.0), jnp.where(low, 0.0, tile)]))
            choice.append((domain[k:k + 1, :] == mine).astype(jnp.float32))
        total += choose(jnp.concatenate(values, axis=1), jnp.concatenate(choice, axis=1))
    out[...] = total / jnp.sqrt(tokens[...].astype(jnp.float32))


def finish(theirs, tokens, cap):
    inside = pl.BlockSpec(memory_space=pltpu.VMEM)
    return pl.pallas_call(
        functools.partial(finish_kernel, cap),
        out_shape=jax.ShapeDtypeStruct((TASKS, tokens.shape[0]), jnp.float32),
        in_specs=[inside] * 2,
        out_specs=inside,
        compiler_params=pltpu.CompilerParams(vmem_limit_bytes=8 * 1024 * 1024),
    )(theirs, tokens[None, :])


def scores(act, grad, rows):
    return row_products(rows[0], act) * row_products(rows[1], grad)


def row_products(left, right):
    return lax.dot_general(left, right, (((1,), (1,)), ((), ())), preferred_element_type=jnp.float32)


def ring_products(act, grad, val, small):
    third = val.shape[1] // 3
    row_count = act.shape[0]
    g = lax.axis_index("groups")
    d = lax.axis_index("dp")
    z, y, c = d // 4, (d // 2) % 2, d % 2
    spot = jnp.where(y == 0, z, 7 - z)
    every = [(gg, pp, cc) for gg in range(2) for pp in range(8) for cc in range(2)]

    def flat(gg, pp, cc):
        pp = pp % 8
        zz, yy = (pp, 0) if pp < 4 else (7 - pp, 1)
        return gg * 16 + zz * 4 + yy * 2 + cc

    def ring(x):
        perm = [(flat(gg, pp, cc), flat(gg, pp + 1 - 2 * cc, cc)) for gg, pp, cc in every]
        return lax.ppermute(x, AXES, perm)

    def across(x):
        return lax.ppermute(x, AXES, [(flat(*e), flat(1 - e[0], e[1], e[2])) for e in every])

    def sibling(x):
        return lax.ppermute(x, AXES, [(flat(*e), flat(e[0], e[1], 1 - e[2])) for e in every])

    def source(step, core):
        pp = lax.rem(spot + step + 8, 8)
        zz = jnp.where(pp < 4, pp, 7 - pp)
        yy = jnp.where(pp < 4, 0, 1)
        return zz * 4 + yy * 2 + core

    def products(left, rows):
        return jnp.sum((left * row_products(rows[1], grad)).reshape(-1, third, row_count), axis=1)

    def left_dots(rows):
        return row_products(rows[0], act)

    tie = lax.optimization_barrier
    cat = lambda *xs: jnp.concatenate(xs, axis=1)

    *small, token = small

    def seen(x):
        nonlocal token
        x, token = tie((x, token))
        return x

    def cross(x):
        perm = [(flat(gg, pp, cc), flat(gg, pp - 1 + 2 * cc, 1 - cc)) for gg, pp, cc in every]
        return lax.ppermute(x, AXES, perm)

    two = lambda v: cat(v[:, :third], jnp.where(g == 0, v[:, third:2 * third], v[:, 2 * third:]))
    own = two(val)
    a1 = ring(own)
    a1 = seen(a1)
    xa1 = across(a1[:, third:])
    xa1 = seen(xa1)
    a2 = ring(a1)
    a2 = seen(a2)
    b1 = cross(own)
    xb1 = across(b1[:, third:])
    xb1 = seen(xb1)
    a3 = ring(a2)
    a3 = seen(a3)
    xa2 = across(a2[:, third:])
    xa2 = seen(xa2)
    s0 = sibling(val)
    s0 = seen(s0)
    h1 = cat(a1, xa1, b1, xb1)
    f1 = sibling(h1)
    q1 = cat(*tie((val, s0, h1, f1)))
    r1l = left_dots(q1)
    r1 = products(r1l, q1)
    r1 = seen(r1)
    b2 = ring(b1)
    xb2 = across(b2[:, third:])
    xb2 = seen(xb2)
    h2 = cat(a2, xa2, b2, xb2)
    f2 = sibling(h2)
    f2 = seen(f2)
    xa3 = across(a3[:, third:])
    xa3 = seen(xa3)
    b3 = ring(b2)
    b3 = seen(b3)
    a4 = ring(a3)
    a4 = seen(a4)
    q2 = cat(h2, f2)
    r2l = left_dots(q2)
    r2l = seen(r2l)
    c3 = ring(xb2)
    c3 = seen(c3)
    h3 = cat(a3, xa3, b3)
    f3 = sibling(h3)
    f3 = seen(f3)
    f4 = sibling(a4)
    f4 = seen(f4)
    c4 = ring(xa3)
    c4 = seen(c4)
    r2 = products(*tie((r2l, q2, token))[:2])
    r2 = seen(r2)
    g3 = sibling(c3)
    e4 = sibling(c4)
    q3 = cat(h3, c3, f3, g3, a4, c4, f4, e4)
    r3 = products(left_dots(q3), q3)
    small = [*small, token]

    near, far = c, 1 - c
    ahead, back = 2 * c - 1, 1 - 2 * c
    ids = []
    ids += [source(0, near), source(0, far)]
    for step in (1, 2, 3):
        ids += [source(step * ahead, near), source(step * ahead, far)]
        ids += [source(step * back, far), source(step * back, near)]
    ids += [source(4, near), source(4, far)]
    return [r1, r2, r3], jnp.stack(ids), small


def shards(act, grad, val_panels, row_domain, block_tasks, block_live, domain_tokens):
    row_count, width = act.shape
    block_count = block_live.shape[0]
    block_rows = row_count // block_count
    n_dp = lax.axis_size("dp")
    owned = domain_tokens.shape[0]
    cap = 2 * row_count // n_dp
    task_ids = jnp.arange(TASKS, dtype=jnp.int32)

    if n_dp == 16 and lax.axis_size("groups") == 2:
        small = (row_domain, block_tasks, block_live, domain_tokens)
        sums, ids, small = ring_products(act, grad, val_panels, small)
        row_domain, block_tasks, block_live, domain_tokens = small
    else:
        rows = lax.all_gather(val_panels, "dp", axis=1, tiled=True)
        sums, ids = [jnp.sum(scores(act, grad, rows).reshape(TASKS, -1, row_count), axis=1)], task_ids

    paired = jnp.sum((block_tasks[:, None, :] == task_ids[None, :, None]).astype(jnp.float32), axis=2)
    weights = paired * block_live.astype(jnp.float32)[:, None]
    weights = jnp.broadcast_to(weights.T[:, :, None], (TASKS, block_count, block_rows)).reshape(TASKS, row_count)

    owner = row_domain // owned
    local = row_domain % owned
    at_owner = (owner[:, None] == jnp.arange(n_dp, dtype=jnp.int32)[None, :])
    before = jnp.arange(row_count)[:, None] > jnp.arange(row_count)[None, :]
    rank = lax.dot_general(
        before.astype(jnp.bfloat16), at_owner.astype(jnp.bfloat16), (((1,), (0,)), ((), ())),
        preferred_element_type=jnp.float32,
    )
    rank = jnp.sum(jnp.where(at_owner, rank, 0.0), axis=1).astype(jnp.int32)
    place = (owner * HALF + rank)[None, :]
    spare = HALF - cap
    lines = -(-cap // spare)
    home = at_owner[:, :, None] & (rank[:, None, None] == jnp.arange(lines * spare, dtype=jnp.int32))
    marks = jnp.sum(jnp.where(home, (local + 1).astype(jnp.float32)[:, None, None], 0.0), axis=0)
    marks = jnp.pad(marks.reshape(n_dp, lines, spare), ((0, 0), (0, TASKS // 2 - lines), (cap, HALF)))

    packed = pack(sums, ids, weights / width, place, marks)
    theirs = lax.all_to_all(packed.reshape(n_dp, 1, -1), "dp", 0, 0, tiled=True)
    return finish(theirs.reshape(packed.shape), domain_tokens, cap)


def solution(mesh):
    return jax.shard_map(
        shards,
        mesh=mesh,
        in_specs=(
            P(("groups", "dp"), None),
            P(("groups", "dp"), None),
            P(None, "dp", None),
            P(("groups", "dp")),
            P(("groups", "dp"), None),
            P(("groups", "dp")),
            P(("groups", "dp")),
        ),
        out_specs=P(None, ("groups", "dp")),
        check_vma=False,
    )
```

```python
import functools

import jax
import jax.numpy as jnp
from jax import lax
from jax.experimental import pallas as pl
from jax.experimental.pallas import tpu as pltpu
from jax.sharding import PartitionSpec as P

TASKS = 16
AXES = ("groups", "dp")
HALF = 64


def three_parts(values):
    top = values.astype(jnp.bfloat16)
    rest = values - top.astype(jnp.float32)
    middle = rest.astype(jnp.bfloat16)
    last = (rest - middle.astype(jnp.float32)).astype(jnp.bfloat16)
    return jnp.concatenate([top, middle, last])


def choose(values, choice):
    m = values.shape[0]
    product = lax.dot_general(
        three_parts(values), choice.astype(jnp.bfloat16), (((1,), (1,)), ((), ())), preferred_element_type=jnp.float32
    )
    return product[:m] + product[m:2 * m] + product[2 * m:]


def pack_kernel(each, arrays, tasks_ref, *refs):
    sums, (weights, place, marks, out, by_task) = refs[:arrays], refs[arrays:]
    position = 0
    for ref in sums:
        for k in range(0, ref.shape[0], each):
            by_task[pl.ds(tasks_ref[position], 1), :] = jnp.sum(ref[k:k + each, :], axis=0, keepdims=True)
            position += 1
    row_task = by_task[...] * weights[...]
    owners, half_tasks, lanes = out.shape
    low = lax.broadcasted_iota(jnp.int32, (half_tasks, lanes), 1) < HALF
    slot = lax.broadcasted_iota(jnp.int32, (2 * lanes, place.shape[1]), 0)
    slot = slot // lanes * HALF + slot % HALF
    for owner in range(0, owners, 2):
        packed = choose(row_task, (place[...] == slot + owner * HALF).astype(jnp.float32))
        for k in range(2):
            part = packed[:, k * lanes:(k + 1) * lanes]
            out[owner + k] = jnp.where(low, part[:half_tasks], part[half_tasks:]) + marks[owner + k]


def pack(sums, tasks, weights, place, marks):
    each = sum(s.shape[0] for s in sums) // tasks.shape[0]
    inside = pl.BlockSpec(memory_space=pltpu.VMEM)
    return pl.pallas_call(
        functools.partial(pack_kernel, each, len(sums)),
        out_shape=jax.ShapeDtypeStruct(marks.shape, jnp.float32),
        in_specs=[pl.BlockSpec(memory_space=pltpu.SMEM)] + [inside] * (len(sums) + 3),
        out_specs=inside,
        scratch_shapes=[pltpu.VMEM(weights.shape, jnp.float32)],
        compiler_params=pltpu.CompilerParams(vmem_limit_bytes=8 * 1024 * 1024),
    )(tasks, *sums, weights, place, marks)


def finish_kernel(cap, theirs, tokens, out):
    senders, half_tasks, lanes = theirs.shape
    owned = out.shape[1]
    spare = HALF - cap
    lane = lax.broadcasted_iota(jnp.int32, (senders, lanes), 1)
    domain = jnp.zeros((senders, lanes), jnp.float32)
    for line in range(-(-cap // spare)):
        first = line * spare
        moved = pltpu.roll(theirs[:, line, :], (first - cap) % lanes, 1)
        domain = jnp.where((lane >= first) & (lane < min(cap, first + spare)), moved, domain)
    domain = domain + pltpu.roll(domain, HALF, 1)
    low = lax.broadcasted_iota(jnp.int32, (half_tasks, lanes), 1) < HALF
    mine = lax.broadcasted_iota(jnp.int32, (owned, lanes), 0).astype(jnp.float32) + 1.0
    total = jnp.zeros((2 * half_tasks, owned), jnp.float32)
    for sender in range(0, senders, 2):
        values, choice = [], []
        for k in (sender, sender + 1):
            tile = theirs[k]
            values.append(jnp.concatenate([jnp.where(low, tile, 0.0), jnp.where(low, 0.0, tile)]))
            choice.append((domain[k:k + 1, :] == mine).astype(jnp.float32))
        total += choose(jnp.concatenate(values, axis=1), jnp.concatenate(choice, axis=1))
    out[...] = total / jnp.sqrt(tokens[...].astype(jnp.float32))


def finish(theirs, tokens, cap):
    inside = pl.BlockSpec(memory_space=pltpu.VMEM)
    return pl.pallas_call(
        functools.partial(finish_kernel, cap),
        out_shape=jax.ShapeDtypeStruct((TASKS, tokens.shape[0]), jnp.float32),
        in_specs=[inside] * 2,
        out_specs=inside,
        compiler_params=pltpu.CompilerParams(vmem_limit_bytes=8 * 1024 * 1024),
    )(theirs, tokens[None, :])


def scores(act, grad, rows):
    return row_products(rows[0], act) * row_products(rows[1], grad)


def row_products(left, right):
    return lax.dot_general(left, right, (((1,), (1,)), ((), ())), preferred_element_type=jnp.float32)


def ring_products(act, grad, val, small):
    third = val.shape[1] // 3
    row_count = act.shape[0]
    g = lax.axis_index("groups")
    d = lax.axis_index("dp")
    z, y, c = d // 4, (d // 2) % 2, d % 2
    spot = jnp.where(y == 0, z, 7 - z)
    every = [(gg, pp, cc) for gg in range(2) for pp in range(8) for cc in range(2)]

    def flat(gg, pp, cc):
        pp = pp % 8
        zz, yy = (pp, 0) if pp < 4 else (7 - pp, 1)
        return gg * 16 + zz * 4 + yy * 2 + cc

    def ring(x):
        perm = [(flat(gg, pp, cc), flat(gg, pp + 1 - 2 * cc, cc)) for gg, pp, cc in every]
        return lax.ppermute(x, AXES, perm)

    def across(x):
        return lax.ppermute(x, AXES, [(flat(*e), flat(1 - e[0], e[1], e[2])) for e in every])

    def sibling(x):
        return lax.ppermute(x, AXES, [(flat(*e), flat(e[0], e[1], 1 - e[2])) for e in every])

    def source(step, core):
        pp = lax.rem(spot + step + 8, 8)
        zz = jnp.where(pp < 4, pp, 7 - pp)
        yy = jnp.where(pp < 4, 0, 1)
        return zz * 4 + yy * 2 + core

    def products(left, rows):
        return jnp.sum((left * row_products(rows[1], grad)).reshape(-1, third, row_count), axis=1)

    def left_dots(rows):
        return row_products(rows[0], act)

    tie = lax.optimization_barrier
    cat = lambda *xs: jnp.concatenate(xs, axis=1)

    *small, token = small

    def seen(x):
        nonlocal token
        x, token = tie((x, token))
        return x

    def cross(x):
        perm = [(flat(gg, pp, cc), flat(gg, pp - 1 + 2 * cc, 1 - cc)) for gg, pp, cc in every]
        return lax.ppermute(x, AXES, perm)

    two = lambda v: cat(v[:, :third], jnp.where(g == 0, v[:, third:2 * third], v[:, 2 * third:]))
    own = two(val)
    a1 = ring(own)
    a1 = seen(a1)
    xa1 = across(a1[:, third:])
    xa1 = seen(xa1)
    a2 = ring(a1)
    a2 = seen(a2)
    b1 = cross(own)
    xb1 = across(b1[:, third:])
    xb1 = seen(xb1)
    a3 = ring(a2)
    a3 = seen(a3)
    xa2 = across(a2[:, third:])
    xa2 = seen(xa2)
    s0 = sibling(val)
    s0 = seen(s0)
    h1 = cat(a1, xa1, b1, xb1)
    f1 = sibling(h1)
    q1 = cat(*tie((val, s0, h1, f1)))
    r1l = left_dots(q1)
    r1 = products(r1l, q1)
    r1 = seen(r1)
    b2 = ring(b1)
    xb2 = across(b2[:, third:])
    xb2 = seen(xb2)
    xa3 = across(a3[:, third:])
    xa3 = seen(xa3)
    h2 = cat(a2, xa2, b2, xb2)
    f2 = sibling(h2)
    f2 = seen(f2)
    b3 = ring(b2)
    b3 = seen(b3)
    a4 = ring(a3)
    a4 = seen(a4)
    q2 = cat(h2, f2)
    r2l = left_dots(q2)
    r2l = seen(r2l)
    c3 = ring(xb2)
    c3 = seen(c3)
    h3 = cat(a3, xa3, b3)
    f3 = sibling(h3)
    f3 = seen(f3)
    f4 = sibling(a4)
    c4 = ring(xa3)
    c4 = seen(c4)
    g3 = sibling(c3)
    g3 = seen(g3)
    e4 = sibling(c4)
    e4 = seen(e4)
    r2 = products(r2l, q2)
    r2 = seen(r2)
    q3 = cat(h3, c3, f3, g3, a4, c4, f4, e4)
    r3 = products(left_dots(q3), q3)
    small = [*small, token]

    near, far = c, 1 - c
    ahead, back = 2 * c - 1, 1 - 2 * c
    ids = []
    ids += [source(0, near), source(0, far)]
    for step in (1, 2, 3):
        ids += [source(step * ahead, near), source(step * ahead, far)]
        ids += [source(step * back, far), source(step * back, near)]
    ids += [source(4, near), source(4, far)]
    return [r1, r2, r3], jnp.stack(ids), small


def shards(act, grad, val_panels, row_domain, block_tasks, block_live, domain_tokens):
    row_count, width = act.shape
    block_count = block_live.shape[0]
    block_rows = row_count // block_count
    n_dp = lax.axis_size("dp")
    owned = domain_tokens.shape[0]
    cap = 2 * row_count // n_dp
    task_ids = jnp.arange(TASKS, dtype=jnp.int32)

    if n_dp == 16 and lax.axis_size("groups") == 2:
        small = (row_domain, block_tasks, block_live, domain_tokens)
        sums, ids, small = ring_products(act, grad, val_panels, small)
        row_domain, block_tasks, block_live, domain_tokens = small
    else:
        rows = lax.all_gather(val_panels, "dp", axis=1, tiled=True)
        sums, ids = [jnp.sum(scores(act, grad, rows).reshape(TASKS, -1, row_count), axis=1)], task_ids

    paired = jnp.sum((block_tasks[:, None, :] == task_ids[None, :, None]).astype(jnp.float32), axis=2)
    weights = paired * block_live.astype(jnp.float32)[:, None]
    weights = jnp.broadcast_to(weights.T[:, :, None], (TASKS, block_count, block_rows)).reshape(TASKS, row_count)

    owner = row_domain // owned
    local = row_domain % owned
    at_owner = (owner[:, None] == jnp.arange(n_dp, dtype=jnp.int32)[None, :])
    before = jnp.arange(row_count)[:, None] > jnp.arange(row_count)[None, :]
    rank = lax.dot_general(
        before.astype(jnp.bfloat16), at_owner.astype(jnp.bfloat16), (((1,), (0,)), ((), ())),
        preferred_element_type=jnp.float32,
    )
    rank = jnp.sum(jnp.where(at_owner, rank, 0.0), axis=1).astype(jnp.int32)
    place = (owner * HALF + rank)[None, :]
    spare = HALF - cap
    lines = -(-cap // spare)
    home = at_owner[:, :, None] & (rank[:, None, None] == jnp.arange(lines * spare, dtype=jnp.int32))
    marks = jnp.sum(jnp.where(home, (local + 1).astype(jnp.float32)[:, None, None], 0.0), axis=0)
    marks = jnp.pad(marks.reshape(n_dp, lines, spare), ((0, 0), (0, TASKS // 2 - lines), (cap, HALF)))

    packed = pack(sums, ids, weights / width, place, marks)
    theirs = lax.all_to_all(packed.reshape(n_dp, 1, -1), "dp", 0, 0, tiled=True)
    return finish(theirs.reshape(packed.shape), domain_tokens, cap)


def solution(mesh):
    return jax.shard_map(
        shards,
        mesh=mesh,
        in_specs=(
            P(("groups", "dp"), None),
            P(("groups", "dp"), None),
            P(None, "dp", None),
            P(("groups", "dp")),
            P(("groups", "dp"), None),
            P(("groups", "dp")),
            P(("groups", "dp")),
        ),
        out_specs=P(None, ("groups", "dp")),
        check_vma=False,
    )
```

```python
import functools

import jax
import jax.numpy as jnp
from jax import lax
from jax.experimental import pallas as pl
from jax.experimental.pallas import tpu as pltpu
from jax.sharding import PartitionSpec as P

TASKS = 16
AXES = ("groups", "dp")
HALF = 64


def three_parts(values):
    top = values.astype(jnp.bfloat16)
    rest = values - top.astype(jnp.float32)
    middle = rest.astype(jnp.bfloat16)
    last = (rest - middle.astype(jnp.float32)).astype(jnp.bfloat16)
    return jnp.concatenate([top, middle, last])


def choose(values, choice):
    m = values.shape[0]
    product = lax.dot_general(
        three_parts(values), choice.astype(jnp.bfloat16), (((1,), (1,)), ((), ())), preferred_element_type=jnp.float32
    )
    return product[:m] + product[m:2 * m] + product[2 * m:]


def pack_kernel(each, arrays, tasks_ref, *refs):
    sums, (weights, place, marks, out, by_task) = refs[:arrays], refs[arrays:]
    position = 0
    for ref in sums:
        for k in range(0, ref.shape[0], each):
            by_task[pl.ds(tasks_ref[position], 1), :] = jnp.sum(ref[k:k + each, :], axis=0, keepdims=True)
            position += 1
    row_task = by_task[...] * weights[...]
    owners, half_tasks, lanes = out.shape
    low = lax.broadcasted_iota(jnp.int32, (half_tasks, lanes), 1) < HALF
    slot = lax.broadcasted_iota(jnp.int32, (2 * lanes, place.shape[1]), 0)
    slot = slot // lanes * HALF + slot % HALF
    for owner in range(0, owners, 2):
        packed = choose(row_task, (place[...] == slot + owner * HALF).astype(jnp.float32))
        for k in range(2):
            part = packed[:, k * lanes:(k + 1) * lanes]
            out[owner + k] = jnp.where(low, part[:half_tasks], part[half_tasks:]) + marks[owner + k]


def pack(sums, tasks, weights, place, marks):
    each = sum(s.shape[0] for s in sums) // tasks.shape[0]
    inside = pl.BlockSpec(memory_space=pltpu.VMEM)
    return pl.pallas_call(
        functools.partial(pack_kernel, each, len(sums)),
        out_shape=jax.ShapeDtypeStruct(marks.shape, jnp.float32),
        in_specs=[pl.BlockSpec(memory_space=pltpu.SMEM)] + [inside] * (len(sums) + 3),
        out_specs=inside,
        scratch_shapes=[pltpu.VMEM(weights.shape, jnp.float32)],
        compiler_params=pltpu.CompilerParams(vmem_limit_bytes=8 * 1024 * 1024),
    )(tasks, *sums, weights, place, marks)


def finish_kernel(cap, theirs, tokens, out):
    senders, half_tasks, lanes = theirs.shape
    owned = out.shape[1]
    spare = HALF - cap
    lane = lax.broadcasted_iota(jnp.int32, (senders, lanes), 1)
    domain = jnp.zeros((senders, lanes), jnp.float32)
    for line in range(-(-cap // spare)):
        first = line * spare
        moved = pltpu.roll(theirs[:, line, :], (first - cap) % lanes, 1)
        domain = jnp.where((lane >= first) & (lane < min(cap, first + spare)), moved, domain)
    domain = domain + pltpu.roll(domain, HALF, 1)
    low = lax.broadcasted_iota(jnp.int32, (half_tasks, lanes), 1) < HALF
    mine = lax.broadcasted_iota(jnp.int32, (owned, lanes), 0).astype(jnp.float32) + 1.0
    total = jnp.zeros((2 * half_tasks, owned), jnp.float32)
    for sender in range(0, senders, 2):
        values, choice = [], []
        for k in (sender, sender + 1):
            tile = theirs[k]
            values.append(jnp.concatenate([jnp.where(low, tile, 0.0), jnp.where(low, 0.0, tile)]))
            choice.append((domain[k:k + 1, :] == mine).astype(jnp.float32))
        total += choose(jnp.concatenate(values, axis=1), jnp.concatenate(choice, axis=1))
    out[...] = total / jnp.sqrt(tokens[...].astype(jnp.float32))


def finish(theirs, tokens, cap):
    inside = pl.BlockSpec(memory_space=pltpu.VMEM)
    return pl.pallas_call(
        functools.partial(finish_kernel, cap),
        out_shape=jax.ShapeDtypeStruct((TASKS, tokens.shape[0]), jnp.float32),
        in_specs=[inside] * 2,
        out_specs=inside,
        compiler_params=pltpu.CompilerParams(vmem_limit_bytes=8 * 1024 * 1024),
    )(theirs, tokens[None, :])


def scores(act, grad, rows):
    return row_products(rows[0], act) * row_products(rows[1], grad)


def row_products(left, right):
    return lax.dot_general(left, right, (((1,), (1,)), ((), ())), preferred_element_type=jnp.float32)


def ring_products(act, grad, val, small):
    third = val.shape[1] // 3
    row_count = act.shape[0]
    g = lax.axis_index("groups")
    d = lax.axis_index("dp")
    z, y, c = d // 4, (d // 2) % 2, d % 2
    spot = jnp.where(y == 0, z, 7 - z)
    every = [(gg, pp, cc) for gg in range(2) for pp in range(8) for cc in range(2)]

    def flat(gg, pp, cc):
        pp = pp % 8
        zz, yy = (pp, 0) if pp < 4 else (7 - pp, 1)
        return gg * 16 + zz * 4 + yy * 2 + cc

    def ring(x):
        perm = [(flat(gg, pp, cc), flat(gg, pp + 1 - 2 * cc, cc)) for gg, pp, cc in every]
        return lax.ppermute(x, AXES, perm)

    def across(x):
        return lax.ppermute(x, AXES, [(flat(*e), flat(1 - e[0], e[1], e[2])) for e in every])

    def sibling(x):
        return lax.ppermute(x, AXES, [(flat(*e), flat(e[0], e[1], 1 - e[2])) for e in every])

    def source(step, core):
        pp = lax.rem(spot + step + 8, 8)
        zz = jnp.where(pp < 4, pp, 7 - pp)
        yy = jnp.where(pp < 4, 0, 1)
        return zz * 4 + yy * 2 + core

    def products(left, rows):
        return jnp.sum((left * row_products(rows[1], grad)).reshape(-1, third, row_count), axis=1)

    def left_dots(rows):
        return row_products(rows[0], act)

    tie = lax.optimization_barrier
    cat = lambda *xs: jnp.concatenate(xs, axis=1)

    *small, token = small

    def seen(x):
        nonlocal token
        x, token = tie((x, token))
        return x

    def cross(x):
        perm = [(flat(gg, pp, cc), flat(gg, pp - 1 + 2 * cc, 1 - cc)) for gg, pp, cc in every]
        return lax.ppermute(x, AXES, perm)

    two = lambda v: cat(v[:, :third], jnp.where(g == 0, v[:, third:2 * third], v[:, 2 * third:]))
    own = two(val)
    a1 = ring(own)
    a1 = seen(a1)
    xa1 = across(a1[:, third:])
    xa1 = seen(xa1)
    a2 = ring(a1)
    a2 = seen(a2)
    b1 = cross(own)
    xb1 = across(b1[:, third:])
    xb1 = seen(xb1)
    a3 = ring(a2)
    a3 = seen(a3)
    xa2 = across(a2[:, third:])
    xa2 = seen(xa2)
    s0 = sibling(val)
    s0 = seen(s0)
    h1 = cat(a1, xa1, b1, xb1)
    f1 = sibling(h1)
    q1 = cat(*tie((val, s0, h1, f1)))
    r1l = left_dots(q1)
    r1 = products(r1l, q1)
    r1 = seen(r1)
    b2 = ring(b1)
    xb2 = across(b2[:, third:])
    xb2 = seen(xb2)
    xa3 = across(a3[:, third:])
    xa3 = seen(xa3)
    h2 = cat(a2, xa2, b2, xb2)
    f2 = sibling(h2)
    f2 = seen(f2)
    b3 = ring(b2)
    b3 = seen(b3)
    a4 = ring(a3)
    a4 = seen(a4)
    q2 = cat(h2, f2)
    r2l = left_dots(q2)
    r2l = seen(r2l)
    f4 = sibling(a4)
    f4 = seen(f4)
    c3 = ring(xb2)
    c3 = seen(c3)
    h3 = cat(a3, xa3, b3)
    f3 = sibling(h3)
    f3 = seen(f3)
    c4 = ring(xa3)
    c4 = seen(c4)
    g3 = sibling(c3)
    g3 = seen(g3)
    e4 = sibling(c4)
    e4 = seen(e4)
    r2 = products(r2l, q2)
    r2 = seen(r2)
    q3 = cat(h3, c3, f3, g3, a4, c4, f4, e4)
    r3 = products(left_dots(q3), q3)
    small = [*small, token]

    near, far = c, 1 - c
    ahead, back = 2 * c - 1, 1 - 2 * c
    ids = []
    ids += [source(0, near), source(0, far)]
    for step in (1, 2, 3):
        ids += [source(step * ahead, near), source(step * ahead, far)]
        ids += [source(step * back, far), source(step * back, near)]
    ids += [source(4, near), source(4, far)]
    return [r1, r2, r3], jnp.stack(ids), small


def shards(act, grad, val_panels, row_domain, block_tasks, block_live, domain_tokens):
    row_count, width = act.shape
    block_count = block_live.shape[0]
    block_rows = row_count // block_count
    n_dp = lax.axis_size("dp")
    owned = domain_tokens.shape[0]
    cap = 2 * row_count // n_dp
    task_ids = jnp.arange(TASKS, dtype=jnp.int32)

    if n_dp == 16 and lax.axis_size("groups") == 2:
        small = (row_domain, block_tasks, block_live, domain_tokens)
        sums, ids, small = ring_products(act, grad, val_panels, small)
        row_domain, block_tasks, block_live, domain_tokens = small
    else:
        rows = lax.all_gather(val_panels, "dp", axis=1, tiled=True)
        sums, ids = [jnp.sum(scores(act, grad, rows).reshape(TASKS, -1, row_count), axis=1)], task_ids

    paired = jnp.sum((block_tasks[:, None, :] == task_ids[None, :, None]).astype(jnp.float32), axis=2)
    weights = paired * block_live.astype(jnp.float32)[:, None]
    weights = jnp.broadcast_to(weights.T[:, :, None], (TASKS, block_count, block_rows)).reshape(TASKS, row_count)

    owner = row_domain // owned
    local = row_domain % owned
    at_owner = (owner[:, None] == jnp.arange(n_dp, dtype=jnp.int32)[None, :])
    before = jnp.arange(row_count)[:, None] > jnp.arange(row_count)[None, :]
    rank = lax.dot_general(
        before.astype(jnp.bfloat16), at_owner.astype(jnp.bfloat16), (((1,), (0,)), ((), ())),
        preferred_element_type=jnp.float32,
    )
    rank = jnp.sum(jnp.where(at_owner, rank, 0.0), axis=1).astype(jnp.int32)
    place = (owner * HALF + rank)[None, :]
    spare = HALF - cap
    lines = -(-cap // spare)
    home = at_owner[:, :, None] & (rank[:, None, None] == jnp.arange(lines * spare, dtype=jnp.int32))
    marks = jnp.sum(jnp.where(home, (local + 1).astype(jnp.float32)[:, None, None], 0.0), axis=0)
    marks = jnp.pad(marks.reshape(n_dp, lines, spare), ((0, 0), (0, TASKS // 2 - lines), (cap, HALF)))

    packed = pack(sums, ids, weights / width, place, marks)
    theirs = lax.all_to_all(packed.reshape(n_dp, 1, -1), "dp", 0, 0, tiled=True)
    return finish(theirs.reshape(packed.shape), domain_tokens, cap)


def solution(mesh):
    return jax.shard_map(
        shards,
        mesh=mesh,
        in_specs=(
            P(("groups", "dp"), None),
            P(("groups", "dp"), None),
            P(None, "dp", None),
            P(("groups", "dp")),
            P(("groups", "dp"), None),
            P(("groups", "dp")),
            P(("groups", "dp")),
        ),
        out_specs=P(None, ("groups", "dp")),
        check_vma=False,
    )
```
